256 devices in a mesh: src: 16 (over y, x), tgt: 16 (over z, core).
Axes of the slice: x: 4, y: 4, z: 8, core: 2. Of those that a mesh axis runs over, the one named last changes fastest.
Arguments:
- src_feat: bfloat16 [64, 131072], P(None, ('src', 'tgt')), may hold values from -0.375 to 0.375
- tgt_feat: bfloat16 [64, 131072], P(None, ('tgt', 'src')), may hold values from -0.375 to 0.375
- row_pot: float32 [131072], P(('src', 'tgt')), may hold values from -1 to 1
- col_pot: float32 [131072], P(('tgt', 'src')), may hold values from -1 to 1
- src_mass: float32 [131072], P(('src', 'tgt')), may hold values from 2 to 20
- tgt_mass: float32 [131072], P(('tgt', 'src')), may hold values from 2 to 20
- rhs_src: float32 [131072], P(('src', 'tgt')), may hold values from -4 to 4
- rhs_tgt: float32 [131072], P(('tgt', 'src')), may hold values from -4 to 4
- tile_rows: int32 [16, 16, 8], P('src', 'tgt'), may hold values from 0 to 7, as said below
- tile_cols: int32 [16, 16, 8], P('src', 'tgt'), may hold values from 0 to 7
- tile_count: int32 [16, 16], P('src', 'tgt'), may hold values from 1 to 8, as said below
Outputs:
- adjoint_src: float32 [131072], P(('src', 'tgt'))
- adjoint_tgt: float32 [131072], P(('tgt', 'src'))
- grad_src: float32 [64, 131072], P(None, ('src', 'tgt'))
- grad_tgt: float32 [64, 131072], P(None, ('tgt', 'src'))
The draws below stay inside these ranges and needn't reach their ends.
Inputs may be any that keep to these rules, and one draw needn't show every extreme that they name: `tile_rows`: the first tile_count slots of a grid position name distinct pairs of source and target blocks; later slots are unused. `tile_count`: some grid position holds exactly 8 tiles.
All inputs are finite; a program needn't handle non-finite values.
Results may differ from the reference program's by a relative error of at most 0.0005.
Values may be sent and summed in bfloat16 or wider, within the bound.
No kernel may reach another device: no remote copies, remote signals or barrier semaphores. Data moves between devices by JAX's collectives and lax.ppermute only.
A program may use at most 128 MiB of HBM per device.

```python
import math
import jax
import jax.numpy as jnp
from jax import lax

F = 64
TILE = 1024
BLOCKS = 8
MAXT = 8
ITERS = 3
NS = 131072
NT = 131072
N_SRC = 16
N_TGT = 16


def tile_slots(key):
    device_keys = jax.random.split(key, N_SRC * N_TGT)

    def shuffled(device_key):
        return jax.random.permutation(device_key, BLOCKS * BLOCKS)
    orders = jax.vmap(shuffled)(device_keys)
    return orders[:, :MAXT].reshape(N_SRC, N_TGT, MAXT).astype(jnp.int32)


def draw_tile_rows(key, part):
    slot_ids = tile_slots(key)
    return (slot_ids // BLOCKS).astype(jnp.int32)


def draw_tile_cols(key, part):
    slot_ids = tile_slots(key)
    return (slot_ids % BLOCKS).astype(jnp.int32)


def draw_tile_count(key, part):
    key = jax.random.fold_in(key, 3)
    level_key, pick_key = jax.random.split(key)
    levels = jax.random.randint(level_key, (N_SRC * N_TGT,), 0, 4)
    counts = jnp.maximum(1, MAXT // jnp.left_shift(1, levels))
    chosen = jax.random.randint(pick_key, (), 0, N_SRC * N_TGT)
    counts = counts.at[chosen].set(MAXT)
    return counts.reshape(N_SRC, N_TGT).astype(jnp.int32)


def potential(key, length):
    block_key, cell_key = jax.random.split(key)
    offsets = jax.random.uniform(block_key, (length // TILE,), jnp.float32, -0.04, 0.04)
    jitter = jax.random.uniform(cell_key, (length,), jnp.float32, -1.0, 1.0)
    return 0.025 * (8.5 - math.log(2.0 * TILE)) + jnp.repeat(offsets, TILE) + 0.03 * jitter


def draw_row_pot(key, part):
    key = jax.random.fold_in(key, 5)
    return potential(key, NS)


def draw_col_pot(key, part):
    key = jax.random.fold_in(key, 7)
    return potential(key, NT)


def slow_wave(length, height):
    places = jnp.arange(length, dtype=jnp.float32) / length
    return height * jnp.sin(6.0 * math.pi * places)


def draw_rhs_src(key, part):
    key = jax.random.fold_in(key, 11)
    noise = 1.2 * jax.random.normal(key, (NS,), jnp.float32)
    level = 0.8 + slow_wave(NS, 0.0)
    return jnp.clip(level + noise, -4.0, 4.0)


def draw_rhs_tgt(key, part):
    key = jax.random.fold_in(key, 13)
    noise = 1.2 * jax.random.normal(key, (NT,), jnp.float32)
    level = -0.8 - slow_wave(NT, 0.0)
    return jnp.clip(level + noise, -4.0, 4.0)


def level_of(own_key, dims, cuts, low, largest):
    level, own = 1.0, jax.random.fold_in(own_key, 6)
    for position, shards_of in cuts:
        draws = jnp.exp(jax.random.uniform(jax.random.fold_in(own, position), (shards_of,), jnp.float32, low / len(cuts), largest / len(cuts)))
        level = level * jnp.repeat(draws, dims[position] // shards_of).reshape([-1 if axis == position else 1 for axis in range(len(dims))])
    return level


def normal_values(own_key, extent, width, reach, cuts=(), held_as=jnp.bfloat16):
    entries = width * jax.random.normal(own_key, extent, jnp.float32)
    if cuts:
        entries = entries * level_of(own_key, extent, cuts, -0.22, 0.18)
    return jnp.clip(entries, -reach, reach).astype(held_as)


def setup_inputs(seed: int = 0) -> dict:
    splits = jax.random.split(jax.random.key(seed), 12)
    src_feat = normal_values(splits[0], (F, NS), (4 * F) ** -0.5, 0.375, ((1, 256),))
    tgt_feat = normal_values(splits[1], (F, NT), (4 * F) ** -0.5, 0.375, ((1, 256),))
    row_pot = draw_row_pot(jax.random.fold_in(splits[11], 71), 0)
    col_pot = draw_col_pot(jax.random.fold_in(splits[11], 71), 0)
    src_mass = jnp.clip(jnp.exp(math.log(20.0) - 2.3025851 * jax.random.uniform(splits[4], (NS,), jnp.float32) ** level_of(splits[4], (NS,), ((0, 256),), -0.2, 0.2)), 2.0, 20.0)
    tgt_mass = jnp.clip(jnp.exp(math.log(20.0) - 2.3025851 * jax.random.uniform(splits[5], (NT,), jnp.float32) ** level_of(splits[5], (NT,), ((0, 256),), -0.2, 0.2)), 2.0, 20.0)
    rhs_src = draw_rhs_src(jax.random.fold_in(splits[11], 71), 0)
    rhs_tgt = draw_rhs_tgt(jax.random.fold_in(splits[11], 71), 0)
    tile_rows = draw_tile_rows(jax.random.fold_in(splits[11], 71), 0)
    tile_cols = draw_tile_cols(jax.random.fold_in(splits[11], 71), 0)
    tile_count = draw_tile_count(jax.random.fold_in(splits[11], 71), 0)
    return {"src_feat": src_feat, "tgt_feat": tgt_feat, "row_pot": row_pot, "col_pot": col_pot, "src_mass": src_mass, "tgt_mass": tgt_mass, "rhs_src": rhs_src, "rhs_tgt": rhs_tgt, "tile_rows": tile_rows, "tile_cols": tile_cols, "tile_count": tile_count}


EPS = 0.05
RHO = 1.0


def add_into(total, start, piece, axis):
    current = lax.dynamic_slice_in_dim(total, start, piece.shape[axis], axis)
    return lax.dynamic_update_slice_in_dim(total, current + piece, start, axis)


def kernel_block(src_block, tgt_block, row_block, col_block):
    products = lax.dot_general(src_block, tgt_block, (((0,), (0,)), ((), ())), preferred_element_type=jnp.float32)
    return jnp.exp((row_block[:, None] + col_block[None, :] + 2.0 * products) / EPS)


def reference(src_feat, tgt_feat, row_pot, col_pot, src_mass, tgt_mass, rhs_src, rhs_tgt, tile_rows, tile_cols, tile_count):
    slots_dev = tile_rows.shape[-1]
    src_wide = src_feat.astype(jnp.float32)
    tgt_wide = tgt_feat.astype(jnp.float32)
    row_term = row_pot - jnp.sum(src_wide * src_wide, axis=0)
    col_term = col_pot - jnp.sum(tgt_wide * tgt_wide, axis=0)
    src_index = jnp.arange(N_SRC, dtype=jnp.int32)[:, None, None]
    tgt_index = jnp.arange(N_TGT, dtype=jnp.int32)[None, :, None]
    row_starts = ((src_index * BLOCKS + tile_rows) * TILE).reshape(-1).astype(jnp.int32)
    col_starts = ((tgt_index * BLOCKS + tile_cols) * TILE).reshape(-1).astype(jnp.int32)
    active = (jnp.arange(slots_dev, dtype=jnp.int32)[None, None, :] < tile_count[:, :, None]).reshape(-1)

    def sweep(update, initial):
        def visit(running, item):
            row_start, col_start, live = item

            def work(inner_run):
                src_block = lax.dynamic_slice_in_dim(src_feat, row_start, TILE, 1)
                tgt_block = lax.dynamic_slice_in_dim(tgt_feat, col_start, TILE, 1)
                kernel = kernel_block(src_block, tgt_block,
                                      lax.dynamic_slice_in_dim(row_term, row_start, TILE, 0),
                                      lax.dynamic_slice_in_dim(col_term, col_start, TILE, 0))
                return update(inner_run, kernel, src_block, tgt_block, row_start, col_start)

            def keep(inner_run):
                return inner_run

            return lax.cond(live, work, keep, running), None

        final_run, unused = lax.scan(visit, initial, (row_starts, col_starts, active))
        return final_run

    def margin_update(running, kernel, src_block, tgt_block, row_start, col_start):
        return (add_into(running[0], row_start, jnp.sum(kernel, axis=1), 0),
                add_into(running[1], col_start, jnp.sum(kernel, axis=0), 0))

    zero_src = jnp.zeros((NS,), jnp.float32)
    zero_tgt = jnp.zeros((NT,), jnp.float32)
    row_marg, col_marg = sweep(margin_update, (zero_src, zero_tgt))
    diag_src = row_marg + (EPS / RHO) * src_mass * jnp.exp(-row_pot / RHO)
    diag_tgt = col_marg + (EPS / RHO) * tgt_mass * jnp.exp(-col_pot / RHO)

    def apply(pair):
        vec_src, vec_tgt = pair

        def update(running, kernel, src_block, tgt_block, row_start, col_start):
            tgt_piece = lax.dynamic_slice_in_dim(vec_tgt, col_start, TILE, 0)
            src_piece = lax.dynamic_slice_in_dim(vec_src, row_start, TILE, 0)
            return (add_into(running[0], row_start, jnp.dot(kernel, tgt_piece, precision=lax.Precision.HIGHEST), 0),
                    add_into(running[1], col_start, jnp.dot(src_piece, kernel, precision=lax.Precision.HIGHEST), 0))

        row_acc, col_acc = sweep(update, (zero_src, zero_tgt))
        return (diag_src * vec_src + row_acc, diag_tgt * vec_tgt + col_acc)

    def inner(left, right):
        return jnp.sum(left[0] * right[0]) + jnp.sum(left[1] * right[1])

    def combine(left, right, factor):
        return (left[0] + factor * right[0], left[1] + factor * right[1])

    solution = (zero_src, zero_tgt)
    residual = (rhs_src, rhs_tgt)
    direction = residual
    norm_now = inner(residual, residual)
    for step in range(ITERS):
        image = apply(direction)
        alpha = norm_now / inner(direction, image)
        solution = combine(solution, direction, alpha)
        residual = combine(residual, image, -alpha)
        norm_next = inner(residual, residual)
        direction = combine(residual, direction, norm_next / norm_now)
        norm_now = norm_next
    adjoint_src, adjoint_tgt = solution

    def grad_update(running, kernel, src_block, tgt_block, row_start, col_start):
        row_w, row_wy, col_w, col_wx = running
        weights = kernel * (lax.dynamic_slice_in_dim(adjoint_src, row_start, TILE, 0)[:, None]
                            + lax.dynamic_slice_in_dim(adjoint_tgt, col_start, TILE, 0)[None, :])
        narrow = weights.astype(jnp.bfloat16)
        row_w = add_into(row_w, row_start, jnp.sum(weights, axis=1), 0)
        col_w = add_into(col_w, col_start, jnp.sum(weights, axis=0), 0)
        row_wy = add_into(row_wy, row_start, lax.dot_general(tgt_block, narrow, (((1,), (1,)), ((), ())), preferred_element_type=jnp.float32), 1)
        col_wx = add_into(col_wx, col_start, jnp.dot(src_block, narrow, preferred_element_type=jnp.float32), 1)
        return (row_w, row_wy, col_w, col_wx)

    row_w, row_wy, col_w, col_wx = sweep(grad_update, (zero_src, jnp.zeros((F, NS), jnp.float32), zero_tgt, jnp.zeros((F, NT), jnp.float32)))
    grad_src = (2.0 / EPS) * (src_wide * row_w[None, :] - row_wy)
    grad_tgt = (2.0 / EPS) * (tgt_wide * col_w[None, :] - col_wx)
    return adjoint_src, adjoint_tgt, grad_src, grad_tgt
```

```python
import math

import jax
import jax.numpy as jnp
from jax import lax
from jax.experimental import pallas as pl
from jax.experimental.pallas import tpu as pltpu
from jax.sharding import PartitionSpec as P

TILE = 1024
FEATS = 64
LANES = 128
BLOCKS = 8
SLOTS = 8
PART = 512
EPS = 0.05
RHO = 1.0
TERM_SCALE = math.log2(math.e) / EPS
DOWN = 2.0**-40
UP = 2.0**40
F32 = jnp.float32
BF16 = jnp.bfloat16
VMEM = pl.BlockSpec(memory_space=pltpu.VMEM)
SMEM = pl.BlockSpec(memory_space=pltpu.SMEM)
ANY = pl.BlockSpec(memory_space=pl.ANY)
HBM = pl.BlockSpec(memory_space=pltpu.HBM)
RING = (0, -1, 1, -2, 2, -3, 3, 4)
QUAD = (0, 1, -1, 2)


def params(mib):
    return pltpu.CompilerParams(vmem_limit_bytes=mib * 2**20)


def shape(dims, dtype=F32):
    return jax.ShapeDtypeStruct(dims, dtype)


def split3(value):
    high = value.astype(BF16).astype(F32)
    rest = value - high
    middle = rest.astype(BF16).astype(F32)
    low = (rest - middle).astype(BF16).astype(F32)
    return high, middle, low


def payload_kernel(*refs):
    sources, (out_s, out_t), held, sems = refs[:8], refs[8:10], refs[10:18], refs[18]
    copies = [
        pltpu.make_async_copy(source, place, sems.at[i])
        for i, (source, place) in enumerate(zip(sources, held))
    ]
    for copy in copies:
        copy.start()
    for copy in copies:
        copy.wait()
    sf, tf, rp, cp, sm, tm, rs, rt = held
    for feat, pot, mass, rhs, out, first in (
        (sf, rp, sm, rs, out_s, True),
        (tf, cp, tm, rt, out_t, False),
    ):
        wide = feat[...].astype(F32)
        potential = pot[...]
        term = (potential - jnp.sum(wide * wide, axis=0, keepdims=True)) * TERM_SCALE
        damp = EPS / RHO * mass[...] * jnp.exp(-potential / RHO)
        ones = jnp.ones((3, PART), F32)
        pieces = list(split3(term))
        rows = pieces + [ones] if first else [ones] + pieces
        rows += list(split3(rhs[...])) + list(split3(damp))
        rows.append(jnp.zeros((4, PART), F32))
        out[0:FEATS, :] = feat[...]
        out[FEATS : FEATS + 16, :] = jnp.concatenate(rows, axis=0).astype(BF16)


def three(rows, start):
    return rows[start : start + 1] + (rows[start + 1 : start + 2] + rows[start + 2 : start + 3])


def column_of(row):
    return jnp.broadcast_to(row, (LANES, TILE)).T


def lane_sum(partial):
    return jnp.sum(partial.T, axis=0, keepdims=True)


def lane_blocks(row, height):
    return [
        jnp.broadcast_to(row[:, LANES * l : LANES * (l + 1)], (height, LANES))
        for l in range(TILE // LANES)
    ]


def add_row(ref, index, row):
    ref[pl.ds(index, 1), :] = ref[pl.ds(index, 1), :] + row


def total(values):
    result = values[0]
    for value in values[1:]:
        result = result + value
    return result


def pair_of(ref, block):
    return jnp.concatenate([ref[2 * block], ref[2 * block + 1]], axis=1)


def ring_block(me, dz, other):
    place = lax.rem(me // 2 + (dz + 8), 8)
    core = lax.rem(me, 2)
    return 2 * place + (1 - core if other else core)


def quad_block(me, dy, dx):
    return 4 * lax.rem(me // 4 + (dy + 4), 4) + lax.rem(lax.rem(me, 4) + (dx + 4), 4)


def build_kernel(
    meta, s0, s1, t0, t1, t2, t3, t4,
    kern, xs, ys, bp, bq, dp, dq, rsum, csum,
    left, right, sums, prods, pcol, sems,
):
    me_s, me_t = meta[17], meta[18]
    copies = []
    for k in range(8):
        for other, stack in enumerate((s0, s1)):
            copies.append((stack.at[k], xs.at[ring_block(me_t, RING[k], other)]))
    for k in range(4):
        far = (t3.at[k] if k < 2 else t4.at[k - 2])
        for dx, piece in ((0, t0.at[k]), (1, t2.at[k]), (-1, t1.at[k]), (2, far)):
            copies.append((piece, ys.at[quad_block(me_s, QUAD[k], dx)]))
    copies = [
        pltpu.make_async_copy(source, place, sems.at[i])
        for i, (source, place) in enumerate(copies)
    ]
    for copy in copies:
        copy.start()
    rsum[...] = jnp.zeros_like(rsum)
    csum[...] = jnp.zeros_like(csum)
    for copy in copies:
        copy.wait()
    for block in range(BLOCKS):
        for ref, vec, damp in ((xs, bp, dp), (ys, bq, dq)):
            for side in range(2):
                rows = ref[2 * block + side, FEATS : FEATS + 16, :].astype(F32)
                cells = slice(PART * side, PART * (side + 1))
                vec[block : block + 1, cells] = three(rows, 6)
                damp[block : block + 1, cells] = three(rows, 9)

    def tile(slot, carry):
        rb, cb = meta[slot], meta[8 + slot]
        x = pair_of(xs, rb)
        y = pair_of(ys, cb)
        keep = lax.broadcasted_iota(jnp.int32, (16, TILE), 0) < 6
        xt = jnp.where(keep, x[FEATS:].astype(F32), 0.0)
        yt = jnp.where(keep, y[FEATS:].astype(F32), 0.0)
        scaled = x[:FEATS].astype(F32) * (2.0 * TERM_SCALE)
        zeros = jnp.zeros((48, TILE), F32)
        left[...] = jnp.concatenate([*split3(scaled), xt, zeros], axis=0).astype(BF16).T
        yf = y[:FEATS]
        right[...] = jnp.concatenate(
            [yf, yf, yf, jnp.concatenate([yt, zeros], axis=0).astype(BF16)], axis=0
        )
        for strip in range(4):
            cells = slice(256 * strip, 256 * (strip + 1))
            kern[slot, :, cells] = jnp.dot(
                left[...], right[:, cells], preferred_element_type=F32
            )
        q = lane_blocks(bq[pl.ds(cb, 1), :], 8)
        pcol[...] = column_of(bp[pl.ds(rb, 1), :])
        count = TILE // LANES

        def rows_of(step, accs):
            csums, cprods = accs
            for u in range(4):
                at = pl.ds(pl.multiple_of(step * 32 + 8 * u, 8), 8)
                ks = [
                    jnp.exp2(kern[slot, at, LANES * l : LANES * (l + 1)]) for l in range(count)
                ]
                for l in range(count):
                    kern[slot, at, LANES * l : LANES * (l + 1)] = ks[l]
                p = pcol[at, :]
                sums[at, :] = total(ks)
                prods[at, :] = total([ks[l] * q[l] for l in range(count)])
                csums = tuple(csums[l] + ks[l] for l in range(count))
                cprods = tuple(cprods[l] + ks[l] * p for l in range(count))
            return csums, cprods

        zero = tuple(jnp.zeros((8, LANES), F32) for l in range(count))
        csums, cprods = lax.fori_loop(0, TILE // 32, rows_of, (zero, zero))
        add_row(rsum, rb, lane_sum(sums[...]))
        add_row(rsum, 8 + rb, lane_sum(prods[...]))
        add_row(csum, cb, jnp.sum(jnp.concatenate(csums, axis=1), axis=0, keepdims=True))
        add_row(csum, 8 + cb, jnp.sum(jnp.concatenate(cprods, axis=1), axis=0, keepdims=True))
        return carry

    lax.fori_loop(0, meta[16], tile, 0)


def lane_partial(value):
    rows = jnp.sum(value, axis=0, keepdims=True)
    return total([rows[:, LANES * l : LANES * (l + 1)] for l in range(TILE // LANES)])


def lane_largest(value):
    rows = jnp.max(value, axis=0, keepdims=True)
    result = rows[:, :LANES]
    for l in range(1, TILE // LANES):
        result = jnp.maximum(result, rows[:, LANES * l : LANES * (l + 1)])
    return result


def scalar(row):
    return jnp.sum(row, axis=1, keepdims=True)


def both_of(pieces):
    return pieces[0][...] + pieces[1][...]


def unpack(value):
    return jnp.concatenate(
        [value[BLOCKS * l : BLOCKS * (l + 1)] for l in range(TILE // LANES)], axis=1
    )


def pack_into(out, value):
    for l in range(TILE // LANES):
        out[BLOCKS * l : BLOCKS * (l + 1), :] = value[:, LANES * l : LANES * (l + 1)]


def apply_kernel(
    meta, r0, r1, c0, c1, bp, bq, dp, dq, kern,
    v1p, v1q, gp, gq, rout, cout,
    prods, pcol, rimg, cimg,
):
    rows = both_of((r0, r1))
    cols = both_of((c0, c1))
    gp[...] = rows[:8] + dp[...]
    gq[...] = cols[:8] + dq[...]
    v1p[...] = gp[...] * (bp[...] * DOWN) + rows[8:] * DOWN
    v1q[...] = gq[...] * (bq[...] * DOWN) + cols[8:] * DOWN
    rimg[...] = jnp.zeros_like(rimg)
    cimg[...] = jnp.zeros_like(cimg)
    for b, v, g, out in ((bp, v1p, gp, cout), (bq, v1q, gq, rout)):
        out[64:72, :] = jnp.zeros((8, LANES), F32)
        for place, value in enumerate(
            (
                lane_partial(b[...] * b[...]),
                lane_partial(b[...] * v[...]),
                lane_partial(v[...] * v[...]),
                lane_largest(g[...]),
            )
        ):
            out[64 + place : 65 + place, :] = value
    count = TILE // LANES

    def tile(slot, carry):
        rb, cb = meta[slot], meta[8 + slot]
        q = lane_blocks(v1q[pl.ds(cb, 1), :], 8)
        pcol[...] = column_of(v1p[pl.ds(rb, 1), :])

        def rows_of(step, cprods):
            for u in range(4):
                at = pl.ds(pl.multiple_of(step * 32 + 8 * u, 8), 8)
                ks = [kern[slot, at, LANES * l : LANES * (l + 1)] for l in range(count)]
                p = pcol[at, :]
                prods[at, :] = total([ks[l] * q[l] for l in range(count)])
                cprods = tuple(cprods[l] + ks[l] * p for l in range(count))
            return cprods

        zero = tuple(jnp.zeros((8, LANES), F32) for l in range(count))
        cprods = lax.fori_loop(0, TILE // 32, rows_of, zero)
        add_row(rimg, rb, lane_sum(prods[...]))
        add_row(cimg, cb, jnp.sum(jnp.concatenate(cprods, axis=1), axis=0, keepdims=True))
        return carry

    lax.fori_loop(0, meta[16], tile, 0)
    pack_into(rout, rimg[...])
    pack_into(cout, cimg[...])


def form_kernel(
    meta, r0, r1, c0, c1, bp, bq, v1p, v1q, gp, gq, kern,
    e1p, e1q, wp, wq, hp, hq, dots, known,
    pcol, acc,
):
    rows = both_of((r0, r1))
    cols = both_of((c0, c1))
    both = rows[64:72] + cols[64:72]
    bb, bv, vv, sigma = (scalar(both[i : i + 1]) for i in range(4))
    rows, cols = unpack(rows), unpack(cols)
    inverse = 1.0 / sigma
    lift = UP * inverse
    alpha = bb / (bv * lift)
    dots[...] = jnp.zeros_like(dots)
    known[...] = jnp.zeros_like(known)
    known[0:1, :] = jnp.broadcast_to(bb, (1, LANES))
    known[1:2, :] = jnp.broadcast_to(bv * lift, (1, LANES))
    known[2:3, :] = jnp.broadcast_to((vv * lift) * lift, (1, LANES))
    known[3:4, :] = jnp.broadcast_to(inverse, (1, LANES))
    found = []
    for b, v1, g, image, e1, w, h in (
        (bp, v1p, gp, rows, e1p, wp, hp),
        (bq, v1q, gq, cols, e1q, wq, hq),
    ):
        second = g[...] * v1[...] + image
        first = v1[...] * lift
        next_image = (second * lift) * inverse
        residual = b[...] - alpha * first
        turned = first - alpha * next_image
        e1[...] = residual
        w[...] = turned
        h[...] = first
        found.append(
            (
                lane_partial(residual * residual),
                lane_partial(residual * turned),
                lane_partial(residual * first),
                lane_partial(turned * turned),
                lane_partial(turned * first),
                lane_partial(next_image * turned),
                lane_partial(first * next_image),
                lane_partial((g[...] * inverse) * turned * turned),
            )
        )
    count = TILE // LANES
    acc[...] = jnp.zeros_like(acc)

    def tile(slot, carry):
        rb, cb = meta[slot], meta[8 + slot]
        q = lane_blocks(wq[pl.ds(cb, 1), :] * inverse, 8)
        pcol[...] = column_of(wp[pl.ds(rb, 1), :])

        def rows_of(step, cprods):
            for u in range(4):
                at = pl.ds(pl.multiple_of(step * 32 + 8 * u, 8), 8)
                p = pcol[at, :]
                cprods = tuple(
                    cprods[l] + kern[slot, at, LANES * l : LANES * (l + 1)] * p
                    for l in range(count)
                )
            return cprods

        zero = tuple(jnp.zeros((8, LANES), F32) for l in range(count))
        cprods = lax.fori_loop(0, TILE // 32, rows_of, zero)
        acc[...] = acc[...] + total([cprods[l] * q[l] for l in range(count)])
        return carry

    lax.fori_loop(0, meta[16], tile, 0)
    for place in range(8):
        value = (found[0][place] + found[1][place]) * (1.0 / 16.0)
        if place == 7:
            value = value + 2.0 * jnp.sum(acc[...], axis=0, keepdims=True)
        dots[place : place + 1, :] = value


def grad_kernel(
    meta, q0, q1, known, bp, bq, e1p, e1q, wp, wq, hp, hq, xs, ys, kern,
    adj_s, adj_t, near, far, x0, x1, x2, x3, x4,
    ap, aq, pcol, half, sums, row_w, col_w, row_wy, col_wx,
):
    me_s, me_t = meta[17], meta[18]
    dots = both_of((q0, q1))
    ee, ew, eh, ww, wh, uw, hu, waw = (scalar(dots[i : i + 1]) for i in range(8))
    bb, bh, hh, inverse = (known[i : i + 1, 0:1] for i in range(4))
    alpha1 = bb / bh
    beta1 = ee / bb
    dad = ew + 2.0 * beta1 * eh + beta1 * beta1 * bh
    alpha2 = ee / dad
    e_ad = ew + beta1 * eh
    ad_ad = ww + 2.0 * beta1 * wh + beta1 * beta1 * hh
    rr2 = ee - 2.0 * alpha2 * e_ad + alpha2 * alpha2 * ad_ad
    beta2 = rr2 / ee
    form = waw + 2.0 * beta1 * uw + beta1 * beta1 * hu
    r_ar = ew - 2.0 * alpha2 * (ww + beta1 * wh) + alpha2 * alpha2 * form
    cross = ew + beta1 * eh - alpha2 * ad_ad
    d2_ar2 = cross
    d3ad3 = r_ar + 2.0 * beta2 * d2_ar2 + beta2 * beta2 * dad
    alpha3 = rr2 / d3ad3
    on_b = (alpha1 + alpha2 * beta1 + alpha3 * beta2 * beta1) * inverse
    on_e = (alpha2 + alpha3 * (1.0 + beta2)) * inverse
    on_w = -(alpha3 * alpha2) * inverse
    on_h = on_w * beta1
    ap[...] = on_b * bp[...] + on_e * e1p[...] + on_w * wp[...] + on_h * hp[...]
    aq[...] = on_b * bq[...] + on_e * e1q[...] + on_w * wq[...] + on_h * hq[...]
    for me, vec, out in ((me_t, ap, adj_s), (me_s, aq, adj_t)):
        row = vec[pl.ds(me // 2, 1), :]
        out[...] = jnp.where(me % 2 == 1, row[:, PART:], row[:, :PART])
    row_w[...] = jnp.zeros_like(row_w)
    col_w[...] = jnp.zeros_like(col_w)
    row_wy[...] = jnp.zeros_like(row_wy)
    col_wx[...] = jnp.zeros_like(col_wx)
    count = TILE // LANES

    def tile(slot, carry):
        rb, cb = meta[slot], meta[8 + slot]
        q = lane_blocks(aq[pl.ds(cb, 1), :], 16)
        pcol[...] = column_of(ap[pl.ds(rb, 1), :])

        def rows_of(step, csums):
            for u in range(2):
                at = pl.ds(pl.multiple_of(step * 32 + 16 * u, 16), 16)
                p = pcol[at, :]
                ws = [
                    kern[slot, at, LANES * l : LANES * (l + 1)] * (p + q[l]) for l in range(count)
                ]
                for l in range(count):
                    half[at, LANES * l : LANES * (l + 1)] = ws[l].astype(BF16)
                sums[at, :] = total(ws)
                csums = tuple(csums[l] + (ws[l][:8] + ws[l][8:]) for l in range(count))
            return csums

        zero = tuple(jnp.zeros((8, LANES), F32) for l in range(count))
        csums = lax.fori_loop(0, TILE // 32, rows_of, zero)
        add_row(row_w, rb, lane_sum(sums[...]))
        add_row(col_w, cb, jnp.sum(jnp.concatenate(csums, axis=1), axis=0, keepdims=True))
        x = jnp.concatenate([xs[2 * rb, :FEATS], xs[2 * rb + 1, :FEATS]], axis=1)
        y = jnp.concatenate([ys[2 * cb, :FEATS], ys[2 * cb + 1, :FEATS]], axis=1)
        row_wy[rb] = row_wy[rb] + lax.dot_general(
            y, half[...], (((1,), (1,)), ((), ())), preferred_element_type=F32
        )
        col_wx[cb] = col_wx[cb] + jnp.dot(x, half[...], preferred_element_type=F32)
        return carry

    lax.fori_loop(0, meta[16], tile, 0)

    def part_of(feat, weight, mixed, block):
        wide = feat[block, :FEATS, :].astype(F32)
        row = weight[pl.ds(block // 2, 1), :]
        odd = block % 2 == 1
        mine = jnp.where(odd, row[:, PART:], row[:, :PART])
        whole = mixed[block // 2]
        return (2.0 / EPS) * (wide * mine - jnp.where(odd, whole[:, PART:], whole[:, :PART]))

    for k in range(8):
        for other, out in enumerate((near, far)):
            out[k] = part_of(xs, row_w, row_wy, ring_block(me_t, RING[k], other))
    for k in range(4):
        for dx, out in ((0, x0), (1, x1), (-1, x2), (2, None)):
            part = part_of(ys, col_w, col_wx, quad_block(me_s, QUAD[k], dx))
            if out is None:
                x3[k] = part[:32]
                x4[k] = part[32:]
            else:
                out[k] = part


def swap(value, axis, mask):
    return lax.ppermute(value, axis, [(i, i ^ mask) for i in range(16)])


def along_z(value, step):
    return lax.ppermute(value, "tgt", [(i, (i + 2 * step) % 16) for i in range(16)])


def along_y(value, step):
    return lax.ppermute(value, "src", [(i, (i + 4 * step) % 16) for i in range(16)])


def along_x(value, step):
    return lax.ppermute(value, "src", [(i, i // 4 * 4 + (i + step) % 4) for i in range(16)])


def doubled(value, axis):
    for mask in (1, 2, 4):
        value = value + swap(value, axis, mask)
    return value


def sum_pieces(row, col):
    for mask in (1, 2, 4):
        row, col = row + swap(row, "tgt", mask), col + swap(col, "src", mask)
    return (row, swap(row, "tgt", 8)), (col, swap(col, "src", 8))


def gather_ring(own):
    up = [own]
    down = [own]
    for step in range(4):
        up.append(along_z(up[-1], 1))
        if step < 3:
            down.append(along_z(down[-1], -1))
    stack = jnp.stack([own, up[1], down[1], up[2], down[2], up[3], down[3], up[4]])
    return stack, swap(stack, "tgt", 1)


def gather_quad(own):
    up, down = along_y(own, 1), along_y(own, -1)
    stack = jnp.stack([own, down, up, along_y(up, 1)])
    right, left = along_x(stack, 1), along_x(stack, -1)
    return stack, right, left, along_x(right[:2], 1), along_x(left[2:], -1)


def scatter_ring(near, far):
    near = near + swap(far, "tgt", 1)
    piece = {dz: near[k] for k, dz in enumerate(RING)}
    up, down = along_z(piece[4], 1), along_z(piece[-3], -1)
    up, down = along_z(piece[3] + up, 1), along_z(piece[-2] + down, -1)
    up, down = along_z(piece[2] + up, 1), along_z(piece[-1] + down, -1)
    up = along_z(piece[1] + up, 1)
    return piece[0] + up + down


def scatter_quad(own, next_up, next_down, across_top, across_bottom, along):
    half = FEATS // 2
    top, bottom = along(across_top, 1), along(across_bottom, -1)
    up = jnp.concatenate([next_up[..., :half, :] + top, next_up[..., half:, :]], axis=-2)
    down = jnp.concatenate([next_down[..., :half, :], next_down[..., half:, :] + bottom], axis=-2)
    return own + along(up, 1) + along(down, -1)


def shards(
    src_feat, tgt_feat, row_pot, col_pot, src_mass, tgt_mass, rhs_src, rhs_tgt,
    tile_rows, tile_cols, tile_count,
):
    me_s, me_t = lax.axis_index("src"), lax.axis_index("tgt")
    meta = jnp.concatenate(
        [
            tile_rows.reshape(8),
            tile_cols.reshape(8),
            tile_count.reshape(1),
            me_s.reshape(1).astype(jnp.int32),
            me_t.reshape(1).astype(jnp.int32),
        ]
    )
    line = lambda v: v.reshape(1, PART)
    pay = (FEATS + 16, PART)
    pay_s, pay_t = pl.pallas_call(
        payload_kernel,
        out_shape=[shape(pay, BF16), shape(pay, BF16)],
        in_specs=[HBM] * 8,
        out_specs=[VMEM] * 2,
        scratch_shapes=[pltpu.VMEM((FEATS, PART), BF16)] * 2
        + [pltpu.VMEM((1, PART), F32)] * 6
        + [pltpu.SemaphoreType.DMA((8,))],
        compiler_params=params(24),
    )(
        src_feat, tgt_feat, line(row_pot), line(col_pot), line(src_mass), line(tgt_mass),
        line(rhs_src), line(rhs_tgt),
    )
    s_parts = gather_ring(pay_s)
    t_parts = gather_quad(pay_t)

    vec = shape((BLOCKS, TILE))
    two = shape((2 * BLOCKS, TILE))
    feats = shape((16, *pay), BF16)
    kern, xs, ys, bp, bq, dp, dq, rsum, csum = pl.pallas_call(
        build_kernel,
        out_shape=[
            pltpu.VMEM((SLOTS, TILE, TILE), F32), feats, feats, vec, vec, vec, vec, two, two,
        ],
        in_specs=[SMEM] + [ANY] * 7,
        out_specs=[VMEM] * 9,
        scratch_shapes=[
            pltpu.VMEM((TILE, 256), BF16),
            pltpu.VMEM((256, TILE), BF16),
            pltpu.VMEM((TILE, LANES), F32),
            pltpu.VMEM((TILE, LANES), F32),
            pltpu.VMEM((TILE, LANES), F32),
            pltpu.SemaphoreType.DMA((32,)),
        ],
        compiler_params=params(24),
    )(meta, *s_parts, *t_parts)
    kern = pltpu.with_memory_space_constraint(kern, pltpu.VMEM)

    row_pieces, col_pieces = sum_pieces(rsum, csum)
    v1p, v1q, gp, gq, rimg, cimg = pl.pallas_call(
        apply_kernel,
        out_shape=[vec, vec, vec, vec] + [shape((72, LANES))] * 2,
        in_specs=[SMEM] + [VMEM] * 9,
        out_specs=[VMEM] * 6,
        scratch_shapes=[pltpu.VMEM((TILE, LANES), F32)] * 2
        + [pltpu.VMEM((BLOCKS, TILE), F32)] * 2,
        compiler_params=params(24),
    )(meta, *row_pieces, *col_pieces, bp, bq, dp, dq, kern)

    row_pieces, col_pieces = sum_pieces(rimg, cimg)
    e1p, e1q, wp, wq, hp, hq, dots, known = pl.pallas_call(
        form_kernel,
        out_shape=[vec] * 6 + [shape((8, LANES))] * 2,
        in_specs=[SMEM] + [VMEM] * 11,
        out_specs=[VMEM] * 8,
        scratch_shapes=[pltpu.VMEM((TILE, LANES), F32), pltpu.VMEM((8, LANES), F32)],
        compiler_params=params(24),
    )(meta, *row_pieces, *col_pieces, bp, bq, v1p, v1q, gp, gq, kern)

    dots = doubled(dots, "tgt")
    dots = dots + swap(dots, "tgt", 8)
    dots = doubled(dots, "src")
    dots = (dots, swap(dots, "src", 8))
    outs = pl.pallas_call(
        grad_kernel,
        out_shape=[shape((1, PART))] * 2
        + [shape((8, FEATS, PART))] * 2
        + [shape((4, FEATS, PART))] * 3
        + [shape((4, FEATS // 2, PART))] * 2,
        in_specs=[SMEM] + [VMEM] * 14,
        out_specs=[VMEM] * 9,
        scratch_shapes=[
            pltpu.VMEM((BLOCKS, TILE), F32),
            pltpu.VMEM((BLOCKS, TILE), F32),
            pltpu.VMEM((TILE, LANES), F32),
            pltpu.VMEM((TILE, TILE), BF16),
            pltpu.VMEM((TILE, LANES), F32),
            pltpu.VMEM((BLOCKS, TILE), F32),
            pltpu.VMEM((BLOCKS, TILE), F32),
            pltpu.VMEM((BLOCKS, FEATS, TILE), F32),
            pltpu.VMEM((BLOCKS, FEATS, TILE), F32),
        ],
        compiler_params=params(24),
    )(meta, *dots, known, bp, bq, e1p, e1q, wp, wq, hp, hq, xs, ys, kern)
    adj_s, adj_t, near, far = outs[:4]
    grad_src = scatter_ring(near, far)
    part = scatter_quad(*outs[4:], along_x)
    half = FEATS // 2
    grad_tgt = scatter_quad(part[0], part[1], part[2], part[3, :half], part[3, half:], along_y)
    return adj_s.reshape(PART), adj_t.reshape(PART), grad_src, grad_tgt


def solution(mesh):
    in_specs = (
        P(None, ("src", "tgt")),
        P(None, ("tgt", "src")),
        P(("src", "tgt")),
        P(("tgt", "src")),
        P(("src", "tgt")),
        P(("tgt", "src")),
        P(("src", "tgt")),
        P(("tgt", "src")),
        P("src", "tgt", None),
        P("src", "tgt", None),
        P("src", "tgt"),
    )
    out_specs = (
        P(("src", "tgt")),
        P(("tgt", "src")),
        P(None, ("src", "tgt")),
        P(None, ("tgt", "src")),
    )
    return jax.shard_map(shards, mesh=mesh, in_specs=in_specs, out_specs=out_specs, check_vma=False)
```

```python
import math

import jax
import jax.numpy as jnp
from jax import lax
from jax.experimental import pallas as pl
from jax.experimental.pallas import tpu as pltpu
from jax.sharding import PartitionSpec as P

TILE = 1024
FEATS = 64
LANES = 128
BLOCKS = 8
SLOTS = 8
PART = 512
EPS = 0.05
RHO = 1.0
SCALE = 2.0 * math.log2(math.e) / EPS
DOWN = 2.0**-40
UP = 2.0**40
F32 = jnp.float32
BF16 = jnp.bfloat16
VMEM = pl.BlockSpec(memory_space=pltpu.VMEM)
SMEM = pl.BlockSpec(memory_space=pltpu.SMEM)
ANY = pl.BlockSpec(memory_space=pl.ANY)
HBM = pl.BlockSpec(memory_space=pltpu.HBM)
RING = (0, -1, 1, 4, -2, -3, 2, 3)
QUAD = (0, 1, -1, 2)


def params(mib):
    return pltpu.CompilerParams(vmem_limit_bytes=mib * 2**20)


def shape(dims, dtype=F32):
    return jax.ShapeDtypeStruct(dims, dtype)


def split3(value):
    high = value.astype(BF16).astype(F32)
    rest = value - high
    middle = rest.astype(BF16).astype(F32)
    low = (rest - middle).astype(BF16).astype(F32)
    return high, middle, low


def to_positions(value, turned):
    turned[...] = value.T
    groups = [turned[pl.ds(g, 8, stride=64), :] for g in range(64)]
    return jnp.concatenate(groups, axis=0).T


def to_cells(value, turned):
    turned[...] = value.T
    groups = [turned[pl.ds(r, 64, stride=8), :] for r in range(8)]
    return jnp.concatenate(groups, axis=0).T


def payload_kernel(*refs):
    sources, (out_s, out_t), held = refs[:8], refs[8:10], refs[10:18]
    turned, sems = refs[18:]
    copies = [
        pltpu.make_async_copy(source, place, sems.at[i])
        for i, (source, place) in enumerate(zip(sources, held))
    ]
    for copy in copies:
        copy.start()
    for copy in copies:
        copy.wait()
    sf, tf, rp, cp, sm, tm, rs, rt = held
    for feat, pot, mass, rhs, out, first in (
        (sf, rp, sm, rs, out_s, True),
        (tf, cp, tm, rt, out_t, False),
    ):
        wide = feat[...].astype(F32)
        potential = pot[...]
        term = (potential - jnp.sum(wide * wide, axis=0, keepdims=True)) * 0.5
        damp = EPS / RHO * mass[...] * jnp.exp(-potential / RHO)
        ones = jnp.ones((3, PART), F32)
        pieces = list(split3(term))
        rows = pieces + [ones] if first else [ones] + pieces
        rows += list(split3(rhs[...])) + list(split3(damp))
        rows.append(jnp.zeros((4, PART), F32))
        tail = jnp.concatenate(rows, axis=0)
        if first:
            whole = jnp.concatenate([wide, tail, jnp.zeros((48, PART), F32)], axis=0)
            whole = to_positions(whole, turned)
            out[0:FEATS, :] = whole[:FEATS].astype(BF16)
            keep = lax.broadcasted_iota(jnp.int32, (16, PART), 0) < 6
            tail = jnp.where(keep, whole[FEATS : FEATS + 16], tail)
        else:
            out[0:FEATS, :] = feat[...]
        out[FEATS : FEATS + 16, :] = tail.astype(BF16)


def three(rows, start):
    return rows[start : start + 1] + (rows[start + 1 : start + 2] + rows[start + 2 : start + 3])


def lane_blocks(row, height):
    return [
        jnp.broadcast_to(row[:, LANES * l : LANES * (l + 1)], (height, LANES))
        for l in range(TILE // LANES)
    ]


def total(values):
    result = values[0]
    for value in values[1:]:
        result = result + value
    return result


def block_rows(block):
    return pl.ds(pl.multiple_of(8 * block, 8), 8)


def fill_columns(column, packed):
    for g in range(LANES):
        column[8 * g : 8 * g + 8, :] = jnp.broadcast_to(packed[:, g : g + 1], (8, LANES))


def lane_sums(partial):
    lane = lax.broadcasted_iota(jnp.int32, (8, LANES), 1)
    result = jnp.zeros((8, LANES), F32)
    for g in range(LANES):
        group = jnp.sum(partial[8 * g : 8 * g + 8, :], axis=1, keepdims=True)
        result = jnp.where(lane == g, group, result)
    return result


def add_block(ref, first, block, value):
    rows = pl.ds(pl.multiple_of(first + 8 * block, 8), 8)
    ref[rows, :] = ref[rows, :] + value


def add_sums(ref, index, sums):
    row = jnp.sum(jnp.concatenate(sums, axis=1), axis=0, keepdims=True)
    ref[pl.ds(index, 1), :] = ref[pl.ds(index, 1), :] + row


def unpack(value):
    return jnp.concatenate(
        [value[BLOCKS * l : BLOCKS * (l + 1)] for l in range(TILE // LANES)], axis=1
    )


def pack_into(out, first, value):
    for l in range(TILE // LANES):
        out[first + BLOCKS * l : first + BLOCKS * (l + 1), :] = value[:, LANES * l : LANES * (l + 1)]


def pair_of(ref, block):
    return jnp.concatenate([ref[2 * block], ref[2 * block + 1]], axis=1)


def ring_block(me, dz, other):
    place = lax.rem(me // 2 + (dz + 8), 8)
    core = lax.rem(me, 2)
    return 2 * place + (1 - core if other else core)


def quad_block(me, dy, dx):
    return 4 * lax.rem(me // 4 + (dy + 4), 4) + lax.rem(lax.rem(me, 4) + (dx + 4), 4)


def fetch(kern, held, sems, slot):
    place = lax.rem(slot, 3)
    return pltpu.make_async_copy(kern.at[slot], held.at[place], sems.at[place])


def start_fetching(kern, held, sems, count):
    fetch(kern, held, sems, 0).start()

    @pl.when(count > 1)
    def _():
        fetch(kern, held, sems, 1).start()


def next_tile(kern, held, sems, slot, count):
    @pl.when(slot + 2 < count)
    def _():
        fetch(kern, held, sems, slot + 2).start()

    fetch(kern, held, sems, slot).wait()
    return held.at[lax.rem(slot, 3)]


WIDE = TILE // LANES


def no_sums():
    return tuple(jnp.zeros((8, LANES), F32) for l in range(WIDE))


def lanes_of(l):
    return slice(LANES * l, LANES * (l + 1))


def build_kernel(
    meta, s0, s1, t0, t1, t2, t3, t4,
    kern, stored, xs, ys, pb, qb, rout, cout,
    left, right, sums, prods, column, csum, parts, sems, out_sems,
):
    me_s, me_t = meta[17], meta[18]
    copies = []
    for k in range(8):
        for other, stack in enumerate((s0, s1)):
            copies.append((stack.at[k], xs.at[ring_block(me_t, RING[k], other)]))
    for k in range(4):
        far = (t3.at[k] if k < 2 else t4.at[k - 2])
        for dx, piece in ((0, t0.at[k]), (1, t2.at[k]), (-1, t1.at[k]), (2, far)):
            copies.append((piece, ys.at[quad_block(me_s, QUAD[k], dx)]))
    copies = [
        pltpu.make_async_copy(source, place, sems.at[i])
        for i, (source, place) in enumerate(copies)
    ]
    for copy in copies:
        copy.start()
    rout[...] = jnp.zeros_like(rout)
    csum[...] = jnp.zeros_like(csum)
    for copy in copies:
        copy.wait()
    for part in range(16):
        for place, ref in ((0, xs), (2, ys)):
            rows = ref[part, FEATS : FEATS + 16, :].astype(F32)
            at = part // 2 + 8 * (part % 2)
            parts[place, at : at + 1, :] = three(rows, 6)
            parts[place + 1, at : at + 1, :] = three(rows, 9)
    for place in range(2):
        even, odd = parts[place, 0:8, :], parts[place, 8:16, :]
        for r in range(8):
            cells = slice(64 * r, 64 * (r + 1))
            pb[pl.ds(64 * place + r, 8, stride=8), :] = jnp.concatenate(
                [even[:, cells], odd[:, cells]], axis=1
            )
        for side in range(2):
            qb[8 * place : 8 * place + 8, PART * side : PART * (side + 1)] = parts[
                2 + place, 8 * side : 8 * side + 8, :
            ]

    def store(slot):
        return pltpu.make_async_copy(kern.at[slot], stored.at[slot], out_sems.at[slot])

    keep = lax.broadcasted_iota(jnp.int32, (16, TILE), 0) < 6
    blank = jnp.zeros((48, TILE), BF16)

    def with_terms(payload):
        terms = jnp.where(keep, payload[FEATS:].astype(F32), 0.0).astype(BF16)
        return jnp.concatenate([payload[:FEATS], terms, blank], axis=0)

    def tile(slot, carry):
        rb, cb = meta[slot], meta[8 + slot]
        kernel = kern.at[slot]
        left[...] = with_terms(pair_of(xs, rb)).T
        right[...] = with_terms(pair_of(ys, cb))
        for strip in range(4):
            cells = slice(256 * strip, 256 * (strip + 1))
            kernel[:, cells] = jnp.dot(left[...], right[:, cells], preferred_element_type=F32)
        q = lane_blocks(qb[pl.ds(cb, 1), :], 8)
        fill_columns(column, pb[block_rows(rb), :])

        def rows_of(step, accs):
            csums, cprods = accs
            for u in range(4):
                at = pl.ds(pl.multiple_of(step * 32 + 8 * u, 8), 8)
                ks = [jnp.exp2(kernel[at, lanes_of(l)] * SCALE) for l in range(WIDE)]
                for l in range(WIDE):
                    kernel[at, lanes_of(l)] = ks[l]
                p = column[at, :]
                sums[at, :] = total(ks)
                prods[at, :] = total([ks[l] * q[l] for l in range(WIDE)])
                csums = tuple(csums[l] + ks[l] for l in range(WIDE))
                cprods = tuple(cprods[l] + ks[l] * p for l in range(WIDE))
            return csums, cprods

        csums, cprods = lax.fori_loop(0, TILE // 32, rows_of, (no_sums(), no_sums()))
        store(slot).start()
        add_block(rout, 0, rb, lane_sums(sums))
        add_block(rout, 64, rb, lane_sums(prods))
        add_sums(csum, cb, csums)
        add_sums(csum, 8 + cb, cprods)
        return carry

    count = meta[16]
    lax.fori_loop(0, count, tile, 0)
    pack_into(cout, 0, csum[:8, :])
    pack_into(cout, 64, csum[8:, :])

    def finish(slot, carry):
        store(slot).wait()
        return carry

    lax.fori_loop(0, count, finish, 0)


def folded(value, join):
    if value.shape[1] == LANES:
        return value
    result = value[:, :LANES]
    for l in range(1, WIDE):
        result = join(result, value[:, lanes_of(l)])
    return result


def lane_partial(value):
    return folded(jnp.sum(value, axis=0, keepdims=True), jnp.add)


def lane_largest(value):
    return folded(jnp.max(value, axis=0, keepdims=True), jnp.maximum)


def scalar(row):
    return jnp.sum(row, axis=1, keepdims=True)


def apply_kernel(
    meta, rows_in, cols_in, pb, qb, kern,
    pv, qv, rout, cout,
    prods, column, csum,
):
    rows = (rows_in[:64, :], rows_in[64:, :])
    cols = (unpack(cols_in[:64, :]), unpack(cols_in[64:, :]))
    rout[...] = jnp.zeros_like(rout)
    csum[...] = jnp.zeros_like(csum)
    cout[64:128, :] = jnp.zeros((64, LANES), F32)
    for (marg, prod), given, out, image, height in (
        (rows, pb, pv, cout, 64),
        (cols, qb, qv, rout, 8),
    ):
        b, d = given[:height, :], given[height:, :]
        g = marg + d
        v = g * (b * DOWN) + prod * DOWN
        out[:height, :] = v
        out[height:, :] = g
        for place, value in enumerate(
            (lane_partial(b * b), lane_partial(b * v), lane_partial(v * v), lane_largest(g))
        ):
            image[64 + place : 65 + place, :] = value

    def tile(slot, carry):
        rb, cb = meta[slot], meta[8 + slot]
        kernel = kern.at[slot]
        q = lane_blocks(qv[pl.ds(cb, 1), :], 8)
        fill_columns(column, pv[block_rows(rb), :])

        def rows_of(step, cprods):
            for u in range(4):
                at = pl.ds(pl.multiple_of(step * 32 + 8 * u, 8), 8)
                ks = [kernel[at, lanes_of(l)] for l in range(WIDE)]
                p = column[at, :]
                prods[at, :] = total([ks[l] * q[l] for l in range(WIDE)])
                cprods = tuple(cprods[l] + ks[l] * p for l in range(WIDE))
            return cprods

        cprods = lax.fori_loop(0, TILE // 32, rows_of, no_sums())
        add_block(rout, 0, rb, lane_sums(prods))
        add_sums(csum, cb, cprods)
        return carry

    lax.fori_loop(0, meta[16], tile, 0)
    pack_into(cout, 0, csum[...])


def form_kernel(
    meta, rows_in, cols_in, pb, qb, pv, qv, kern,
    pw, qw, dots, known,
    column, acc,
):
    both = rows_in[64:72, :] + cols_in[64:72, :]
    bb, bv, vv, sigma = (scalar(both[i : i + 1]) for i in range(4))
    rows, cols = rows_in[:64, :], unpack(cols_in[:64, :])
    inverse = 1.0 / sigma
    lift = UP * inverse
    alpha = bb / (bv * lift)
    known[...] = jnp.zeros_like(known)
    for place, value in enumerate((bb, bv * lift, (vv * lift) * lift, inverse)):
        known[place : place + 1, :] = jnp.broadcast_to(value, (1, LANES))
    found = []
    for given, vectors, image, out, height in ((pb, pv, rows, pw, 64), (qb, qv, cols, qw, 8)):
        b, v, g = given[:height, :], vectors[:height, :], vectors[height:, :]
        second = g * v + image
        first = v * lift
        next_image = (second * lift) * inverse
        residual = b - alpha * first
        turned = first - alpha * next_image
        out[:height, :] = residual
        out[height : 2 * height, :] = turned
        out[2 * height :, :] = first
        found.append(
            (
                lane_partial(residual * residual),
                lane_partial(residual * turned),
                lane_partial(residual * first),
                lane_partial(turned * turned),
                lane_partial(turned * first),
                lane_partial(next_image * turned),
                lane_partial(first * next_image),
                lane_partial((g * inverse) * turned * turned),
            )
        )
    acc[...] = jnp.zeros_like(acc)

    def tile(slot, carry):
        rb, cb = meta[slot], meta[8 + slot]
        kernel = kern.at[slot]
        q = lane_blocks(qw[pl.ds(8 + cb, 1), :] * inverse, 8)
        fill_columns(column, pw[pl.ds(pl.multiple_of(64 + 8 * rb, 8), 8), :])

        def rows_of(step, cprods):
            for u in range(4):
                at = pl.ds(pl.multiple_of(step * 32 + 8 * u, 8), 8)
                p = column[at, :]
                cprods = tuple(cprods[l] + kernel[at, lanes_of(l)] * p for l in range(WIDE))
            return cprods

        cprods = lax.fori_loop(0, TILE // 32, rows_of, no_sums())
        acc[...] = acc[...] + total([cprods[l] * q[l] for l in range(WIDE)])
        return carry

    lax.fori_loop(0, meta[16], tile, 0)
    for place in range(8):
        value = (found[0][place] + found[1][place]) * (1.0 / 16.0)
        if place == 7:
            value = value + 2.0 * jnp.sum(acc[...], axis=0, keepdims=True)
        dots[place : place + 1, :] = value


def grad_kernel(
    meta, dots, known, pb, qb, pw, qw, xs, ys, kern,
    adj_s, adj_t, near, far, x0, x1, x2, x3, x4,
    ap, aq, column, half, row_wy, col_wx, held, sems,
):
    tiles = meta[16]
    start_fetching(kern, held, sems, tiles)
    me_s, me_t = meta[17], meta[18]
    ee, ew, eh, ww, wh, uw, hu, waw = (scalar(dots[i : i + 1, :]) for i in range(8))
    bb, bh, hh, inverse = (known[i : i + 1, 0:1] for i in range(4))
    alpha1 = bb / bh
    beta1 = ee / bb
    dad = ew + 2.0 * beta1 * eh + beta1 * beta1 * bh
    alpha2 = ee / dad
    e_ad = ew + beta1 * eh
    ad_ad = ww + 2.0 * beta1 * wh + beta1 * beta1 * hh
    rr2 = ee - 2.0 * alpha2 * e_ad + alpha2 * alpha2 * ad_ad
    beta2 = rr2 / ee
    form = waw + 2.0 * beta1 * uw + beta1 * beta1 * hu
    r_ar = ew - 2.0 * alpha2 * (ww + beta1 * wh) + alpha2 * alpha2 * form
    d2_ar2 = ew + beta1 * eh - alpha2 * ad_ad
    d3ad3 = r_ar + 2.0 * beta2 * d2_ar2 + beta2 * beta2 * dad
    alpha3 = rr2 / d3ad3
    on_b = (alpha1 + alpha2 * beta1 + alpha3 * beta2 * beta1) * inverse
    on_e = (alpha2 + alpha3 * (1.0 + beta2)) * inverse
    on_w = -(alpha3 * alpha2) * inverse
    on_h = on_w * beta1
    for given, vectors, out, height in ((pb, pw, ap, 64), (qb, qw, aq, 8)):
        e, w, h = (vectors[height * i : height * (i + 1), :] for i in range(3))
        out[...] = on_b * given[:height, :] + on_e * e + on_w * w + on_h * h
    own = ap[block_rows(me_t // 2), :]
    own = jnp.where(me_t % 2 == 1, own[:, 64:], own[:, :64])
    for r in range(8):
        adj_s[:, 64 * r : 64 * (r + 1)] = own[r : r + 1, :]
    row = aq[pl.ds(me_s // 2, 1), :]
    adj_t[...] = jnp.where(me_s % 2 == 1, row[:, PART:], row[:, :PART])
    row_wy[...] = jnp.zeros_like(row_wy)
    col_wx[...] = jnp.zeros_like(col_wx)

    def tile(slot, carry):
        rb, cb = meta[slot], meta[8 + slot]
        fill_columns(column, ap[block_rows(rb), :])
        q = lane_blocks(aq[pl.ds(cb, 1), :], 16)
        kernel = next_tile(kern, held, sems, slot, tiles)

        def rows_of(step, unused):
            for u in range(2):
                at = pl.ds(pl.multiple_of(step * 32 + 16 * u, 16), 16)
                p = column[at, :]
                for l in range(WIDE):
                    half[at, lanes_of(l)] = (kernel[at, lanes_of(l)] * (p + q[l])).astype(BF16)
            return unused

        lax.fori_loop(0, TILE // 32, rows_of, 0)
        row_wy[rb] = row_wy[rb] + lax.dot_general(
            pair_of(ys, cb), half[...], (((1,), (1,)), ((), ())), preferred_element_type=F32
        )
        col_wx[cb] = col_wx[cb] + jnp.dot(
            pair_of(xs, rb), half[...], preferred_element_type=F32
        )
        return carry

    lax.fori_loop(0, tiles, tile, 0)


    def part_of(feat, mixed, ones, block):
        wide = feat[block, :FEATS, :].astype(F32)
        odd = block % 2 == 1
        whole = mixed[block // 2]
        mine = jnp.where(odd, whole[:, PART:], whole[:, :PART])
        return (2.0 / EPS) * (wide * mine[ones : ones + 1] - mine[:FEATS])

    for k in range(8):
        for other, out in enumerate((near, far)):
            out[k] = part_of(xs, row_wy, FEATS, ring_block(me_t, RING[k], other))
    for k in range(4):
        for dx, out in ((0, x0), (1, x1), (-1, x2), (2, None)):
            part = part_of(ys, col_wx, FEATS + 3, quad_block(me_s, QUAD[k], dx))
            if out is None:
                x3[k] = part[:32]
                x4[k] = part[32:]
            else:
                out[k] = part


def finish_kernel(p0, p1, p2, p3, p4, p5, out, turned):
    value = ((p0[...] + p1[...]) + p2[...]) + ((p3[...] + p4[...]) + p5[...])
    value = jnp.concatenate([value, jnp.zeros_like(value)], axis=0)
    out[...] = to_cells(value, turned)[:FEATS]


def swap(value, axis, mask):
    return lax.ppermute(value, axis, [(i, i ^ mask) for i in range(16)])


def along_z(value, step):
    return lax.ppermute(value, "tgt", [(i, (i + 2 * step) % 16) for i in range(16)])


def along_y(value, step):
    return lax.ppermute(value, "src", [(i, (i + 4 * step) % 16) for i in range(16)])


def along_x(value, step):
    return lax.ppermute(value, "src", [(i, i // 4 * 4 + (i + step) % 4) for i in range(16)])


def exchange(value, axis):
    return lax.all_to_all(value, axis, 0, 0)


def summed(value, axis):
    everywhere = jnp.broadcast_to(value[None], (16, *value.shape))
    return jnp.sum(exchange(everywhere, axis), axis=0)


def sum_pieces(row, col):
    for mask in (1, 2, 4, 8):
        row, col = together(row + swap(row, "tgt", mask), col + swap(col, "src", mask))
    return row, col


def together(*values):
    return lax.optimization_barrier(values)


def gather_all(own_s, own_t):
    after, before, across = along_z(own_s, 1), along_z(own_s, -1), along_z(own_s, 4)
    up, down, over = along_y(own_t, 1), along_y(own_t, -1), along_y(own_t, 2)
    after, before, across, up, down, over = together(after, before, across, up, down, over)
    stack = jnp.stack([own_t, down, up, over])
    low, high = jnp.stack([own_s, after]), jnp.stack([own_s, before])
    right, left = along_x(stack, 1), along_x(stack, -1)
    low, high = along_z(low, 2), along_z(high, -2)
    right, left, low, high = together(right, left, low, high)
    near = jnp.concatenate([jnp.stack([own_s, after, before, across]), low, high])
    far = swap(near, "tgt", 1)
    return (near, far), (stack, right, left, along_x(right[:2], 1), along_x(left[2:], -1))


def scatter_all(near, far, own, next_up, next_down, top, bottom):
    half = FEATS // 2
    other = swap(far, "tgt", 1)
    top, bottom = along_x(top, 1), along_x(bottom, -1)
    other, top, bottom = together(other, top, bottom)
    near = near + other
    up = jnp.concatenate([next_up[:, :half] + top, next_up[:, half:]], axis=1)
    down = jnp.concatenate([next_down[:, :half], next_down[:, half:] + bottom], axis=1)
    up, down = along_x(up, 1), along_x(down, -1)
    after, before = along_z(near[6:8], 2), along_z(near[4:6], -2)
    up, down, after, before = together(up, down, after, before)
    part = (own + up) + down
    last = (
        along_z(near[2] + after[1], 1),
        along_z(near[1] + before[1], -1),
        along_z(near[3], 4),
        along_y(part[1], 1),
        along_y(part[2], -1),
        along_y(part[3], 2),
    )
    last = together(*last)
    grad_src = pl.pallas_call(
        finish_kernel,
        out_shape=shape((FEATS, PART)),
        in_specs=[VMEM] * 6,
        out_specs=VMEM,
        scratch_shapes=[pltpu.VMEM((PART, LANES), F32)],
        compiler_params=params(24),
    )(near[0], after[0], before[0], *last[:3])
    grad_tgt = (part[0] + last[3]) + (last[4] + last[5])
    return grad_src, grad_tgt


def shards(
    src_feat, tgt_feat, row_pot, col_pot, src_mass, tgt_mass, rhs_src, rhs_tgt,
    tile_rows, tile_cols, tile_count,
):
    me_s, me_t = lax.axis_index("src"), lax.axis_index("tgt")
    meta = jnp.concatenate(
        [
            tile_rows.reshape(8),
            tile_cols.reshape(8),
            tile_count.reshape(1),
            me_s.reshape(1).astype(jnp.int32),
            me_t.reshape(1).astype(jnp.int32),
        ]
    )
    line = lambda v: v.reshape(1, PART)
    pay = (FEATS + 16, PART)
    pay_s, pay_t = pl.pallas_call(
        payload_kernel,
        out_shape=[shape(pay, BF16), shape(pay, BF16)],
        in_specs=[HBM] * 8,
        out_specs=[VMEM] * 2,
        scratch_shapes=[pltpu.VMEM((FEATS, PART), BF16)] * 2
        + [pltpu.VMEM((1, PART), F32)] * 6
        + [pltpu.VMEM((PART, LANES), F32), pltpu.SemaphoreType.DMA((8,))],
        compiler_params=params(24),
    )(
        *(
            pltpu.with_memory_space_constraint(value, pltpu.HBM)
            for value in (
                src_feat, tgt_feat, line(row_pot), line(col_pot), line(src_mass), line(tgt_mass),
                line(rhs_src), line(rhs_tgt),
            )
        )
    )
    s_parts, t_parts = gather_all(pay_s, pay_t)

    feats = shape((16, *pay), BF16)
    packed = shape((2 * 64, LANES))
    natural = shape((2 * BLOCKS, TILE))
    column = pltpu.VMEM((TILE, LANES), F32)
    kern, stored, xs, ys, pb, qb, rsum, csum = pl.pallas_call(
        build_kernel,
        out_shape=[
            pltpu.VMEM((SLOTS, TILE, TILE), F32), shape((SLOTS, TILE, TILE)),
            feats, feats, packed, natural, packed, packed,
        ],
        in_specs=[SMEM] + [ANY] * 7,
        out_specs=[VMEM, ANY] + [VMEM] * 6,
        scratch_shapes=[
            pltpu.VMEM((TILE, LANES), BF16),
            pltpu.VMEM((LANES, TILE), BF16),
            column,
            column,
            column,
            pltpu.VMEM((2 * BLOCKS, TILE), F32),
            pltpu.VMEM((4, 16, PART), F32),
            pltpu.SemaphoreType.DMA((32,)),
            pltpu.SemaphoreType.DMA((SLOTS,)),
        ],
        compiler_params=params(24),
    )(meta, *s_parts, *t_parts)
    kern = pltpu.with_memory_space_constraint(kern, pltpu.VMEM)

    rsum, csum = sum_pieces(rsum, csum)
    pv, qv, rimg, cimg = pl.pallas_call(
        apply_kernel,
        out_shape=[packed, natural, packed, packed],
        in_specs=[SMEM] + [VMEM] * 5,
        out_specs=[VMEM] * 4,
        scratch_shapes=[column, column, pltpu.VMEM((BLOCKS, TILE), F32)],
        compiler_params=params(24),
    )(meta, rsum, csum, pb, qb, kern)

    rimg, cimg = sum_pieces(rimg, cimg)
    pw, qw, dots, known = pl.pallas_call(
        form_kernel,
        out_shape=[shape((3 * 64, LANES)), shape((3 * BLOCKS, TILE))] + [shape((8, LANES))] * 2,
        in_specs=[SMEM] + [VMEM] * 7,
        out_specs=[VMEM] * 4,
        scratch_shapes=[column, pltpu.VMEM((8, LANES), F32)],
        compiler_params=params(24),
    )(meta, rimg, cimg, pb, qb, pv, qv, kern)

    dots = summed(summed(dots, "tgt"), "src")
    outs = pl.pallas_call(
        grad_kernel,
        out_shape=[shape((1, PART))] * 2
        + [shape((8, FEATS, PART))] * 2
        + [shape((4, FEATS, PART))] * 3
        + [shape((4, FEATS // 2, PART))] * 2,
        in_specs=[SMEM] + [VMEM] * 8 + [ANY],
        out_specs=[VMEM] * 9,
        scratch_shapes=[
            pltpu.VMEM((64, LANES), F32),
            pltpu.VMEM((BLOCKS, TILE), F32),
            column,
            pltpu.VMEM((TILE, TILE), BF16),
            pltpu.VMEM((BLOCKS, FEATS + 16, TILE), F32),
            pltpu.VMEM((BLOCKS, FEATS + 16, TILE), F32),
            pltpu.VMEM((3, TILE, TILE), F32),
            pltpu.SemaphoreType.DMA((3,)),
        ],
        compiler_params=params(40),
    )(meta, dots, known, pb, qb, pw, qw, xs, ys, stored)
    adj_s, adj_t = outs[:2]
    grad_src, grad_tgt = scatter_all(*outs[2:])
    return adj_s.reshape(PART), adj_t.reshape(PART), grad_src, grad_tgt


def solution(mesh):
    in_specs = (
        P(None, ("src", "tgt")),
        P(None, ("tgt", "src")),
        P(("src", "tgt")),
        P(("tgt", "src")),
        P(("src", "tgt")),
        P(("tgt", "src")),
        P(("src", "tgt")),
        P(("tgt", "src")),
        P("src", "tgt", None),
        P("src", "tgt", None),
        P("src", "tgt"),
    )
    out_specs = (
        P(("src", "tgt")),
        P(("tgt", "src")),
        P(None, ("src", "tgt")),
        P(None, ("tgt", "src")),
    )
    return jax.shard_map(shards, mesh=mesh, in_specs=in_specs, out_specs=out_specs, check_vma=False)
```

```python
import math

import jax
import jax.numpy as jnp
from jax import lax
from jax.experimental import pallas as pl
from jax.experimental.pallas import tpu as pltpu
from jax.sharding import PartitionSpec as P

TILE = 1024
FEATS = 64
LANES = 128
BLOCKS = 8
SLOTS = 8
PART = 512
EPS = 0.05
RHO = 1.0
SCALE = 2.0 * math.log2(math.e) / EPS
DOWN = 2.0**-40
UP = 2.0**40
F32 = jnp.float32
BF16 = jnp.bfloat16
VMEM = pl.BlockSpec(memory_space=pltpu.VMEM)
SMEM = pl.BlockSpec(memory_space=pltpu.SMEM)
ANY = pl.BlockSpec(memory_space=pl.ANY)
HBM = pl.BlockSpec(memory_space=pltpu.HBM)
RING = (0, -1, 1, 4, -2, -3, 2, 3)
QUAD = (0, 1, -1, 2)


def params(mib):
    return pltpu.CompilerParams(vmem_limit_bytes=mib * 2**20)


def shape(dims, dtype=F32):
    return jax.ShapeDtypeStruct(dims, dtype)


def split3(value):
    high = value.astype(BF16).astype(F32)
    rest = value - high
    middle = rest.astype(BF16).astype(F32)
    low = (rest - middle).astype(BF16).astype(F32)
    return high, middle, low


def to_positions(value, turned):
    turned[...] = value.T
    groups = [turned[pl.ds(g, 8, stride=64), :] for g in range(64)]
    return jnp.concatenate(groups, axis=0).T


def to_cells(value, turned):
    turned[...] = value.T
    groups = [turned[pl.ds(r, 64, stride=8), :] for r in range(8)]
    return jnp.concatenate(groups, axis=0).T


def payload_kernel(*refs):
    sources, (out_s, out_t), held = refs[:8], refs[8:10], refs[10:18]
    turned, sems = refs[18:]
    copies = [
        pltpu.make_async_copy(source, place, sems.at[i])
        for i, (source, place) in enumerate(zip(sources, held))
    ]
    for copy in copies:
        copy.start()
    for copy in copies:
        copy.wait()
    sf, tf, rp, cp, sm, tm, rs, rt = held
    for feat, pot, mass, rhs, out, first in (
        (sf, rp, sm, rs, out_s, True),
        (tf, cp, tm, rt, out_t, False),
    ):
        wide = feat[...].astype(F32)
        potential = pot[...]
        term = (potential - jnp.sum(wide * wide, axis=0, keepdims=True)) * 0.5
        damp = EPS / RHO * mass[...] * jnp.exp(-potential / RHO)
        ones = jnp.ones((3, PART), F32)
        pieces = list(split3(term))
        rows = pieces + [ones] if first else [ones] + pieces
        rows += list(split3(rhs[...])) + list(split3(damp))
        rows.append(jnp.zeros((4, PART), F32))
        tail = jnp.concatenate(rows, axis=0)
        if first:
            whole = jnp.concatenate([wide, tail, jnp.zeros((48, PART), F32)], axis=0)
            whole = to_positions(whole, turned)
            out[0:FEATS, :] = whole[:FEATS].astype(BF16)
            keep = lax.broadcasted_iota(jnp.int32, (16, PART), 0) < 6
            tail = jnp.where(keep, whole[FEATS : FEATS + 16], tail)
        else:
            out[0:FEATS, :] = feat[...]
        out[FEATS : FEATS + 16, :] = tail.astype(BF16)


def three(rows, start):
    return rows[start : start + 1] + (rows[start + 1 : start + 2] + rows[start + 2 : start + 3])


def lane_blocks(row, height):
    return [
        jnp.broadcast_to(row[:, LANES * l : LANES * (l + 1)], (height, LANES))
        for l in range(TILE // LANES)
    ]


def total(values):
    while len(values) > 1:
        joined = [values[i] + values[i + 1] for i in range(0, len(values) - 1, 2)]
        values = joined + list(values[len(values) // 2 * 2 :])
    return values[0]


def block_rows(block):
    return pl.ds(pl.multiple_of(8 * block, 8), 8)


def fill_columns(column, packed):
    for g in range(LANES):
        column[8 * g : 8 * g + 8, :] = jnp.broadcast_to(packed[:, g : g + 1], (8, LANES))


def lane_sums(partial):
    lane = lax.broadcasted_iota(jnp.int32, (8, LANES), 1)
    result = jnp.zeros((8, LANES), F32)
    for g in range(LANES):
        group = jnp.sum(partial[8 * g : 8 * g + 8, :], axis=1, keepdims=True)
        result = jnp.where(lane == g, group, result)
    return result


def add_block(ref, first, block, value):
    rows = pl.ds(pl.multiple_of(first + 8 * block, 8), 8)
    ref[rows, :] = ref[rows, :] + value


def add_sums(ref, index, sums):
    row = jnp.sum(jnp.concatenate(sums, axis=1), axis=0, keepdims=True)
    ref[pl.ds(index, 1), :] = ref[pl.ds(index, 1), :] + row


def unpack(value):
    return jnp.concatenate(
        [value[BLOCKS * l : BLOCKS * (l + 1)] for l in range(TILE // LANES)], axis=1
    )


def pack_into(out, first, value):
    for l in range(TILE // LANES):
        out[first + BLOCKS * l : first + BLOCKS * (l + 1), :] = value[:, LANES * l : LANES * (l + 1)]


def pair_of(ref, block):
    return jnp.concatenate([ref[2 * block], ref[2 * block + 1]], axis=1)


def ring_block(me, dz, other):
    place = lax.rem(me // 2 + (dz + 8), 8)
    core = lax.rem(me, 2)
    return 2 * place + (1 - core if other else core)


def quad_block(me, dy, dx):
    return 4 * lax.rem(me // 4 + (dy + 4), 4) + lax.rem(lax.rem(me, 4) + (dx + 4), 4)


def fetch(kern, held, sems, slot):
    place = lax.rem(slot, 3)
    return pltpu.make_async_copy(kern.at[slot], held.at[place], sems.at[place])


def start_fetching(kern, held, sems, count):
    fetch(kern, held, sems, 0).start()

    @pl.when(count > 1)
    def _():
        fetch(kern, held, sems, 1).start()


def next_tile(kern, held, sems, slot, count):
    @pl.when(slot + 2 < count)
    def _():
        fetch(kern, held, sems, slot + 2).start()

    fetch(kern, held, sems, slot).wait()
    return held.at[lax.rem(slot, 3)]


WIDE = TILE // LANES
CHUNK = 256


def no_sums():
    return tuple(jnp.zeros((8, LANES), F32) for l in range(WIDE))


def lanes_of(l):
    return slice(LANES * l, LANES * (l + 1))


def part_copies(me_s, me_t, pieces, xs, ys, sems):
    s0, s1, t0, t1, t2, t3, t4 = pieces
    copies = []
    for k in range(8):
        for other, stack in enumerate((s0, s1)):
            copies.append((stack.at[k], xs.at[ring_block(me_t, RING[k], other)]))
    for k in range(4):
        far = (t3.at[k] if k < 2 else t4.at[k - 2])
        for dx, piece in ((0, t0.at[k]), (1, t2.at[k]), (-1, t1.at[k]), (2, far)):
            copies.append((piece, ys.at[quad_block(me_s, QUAD[k], dx)]))
    return [
        pltpu.make_async_copy(source, place, sems.at[i])
        for i, (source, place) in enumerate(copies)
    ]


def build_kernel(
    meta, s0, s1, t0, t1, t2, t3, t4,
    kern, pb, qb, rout, cout,
    xs, ys, left, right, sums, prods, column, csum, parts, ahead, behind, sems,
):
    me_s, me_t = meta[17], meta[18]
    pieces = (s0, s1, t0, t1, t2, t3, t4)
    copies = part_copies(me_s, me_t, pieces, xs, ys, sems)
    for copy in copies:
        copy.start()
    rout[...] = jnp.zeros_like(rout)
    csum[...] = jnp.zeros_like(csum)
    for copy in copies:
        copy.wait()
    for part in range(16):
        for place, ref in ((0, xs), (2, ys)):
            rows = ref[part, FEATS : FEATS + 16, :].astype(F32)
            at = part // 2 + 8 * (part % 2)
            parts[place, at : at + 1, :] = three(rows, 6)
            parts[place + 1, at : at + 1, :] = three(rows, 9)
    for place in range(2):
        even, odd = parts[place, 0:8, :], parts[place, 8:16, :]
        for r in range(8):
            cells = slice(64 * r, 64 * (r + 1))
            pb[pl.ds(64 * place + r, 8, stride=8), :] = jnp.concatenate(
                [even[:, cells], odd[:, cells]], axis=1
            )
        for side in range(2):
            qb[8 * place : 8 * place + 8, PART * side : PART * (side + 1)] = parts[
                2 + place, 8 * side : 8 * side + 8, :
            ]

    keep = lax.broadcasted_iota(jnp.int32, (16, TILE), 0) < 6
    blank = jnp.zeros((48, TILE), BF16)

    def with_terms(payload):
        terms = jnp.where(keep, payload[FEATS:].astype(F32), 0.0).astype(BF16)
        return jnp.concatenate([payload[:FEATS], terms, blank], axis=0)

    def tile(slot, carry):
        rb, cb = meta[slot], meta[8 + slot]
        kernel = kern.at[slot]
        left[...] = with_terms(pair_of(xs, rb)).T
        right[...] = with_terms(pair_of(ys, cb))
        q = lane_blocks(qb[pl.ds(cb, 1), :], 8)
        fill_columns(column, pb[block_rows(rb), :])

        products = (ahead, behind)

        def product(chunk):
            products[chunk % 2][...] = jnp.dot(
                left[CHUNK * chunk : CHUNK * (chunk + 1), :],
                right[...],
                preferred_element_type=F32,
            )

        csums, cprods = no_sums(), no_sums()
        product(0)
        for chunk in range(TILE // CHUNK):
            if CHUNK * (chunk + 1) < TILE:
                product(chunk + 1)
            for u in range(CHUNK // 8):
                near = slice(8 * u, 8 * u + 8)
                at = slice(CHUNK * chunk + 8 * u, CHUNK * chunk + 8 * u + 8)
                ks = [
                    jnp.exp2(products[chunk % 2][near, lanes_of(l)] * SCALE) for l in range(WIDE)
                ]
                for l in range(WIDE):
                    kernel[at, lanes_of(l)] = ks[l]
                p = column[at, :]
                sums[at, :] = total(ks)
                prods[at, :] = total([ks[l] * q[l] for l in range(WIDE)])
                csums = tuple(csums[l] + ks[l] for l in range(WIDE))
                cprods = tuple(cprods[l] + ks[l] * p for l in range(WIDE))
        add_block(rout, 0, rb, lane_sums(sums))
        add_block(rout, 64, rb, lane_sums(prods))
        add_sums(csum, cb, csums)
        add_sums(csum, 8 + cb, cprods)
        return carry

    lax.fori_loop(0, meta[16], tile, 0)
    pack_into(cout, 0, csum[:8, :])
    pack_into(cout, 64, csum[8:, :])


def folded(value, join):
    if value.shape[1] == LANES:
        return value
    result = value[:, :LANES]
    for l in range(1, WIDE):
        result = join(result, value[:, lanes_of(l)])
    return result


def lane_partial(value):
    return folded(jnp.sum(value, axis=0, keepdims=True), jnp.add)


def lane_largest(value):
    return folded(jnp.max(value, axis=0, keepdims=True), jnp.maximum)


def scalar(row):
    return jnp.sum(row, axis=1, keepdims=True)


def apply_kernel(
    meta, rows_in, cols_in, pb, qb, kern,
    pv, qv, rout, cout, stored,
    prods, column, csum, out_sems,
):
    def store(slot):
        return pltpu.make_async_copy(kern.at[slot], stored.at[slot], out_sems.at[slot])

    def begin(slot, carry):
        store(slot).start()
        return carry

    def finish(slot, carry):
        store(slot).wait()
        return carry

    lax.fori_loop(0, meta[16], begin, 0)
    rows = (rows_in[:64, :], rows_in[64:, :])
    cols = (unpack(cols_in[:64, :]), unpack(cols_in[64:, :]))
    rout[...] = jnp.zeros_like(rout)
    csum[...] = jnp.zeros_like(csum)
    cout[64:128, :] = jnp.zeros((64, LANES), F32)
    for (marg, prod), given, out, image, height in (
        (rows, pb, pv, cout, 64),
        (cols, qb, qv, rout, 8),
    ):
        b, d = given[:height, :], given[height:, :]
        g = marg + d
        v = g * (b * DOWN) + prod * DOWN
        out[:height, :] = v
        out[height:, :] = g
        for place, value in enumerate(
            (lane_partial(b * b), lane_partial(b * v), lane_partial(v * v), lane_largest(g))
        ):
            image[64 + place : 65 + place, :] = value

    def tile(slot, carry):
        rb, cb = meta[slot], meta[8 + slot]
        kernel = kern.at[slot]
        q = lane_blocks(qv[pl.ds(cb, 1), :], 8)
        fill_columns(column, pv[block_rows(rb), :])

        def rows_of(step, cprods):
            for u in range(16):
                at = pl.ds(pl.multiple_of(step * 128 + 8 * u, 8), 8)
                ks = [kernel[at, lanes_of(l)] for l in range(WIDE)]
                p = column[at, :]
                prods[at, :] = total([ks[l] * q[l] for l in range(WIDE)])
                cprods = tuple(cprods[l] + ks[l] * p for l in range(WIDE))
            return cprods

        cprods = lax.fori_loop(0, TILE // 128, rows_of, no_sums())
        add_block(rout, 0, rb, lane_sums(prods))
        add_sums(csum, cb, cprods)
        return carry

    lax.fori_loop(0, meta[16], tile, 0)
    pack_into(cout, 0, csum[...])
    lax.fori_loop(0, meta[16], finish, 0)


def form_kernel(
    meta, rows_in, cols_in, pb, qb, pv, qv, kern,
    pw, qw, dots, known,
    column, acc,
):
    both = rows_in[64:72, :] + cols_in[64:72, :]
    bb, bv, vv, sigma = (scalar(both[i : i + 1]) for i in range(4))
    rows, cols = rows_in[:64, :], unpack(cols_in[:64, :])
    inverse = 1.0 / sigma
    lift = UP * inverse
    alpha = bb / (bv * lift)
    known[...] = jnp.zeros_like(known)
    for place, value in enumerate((bb, bv * lift, (vv * lift) * lift, inverse)):
        known[place : place + 1, :] = jnp.broadcast_to(value, (1, LANES))
    found = []
    for given, vectors, image, out, height in ((pb, pv, rows, pw, 64), (qb, qv, cols, qw, 8)):
        b, v, g = given[:height, :], vectors[:height, :], vectors[height:, :]
        second = g * v + image
        first = v * lift
        next_image = (second * lift) * inverse
        residual = b - alpha * first
        turned = first - alpha * next_image
        out[:height, :] = residual
        out[height : 2 * height, :] = turned
        out[2 * height :, :] = first
        found.append(
            (
                lane_partial(residual * residual),
                lane_partial(residual * turned),
                lane_partial(residual * first),
                lane_partial(turned * turned),
                lane_partial(turned * first),
                lane_partial(next_image * turned),
                lane_partial(first * next_image),
                lane_partial((g * inverse) * turned * turned),
                *(lane_largest(jnp.abs(vector)) for vector in (b, residual, turned, first)),
                lane_largest(g),
            )
        )
    acc[...] = jnp.zeros_like(acc)

    def tile(slot, carry):
        rb, cb = meta[slot], meta[8 + slot]
        kernel = kern.at[slot]
        q = lane_blocks(qw[pl.ds(8 + cb, 1), :] * inverse, 8)
        fill_columns(column, pw[pl.ds(pl.multiple_of(64 + 8 * rb, 8), 8), :])

        def rows_of(step, cprods):
            for u in range(16):
                at = pl.ds(pl.multiple_of(step * 128 + 8 * u, 8), 8)
                p = column[at, :]
                cprods = tuple(cprods[l] + kernel[at, lanes_of(l)] * p for l in range(WIDE))
            return cprods

        cprods = lax.fori_loop(0, TILE // 128, rows_of, no_sums())
        acc[...] = acc[...] + total([cprods[l] * q[l] for l in range(WIDE)])
        return carry

    lax.fori_loop(0, meta[16], tile, 0)
    for place in range(8):
        value = (found[0][place] + found[1][place]) * (1.0 / 16.0)
        if place == 7:
            value = value + 2.0 * jnp.sum(acc[...], axis=0, keepdims=True)
        dots[place : place + 1, :] = value
    for place in range(8, 13):
        dots[place : place + 1, :] = jnp.maximum(found[0][place], found[1][place])
    dots[13:16, :] = jnp.zeros((3, LANES), F32)


def grad_kernel(
    meta, dots, known_in, pb_in, qb_in, pw_in, qw_in, s0, s1, t0, t1, t2, t3, t4, kern,
    adj_s, adj_t, level, near, far, x0, x1, x2, x3, x4,
    known, pb, qb, pw, qw, xs, ys,
    ap, aq, column, ahead, behind, x_block, y_block, row_wy, col_wx, held, sems, vector_sems,
    part_sems,
):
    tiles = meta[16]
    me_s, me_t = meta[17], meta[18]
    vectors_in = ((known_in, known), (pb_in, pb), (qb_in, qb), (pw_in, pw), (qw_in, qw))
    copies = [
        pltpu.make_async_copy(source, place, vector_sems.at[i])
        for i, (source, place) in enumerate(vectors_in)
    ]
    for copy in copies:
        copy.start()
    start_fetching(kern, held, sems, tiles)
    part_moves = part_copies(me_s, me_t, (s0, s1, t0, t1, t2, t3, t4), xs, ys, part_sems)
    for copy in part_moves:
        copy.start()
    row_wy[...] = jnp.zeros_like(row_wy)
    col_wx[...] = jnp.zeros_like(col_wx)
    for copy in copies:
        copy.wait()
    ee, ew, eh, ww, wh, uw, hu, waw = (scalar(dots[i : i + 1, :]) for i in range(8))
    bb, bh, hh, inverse = (known[i : i + 1, 0:1] for i in range(4))
    alpha1 = bb / bh
    beta1 = ee / bb
    dad = ew + 2.0 * beta1 * eh + beta1 * beta1 * bh
    alpha2 = ee / dad
    e_ad = ew + beta1 * eh
    ad_ad = ww + 2.0 * beta1 * wh + beta1 * beta1 * hh
    rr2 = ee - 2.0 * alpha2 * e_ad + alpha2 * alpha2 * ad_ad
    beta2 = rr2 / ee
    form = waw + 2.0 * beta1 * uw + beta1 * beta1 * hu
    r_ar = ew - 2.0 * alpha2 * (ww + beta1 * wh) + alpha2 * alpha2 * form
    d2_ar2 = ew + beta1 * eh - alpha2 * ad_ad
    d3ad3 = r_ar + 2.0 * beta2 * d2_ar2 + beta2 * beta2 * dad
    alpha3 = rr2 / d3ad3
    on_b = (alpha1 + alpha2 * beta1 + alpha3 * beta2 * beta1) * inverse
    on_e = (alpha2 + alpha3 * (1.0 + beta2)) * inverse
    on_w = -(alpha3 * alpha2) * inverse
    on_h = on_w * beta1
    for given, vectors, out, height in ((pb, pw, ap, 64), (qb, qw, aq, 8)):
        e, w, h = (vectors[height * i : height * (i + 1), :] for i in range(3))
        out[...] = on_b * given[:height, :] + on_e * e + on_w * w + on_h * h
    own = ap[block_rows(me_t // 2), :]
    own = jnp.where(me_t % 2 == 1, own[:, 64:], own[:, :64])
    for r in range(8):
        adj_s[:, 64 * r : 64 * (r + 1)] = own[r : r + 1, :]
    row = aq[pl.ds(me_s // 2, 1), :]
    adj_t[...] = jnp.where(me_s % 2 == 1, row[:, PART:], row[:, :PART])


    largest = [jnp.max(dots[i : i + 1, :], axis=1, keepdims=True) for i in range(8, 13)]
    reach = total(
        [jnp.abs(c) * m for c, m in zip((on_b, on_e, on_w, on_h), largest[:4])]
    )
    bound = jnp.maximum((60.0 * 1.05) * (reach * largest[4]), 1e-30)
    scale = 60000.0 / bound
    level[...] = jnp.broadcast_to(1.0 / scale, (8, LANES))

    def tile(slot, carry):
        rb, cb = meta[slot], meta[8 + slot]
        fill_columns(column, ap[block_rows(rb), :])
        q = lane_blocks(aq[pl.ds(cb, 1), :], 16)
        kernel = next_tile(kern, held, sems, slot, tiles)


        @pl.when(slot == 0)
        def _():
            for copy in part_moves:
                copy.wait()

        x_block[...] = pair_of(xs, rb)
        y_block[...] = pair_of(ys, cb)
        halves = (ahead, behind)

        def weights(chunk):
            for u in range(CHUNK // 16):
                at = slice(CHUNK * chunk + 16 * u, CHUNK * chunk + 16 * u + 16)
                p = column[at, :]
                for l in range(WIDE):
                    halves[chunk % 2][16 * u : 16 * u + 16, lanes_of(l)] = (
                        kernel[at, lanes_of(l)] * (p + q[l])
                    ).astype(BF16)

        weights(0)
        for chunk in range(TILE // CHUNK):
            cells = slice(CHUNK * chunk, CHUNK * (chunk + 1))
            if CHUNK * (chunk + 1) < TILE:
                weights(chunk + 1)
            half = halves[chunk % 2][...]
            row_wy[rb, :, cells] = row_wy[rb, :, cells] + lax.dot_general(
                y_block[...], half, (((1,), (1,)), ((), ())), preferred_element_type=F32
            )
            col_wx[cb] = col_wx[cb] + jnp.dot(
                x_block[:, cells], half, preferred_element_type=F32
            )
        return carry

    lax.fori_loop(0, tiles, tile, 0)


    def part_of(feat, mixed, ones, block):
        wide = feat[block, :FEATS, :].astype(F32)
        odd = block % 2 == 1
        whole = mixed[block // 2]
        mine = jnp.where(odd, whole[:, PART:], whole[:, :PART])
        return (wide * mine[ones : ones + 1] - mine[:FEATS]) * (scale * (2.0 / EPS))

    for k in range(8):
        for other, out in enumerate((near, far)):
            out[k] = part_of(xs, row_wy, FEATS, ring_block(me_t, RING[k], other))
    for k in range(4):
        for dx, out in ((0, x0), (1, x1), (-1, x2), (2, None)):
            part = part_of(ys, col_wx, FEATS + 3, quad_block(me_s, QUAD[k], dx))
            if out is None:
                x3[k] = part[:32]
                x4[k] = part[32:]
            else:
                out[k] = part


def finish_kernel(value, level, out, turned):
    whole = jnp.concatenate([value[...], jnp.zeros((FEATS, PART), F32)], axis=0)
    out[...] = to_cells(whole, turned)[:FEATS] * level[0:1, 0:1]


def swap(value, axis, mask):
    return lax.ppermute(value, axis, [(i, i ^ mask) for i in range(16)])


def along_z(value, step):
    return lax.ppermute(value, "tgt", [(i, (i + 2 * step) % 16) for i in range(16)])


def along_y(value, step):
    return lax.ppermute(value, "src", [(i, (i + 4 * step) % 16) for i in range(16)])


def along_x(value, step):
    return lax.ppermute(value, "src", [(i, i // 4 * 4 + (i + step) % 4) for i in range(16)])


def exchange(value, axis):
    return lax.all_to_all(value, axis, 0, 0)


def summed(value, axis):
    everywhere = jnp.broadcast_to(value[None], (16, *value.shape))
    found = exchange(everywhere, axis)
    return jnp.concatenate([jnp.sum(found[:, :8], axis=0), jnp.max(found[:, 8:], axis=0)])


def sum_pieces(row, col):
    for masks in ((4, 8, 12), (1, 2, 3)):
        rows = [row] + [swap(row, "tgt", mask) for mask in masks]
        cols = [col] + [swap(col, "src", mask) for mask in masks]
        both = together(*rows, *cols)
        row = (both[0] + both[1]) + (both[2] + both[3])
        col = (both[4] + both[5]) + (both[6] + both[7])
    return row, col


def together(*values):
    return lax.optimization_barrier(values)


def gather_all(own_s, own_t):
    after, before, across = along_z(own_s, 1), along_z(own_s, -1), along_z(own_s, 4)
    up, down, over = along_y(own_t, 1), along_y(own_t, -1), along_y(own_t, 2)
    after, before, across, up, down, over = together(after, before, across, up, down, over)
    stack = jnp.stack([own_t, down, up, over])
    low, high = jnp.stack([own_s, after]), jnp.stack([own_s, before])
    right, left = along_x(stack, 1), along_x(stack, -1)
    low, high = along_z(low, 2), along_z(high, -2)
    right, left, low, high = together(right, left, low, high)
    near = jnp.concatenate([jnp.stack([own_s, after, before, across]), low, high])
    far = swap(near, "tgt", 1)
    return (near, far), (stack, right, left, along_x(right[:2], 1), along_x(left[2:], -1))


def narrow(value):
    return value.astype(jnp.float16)


def widened(values):
    return [value.astype(F32) for value in values]


def scatter_all(level, near, far, own, next_up, next_down, top, bottom):
    half = FEATS // 2
    other = swap(far, "tgt", 1)
    top, bottom = along_x(narrow(top), 1), along_x(narrow(bottom), -1)
    other, top, bottom = together(other, top, bottom)
    near = near + other
    top, bottom = widened((top, bottom))
    up = jnp.concatenate([next_up[:, :half] + top, next_up[:, half:]], axis=1)
    down = jnp.concatenate([next_down[:, :half], next_down[:, half:] + bottom], axis=1)
    up, down = along_x(narrow(up), 1), along_x(narrow(down), -1)
    after, before = along_z(narrow(near[6:8]), 2), along_z(narrow(near[4:6]), -2)
    up, down, after, before = widened(together(up, down, after, before))
    part = (own + up) + down
    last = (
        along_z(narrow(near[2] + after[1]), 1),
        along_z(narrow(near[1] + before[1]), -1),
        along_z(narrow(near[3]), 4),
        along_y(narrow(part[1]), 1),
        along_y(narrow(part[2]), -1),
        along_y(narrow(part[3]), 2),
    )
    last = widened(together(*last))
    grad_src = ((near[0] + after[0]) + before[0]) + ((last[0] + last[1]) + last[2])
    grad_src = pl.pallas_call(
        finish_kernel,
        out_shape=shape((FEATS, PART)),
        in_specs=[VMEM] * 2,
        out_specs=VMEM,
        scratch_shapes=[pltpu.VMEM((PART, LANES), F32)],
        compiler_params=params(24),
    )(grad_src, level)
    grad_tgt = ((part[0] + last[3]) + (last[4] + last[5])) * level[0, 0]
    return grad_src, grad_tgt


def shards(
    src_feat, tgt_feat, row_pot, col_pot, src_mass, tgt_mass, rhs_src, rhs_tgt,
    tile_rows, tile_cols, tile_count,
):
    me_s, me_t = lax.axis_index("src"), lax.axis_index("tgt")
    meta = jnp.concatenate(
        [
            tile_rows.reshape(8),
            tile_cols.reshape(8),
            tile_count.reshape(1),
            me_s.reshape(1).astype(jnp.int32),
            me_t.reshape(1).astype(jnp.int32),
        ]
    )
    line = lambda v: v.reshape(1, PART)
    pay = (FEATS + 16, PART)
    pay_s, pay_t = pl.pallas_call(
        payload_kernel,
        out_shape=[shape(pay, BF16), shape(pay, BF16)],
        in_specs=[HBM] * 8,
        out_specs=[VMEM] * 2,
        scratch_shapes=[pltpu.VMEM((FEATS, PART), BF16)] * 2
        + [pltpu.VMEM((1, PART), F32)] * 6
        + [pltpu.VMEM((PART, LANES), F32), pltpu.SemaphoreType.DMA((8,))],
        compiler_params=params(24),
    )(
        *(
            pltpu.with_memory_space_constraint(value, pltpu.HBM)
            for value in (
                src_feat, tgt_feat, line(row_pot), line(col_pot), line(src_mass), line(tgt_mass),
                line(rhs_src), line(rhs_tgt),
            )
        )
    )
    s_parts, t_parts = gather_all(pay_s, pay_t)

    feats = pltpu.VMEM((16, *pay), BF16)
    packed = shape((2 * 64, LANES))
    natural = shape((2 * BLOCKS, TILE))
    column = pltpu.VMEM((TILE, LANES), F32)
    kern, pb, qb, rsum, csum = pl.pallas_call(
        build_kernel,
        out_shape=[
            pltpu.VMEM((SLOTS, TILE, TILE), F32),
            packed, natural, packed, packed,
        ],
        in_specs=[SMEM] + [ANY] * 7,
        out_specs=[VMEM] * 5,
        scratch_shapes=[
            feats,
            feats,
            pltpu.VMEM((TILE, LANES), BF16),
            pltpu.VMEM((LANES, TILE), BF16),
            column,
            column,
            column,
            pltpu.VMEM((2 * BLOCKS, TILE), F32),
            pltpu.VMEM((4, 16, PART), F32),
            pltpu.VMEM((CHUNK, TILE), F32),
            pltpu.VMEM((CHUNK, TILE), F32),
            pltpu.SemaphoreType.DMA((32,)),
        ],
        compiler_params=params(24),
    )(meta, *s_parts, *t_parts)
    kern = pltpu.with_memory_space_constraint(kern, pltpu.VMEM)

    rsum, csum = sum_pieces(rsum, csum)
    pv, qv, rimg, cimg, stored = pl.pallas_call(
        apply_kernel,
        out_shape=[packed, natural, packed, packed, shape((SLOTS, TILE, TILE))],
        in_specs=[SMEM] + [VMEM] * 5,
        out_specs=[VMEM] * 4 + [ANY],
        scratch_shapes=[
            column, column, pltpu.VMEM((BLOCKS, TILE), F32), pltpu.SemaphoreType.DMA((SLOTS,)),
        ],
        compiler_params=params(24),
    )(meta, rsum, csum, pb, qb, kern)

    rimg, cimg = sum_pieces(rimg, cimg)
    pw, qw, dots, known = pl.pallas_call(
        form_kernel,
        out_shape=[
            shape((3 * 64, LANES)), shape((3 * BLOCKS, TILE)), shape((16, LANES)), shape((8, LANES)),
        ],
        in_specs=[SMEM] + [VMEM] * 7,
        out_specs=[VMEM] * 4,
        scratch_shapes=[column, pltpu.VMEM((8, LANES), F32)],
        compiler_params=params(24),
    )(meta, rimg, cimg, pb, qb, pv, qv, kern)

    dots = summed(summed(dots, "tgt"), "src")
    vectors = [
        pltpu.with_memory_space_constraint(value, pltpu.HBM) for value in (known, pb, qb, pw, qw)
    ]
    outs = pl.pallas_call(
        grad_kernel,
        out_shape=[shape((1, PART))] * 2
        + [shape((8, LANES))]
        + [shape((8, FEATS, PART))] * 2
        + [shape((4, FEATS, PART))] * 3
        + [shape((4, FEATS // 2, PART))] * 2,
        in_specs=[SMEM, VMEM] + [HBM] * 5 + [ANY] * 8,
        out_specs=[VMEM] * 10,
        scratch_shapes=[
            *(pltpu.VMEM(value.shape, F32) for value in (known, pb, qb, pw, qw)),
            feats,
            feats,
            pltpu.VMEM((64, LANES), F32),
            pltpu.VMEM((BLOCKS, TILE), F32),
            column,
            pltpu.VMEM((CHUNK, TILE), BF16),
            pltpu.VMEM((CHUNK, TILE), BF16),
            pltpu.VMEM((FEATS + 16, TILE), BF16),
            pltpu.VMEM((FEATS + 16, TILE), BF16),
            pltpu.VMEM((BLOCKS, FEATS + 16, TILE), F32),
            pltpu.VMEM((BLOCKS, FEATS + 16, TILE), F32),
            pltpu.VMEM((3, TILE, TILE), F32),
            pltpu.SemaphoreType.DMA((3,)),
            pltpu.SemaphoreType.DMA((5,)),
            pltpu.SemaphoreType.DMA((32,)),
        ],
        compiler_params=params(40),
    )(meta, dots, *vectors, *s_parts, *t_parts, stored)
    adj_s, adj_t = outs[:2]
    grad_src, grad_tgt = scatter_all(*outs[2:])
    return adj_s.reshape(PART), adj_t.reshape(PART), grad_src, grad_tgt


def solution(mesh):
    in_specs = (
        P(None, ("src", "tgt")),
        P(None, ("tgt", "src")),
        P(("src", "tgt")),
        P(("tgt", "src")),
        P(("src", "tgt")),
        P(("tgt", "src")),
        P(("src", "tgt")),
        P(("tgt", "src")),
        P("src", "tgt", None),
        P("src", "tgt", None),
        P("src", "tgt"),
    )
    out_specs = (
        P(("src", "tgt")),
        P(("tgt", "src")),
        P(None, ("src", "tgt")),
        P(None, ("tgt", "src")),
    )
    return jax.shard_map(shards, mesh=mesh, in_specs=in_specs, out_specs=out_specs, check_vma=False)
```

```python
import math

import jax
import jax.numpy as jnp
from jax import lax
from jax.experimental import pallas as pl
from jax.experimental.pallas import tpu as pltpu
from jax.sharding import PartitionSpec as P

TILE = 1024
FEATS = 64
LANES = 128
BLOCKS = 8
SLOTS = 8
PART = 512
EPS = 0.05
RHO = 1.0
SCALE = 2.0 * math.log2(math.e) / EPS
DOWN = 2.0**-40
UP = 2.0**40
F32 = jnp.float32
BF16 = jnp.bfloat16
VMEM = pl.BlockSpec(memory_space=pltpu.VMEM)
SMEM = pl.BlockSpec(memory_space=pltpu.SMEM)
ANY = pl.BlockSpec(memory_space=pl.ANY)
HBM = pl.BlockSpec(memory_space=pltpu.HBM)
RING = (0, -1, 1, 4, -2, -3, 2, 3)
QUAD = (0, 1, -1, 2)


def params(mib):
    return pltpu.CompilerParams(vmem_limit_bytes=mib * 2**20)


def shape(dims, dtype=F32):
    return jax.ShapeDtypeStruct(dims, dtype)


def split3(value):
    high = value.astype(BF16).astype(F32)
    rest = value - high
    middle = rest.astype(BF16).astype(F32)
    low = (rest - middle).astype(BF16).astype(F32)
    return high, middle, low


def to_positions(value, turned):
    turned[...] = value.T
    groups = [turned[pl.ds(g, 8, stride=64), :] for g in range(64)]
    return jnp.concatenate(groups, axis=0).T


def to_cells(value, turned):
    turned[...] = value.T
    groups = [turned[pl.ds(r, 64, stride=8), :] for r in range(8)]
    return jnp.concatenate(groups, axis=0).T


def payload_kernel(*refs):
    sources, (out_s, out_t), held = refs[:8], refs[8:10], refs[10:18]
    turned, sems = refs[18:]
    copies = [
        pltpu.make_async_copy(source, place, sems.at[i])
        for i, (source, place) in enumerate(zip(sources, held))
    ]
    for copy in copies:
        copy.start()
    for copy in copies:
        copy.wait()
    sf, tf, rp, cp, sm, tm, rs, rt = held
    for feat, pot, mass, rhs, out, first in (
        (sf, rp, sm, rs, out_s, True),
        (tf, cp, tm, rt, out_t, False),
    ):
        wide = feat[...].astype(F32)
        potential = pot[...]
        term = (potential - jnp.sum(wide * wide, axis=0, keepdims=True)) * 0.5
        damp = EPS / RHO * mass[...] * jnp.exp(-potential / RHO)
        ones = jnp.ones((3, PART), F32)
        pieces = list(split3(term))
        rows = pieces + [ones] if first else [ones] + pieces
        rows += list(split3(rhs[...])) + list(split3(damp))
        rows.append(jnp.zeros((4, PART), F32))
        tail = jnp.concatenate(rows, axis=0)
        if first:
            whole = jnp.concatenate([wide, tail, jnp.zeros((48, PART), F32)], axis=0)
            whole = to_positions(whole, turned)
            out[0:FEATS, :] = whole[:FEATS].astype(BF16)
            keep = lax.broadcasted_iota(jnp.int32, (16, PART), 0) < 6
            tail = jnp.where(keep, whole[FEATS : FEATS + 16], tail)
        else:
            out[0:FEATS, :] = feat[...]
        out[FEATS : FEATS + 16, :] = tail.astype(BF16)


def three(rows, start):
    return rows[start : start + 1] + (rows[start + 1 : start + 2] + rows[start + 2 : start + 3])


def lane_blocks(row, height):
    return [
        jnp.broadcast_to(row[:, LANES * l : LANES * (l + 1)], (height, LANES))
        for l in range(TILE // LANES)
    ]


def total(values):
    while len(values) > 1:
        joined = [values[i] + values[i + 1] for i in range(0, len(values) - 1, 2)]
        values = joined + list(values[len(values) // 2 * 2 :])
    return values[0]


def block_rows(block):
    return pl.ds(pl.multiple_of(8 * block, 8), 8)


def fill_columns(column, packed):
    for g in range(LANES):
        column[8 * g : 8 * g + 8, :] = jnp.broadcast_to(packed[:, g : g + 1], (8, LANES))


def lane_sums(partial):
    lane = lax.broadcasted_iota(jnp.int32, (8, LANES), 1)
    result = jnp.zeros((8, LANES), F32)
    for g in range(LANES):
        group = jnp.sum(partial[8 * g : 8 * g + 8, :], axis=1, keepdims=True)
        result = jnp.where(lane == g, group, result)
    return result


def add_block(ref, first, block, value):
    rows = pl.ds(pl.multiple_of(first + 8 * block, 8), 8)
    ref[rows, :] = ref[rows, :] + value


def add_sums(ref, index, sums):
    row = jnp.sum(jnp.concatenate(sums, axis=1), axis=0, keepdims=True)
    ref[pl.ds(index, 1), :] = ref[pl.ds(index, 1), :] + row


def unpack(value):
    return jnp.concatenate(
        [value[BLOCKS * l : BLOCKS * (l + 1)] for l in range(TILE // LANES)], axis=1
    )


def pack_into(out, first, value):
    for l in range(TILE // LANES):
        out[first + BLOCKS * l : first + BLOCKS * (l + 1), :] = value[:, LANES * l : LANES * (l + 1)]


def ring_block(me, dz, other):
    place = lax.rem(me // 2 + (dz + 8), 8)
    core = lax.rem(me, 2)
    return 2 * place + (1 - core if other else core)


def quad_block(me, dy, dx):
    return 4 * lax.rem(me // 4 + (dy + 4), 4) + lax.rem(lax.rem(me, 4) + (dx + 4), 4)


def fetch(kern, held, sems, slot):
    place = lax.rem(slot, 3)
    return pltpu.make_async_copy(kern, held.at[place], sems.at[place])


def start_fetch(low, high, held, sems, slot):
    @pl.when(slot < SLOTS // 2)
    def _():
        fetch(low.at[slot], held, sems, slot).start()

    @pl.when(slot >= SLOTS // 2)
    def _():
        fetch(high.at[slot - SLOTS // 2], held, sems, slot).start()


def start_fetching(low, held, sems, count):
    fetch(low.at[0], held, sems, 0).start()

    @pl.when(count > 1)
    def _():
        fetch(low.at[1], held, sems, 1).start()


def next_tile(low, high, held, sems, slot, count):
    @pl.when(slot + 2 < count)
    def _():
        start_fetch(low, high, held, sems, slot + 2)

    fetch(low.at[0], held, sems, slot).wait()
    return held.at[lax.rem(slot, 3)]


WIDE = TILE // LANES
CHUNK = 256


def no_sums():
    return tuple(jnp.zeros((8, LANES), F32) for l in range(WIDE))


def lanes_of(l):
    return slice(LANES * l, LANES * (l + 1))


def part_copies(pieces, xs, ys, sems):
    s0, s1, t0, t1, t2, t3, t4 = pieces
    moves = (
        (s0, xs.at[0:8]),
        (s1, xs.at[8:16]),
        (t0, ys.at[0:4]),
        (t1, ys.at[4:8]),
        (t2, ys.at[8:12]),
        (t3, ys.at[12:14]),
        (t4, ys.at[14:16]),
    )
    return [
        pltpu.make_async_copy(source, place, sems.at[i])
        for i, (source, place) in enumerate(moves)
    ]


def places(me_s, me_t):
    part = jnp.arange(16, dtype=jnp.int32)
    dz = lax.rem(part // 2 - me_t // 2 + 8, 8)
    src = sum(jnp.where(dz == z % 8, k, 0) for k, z in enumerate(RING))
    src = src + 8 * jnp.not_equal(lax.rem(part, 2), lax.rem(me_t, 2)).astype(jnp.int32)
    dy = lax.rem(part // 4 - me_s // 4 + 4, 4)
    dx = lax.rem(lax.rem(part, 4) - lax.rem(me_s, 4) + 4, 4)
    tgt = sum(jnp.where(dy == y % 4, k, 0) for k, y in enumerate(QUAD))
    tgt = tgt + sum(jnp.where(dx == x % 4, 4 * k, 0) for k, x in enumerate((0, -1, 1, 2)))
    return src, tgt


def src_pair(meta, ref, block):
    return jnp.concatenate([ref[meta[19 + 2 * block]], ref[meta[20 + 2 * block]]], axis=1)


def tgt_pair(meta, ref, block):
    return jnp.concatenate([ref[meta[35 + 2 * block]], ref[meta[36 + 2 * block]]], axis=1)


def build_kernel(
    meta, s0, s1, t0, t1, t2, t3, t4,
    kern, pb, qb, rout, cout,
    xs, ys, left, right, sums, prods, column, csum, parts, ahead, behind, sems,
):
    pieces = (s0, s1, t0, t1, t2, t3, t4)
    copies = part_copies(pieces, xs, ys, sems)
    for copy in copies:
        copy.start()
    rout[...] = jnp.zeros_like(rout)
    csum[...] = jnp.zeros_like(csum)
    for copy in copies:
        copy.wait()
    for part in range(16):
        for place, ref, first in ((0, xs, 19), (2, ys, 35)):
            rows = ref[meta[first + part], FEATS : FEATS + 16, :].astype(F32)
            at = part // 2 + 8 * (part % 2)
            parts[place, at : at + 1, :] = three(rows, 6)
            parts[place + 1, at : at + 1, :] = three(rows, 9)
    for place in range(2):
        even, odd = parts[place, 0:8, :], parts[place, 8:16, :]
        for r in range(8):
            cells = slice(64 * r, 64 * (r + 1))
            pb[pl.ds(64 * place + r, 8, stride=8), :] = jnp.concatenate(
                [even[:, cells], odd[:, cells]], axis=1
            )
        for side in range(2):
            qb[8 * place : 8 * place + 8, PART * side : PART * (side + 1)] = parts[
                2 + place, 8 * side : 8 * side + 8, :
            ]

    keep = lax.broadcasted_iota(jnp.int32, (16, TILE), 0) < 6
    blank = jnp.zeros((48, TILE), BF16)

    def with_terms(payload):
        terms = jnp.where(keep, payload[FEATS:].astype(F32), 0.0).astype(BF16)
        return jnp.concatenate([payload[:FEATS], terms, blank], axis=0)

    def tile(slot, carry):
        rb, cb = meta[slot], meta[8 + slot]
        kernel = kern.at[slot]
        left[...] = with_terms(src_pair(meta, xs, rb)).T
        right[...] = with_terms(tgt_pair(meta, ys, cb))
        q = lane_blocks(qb[pl.ds(cb, 1), :], 8)
        fill_columns(column, pb[block_rows(rb), :])

        products = (ahead, behind)

        def product(chunk):
            products[chunk % 2][...] = jnp.dot(
                left[CHUNK * chunk : CHUNK * (chunk + 1), :],
                right[...],
                preferred_element_type=F32,
            )

        csums, cprods = no_sums(), no_sums()
        product(0)
        for chunk in range(TILE // CHUNK):
            if CHUNK * (chunk + 1) < TILE:
                product(chunk + 1)
            for u in range(CHUNK // 8):
                near = slice(8 * u, 8 * u + 8)
                at = slice(CHUNK * chunk + 8 * u, CHUNK * chunk + 8 * u + 8)
                ks = [
                    jnp.exp2(products[chunk % 2][near, lanes_of(l)] * SCALE) for l in range(WIDE)
                ]
                for l in range(WIDE):
                    kernel[at, lanes_of(l)] = ks[l]
                p = column[at, :]
                sums[at, :] = total(ks)
                prods[at, :] = total([ks[l] * q[l] for l in range(WIDE)])
                csums = tuple(csums[l] + ks[l] for l in range(WIDE))
                cprods = tuple(cprods[l] + ks[l] * p for l in range(WIDE))
        add_block(rout, 0, rb, lane_sums(sums))
        add_block(rout, 64, rb, lane_sums(prods))
        add_sums(csum, cb, csums)
        add_sums(csum, 8 + cb, cprods)
        return carry

    lax.fori_loop(0, meta[16], tile, 0)
    pack_into(cout, 0, csum[:8, :])
    pack_into(cout, 64, csum[8:, :])


def folded(value, join):
    if value.shape[1] == LANES:
        return value
    result = value[:, :LANES]
    for l in range(1, WIDE):
        result = join(result, value[:, lanes_of(l)])
    return result


def lane_partial(value):
    return folded(jnp.sum(value, axis=0, keepdims=True), jnp.add)


def lane_largest(value):
    return folded(jnp.max(value, axis=0, keepdims=True), jnp.maximum)


def scalar(row):
    return jnp.sum(row, axis=1, keepdims=True)


def storing(kern, stored, sems, first, slot):
    return pltpu.make_async_copy(kern.at[first + slot], stored.at[slot], sems.at[slot])


def start_storing(kern, stored, sems, first, count):
    def begin(slot, carry):
        storing(kern, stored, sems, first, slot).start()
        return carry

    lax.fori_loop(0, count, begin, 0)


def finish_storing(kern, stored, sems, first, count):
    def finish(slot, carry):
        storing(kern, stored, sems, first, slot).wait()
        return carry

    lax.fori_loop(0, count, finish, 0)


def apply_kernel(
    meta, rows_in, cols_in, pb, qb, kern,
    pv, qv, rout, cout, stored,
    prods, column, csum, out_sems,
):
    count = jnp.minimum(meta[16], SLOTS // 2)
    start_storing(kern, stored, out_sems, 0, count)
    rows = (rows_in[:64, :], rows_in[64:, :])
    cols = (unpack(cols_in[:64, :]), unpack(cols_in[64:, :]))
    rout[...] = jnp.zeros_like(rout)
    csum[...] = jnp.zeros_like(csum)
    cout[64:128, :] = jnp.zeros((64, LANES), F32)
    for (marg, prod), given, out, image, height in (
        (rows, pb, pv, cout, 64),
        (cols, qb, qv, rout, 8),
    ):
        b, d = given[:height, :], given[height:, :]
        g = marg + d
        v = g * (b * DOWN) + prod * DOWN
        out[:height, :] = v
        out[height:, :] = g
        for place, value in enumerate(
            (lane_partial(b * b), lane_partial(b * v), lane_partial(v * v), lane_largest(g))
        ):
            image[64 + place : 65 + place, :] = value

    def tile(slot, carry):
        rb, cb = meta[slot], meta[8 + slot]
        kernel = kern.at[slot]
        q = lane_blocks(qv[pl.ds(cb, 1), :], 8)
        fill_columns(column, pv[block_rows(rb), :])

        cprods = no_sums()
        for u in range(TILE // 8):
            at = slice(8 * u, 8 * u + 8)
            ks = [kernel[at, lanes_of(l)] for l in range(WIDE)]
            p = column[at, :]
            prods[at, :] = total([ks[l] * q[l] for l in range(WIDE)])
            cprods = tuple(cprods[l] + ks[l] * p for l in range(WIDE))
        add_block(rout, 0, rb, lane_sums(prods))
        add_sums(csum, cb, cprods)
        return carry

    lax.fori_loop(0, meta[16], tile, 0)
    pack_into(cout, 0, csum[...])
    finish_storing(kern, stored, out_sems, 0, count)


def form_kernel(
    meta, rows_in, cols_in, pb, qb, pv, qv, kern,
    pw, qw, dots, known, stored,
    column, acc, out_sems,
):
    count = jnp.maximum(meta[16] - SLOTS // 2, 0)
    start_storing(kern, stored, out_sems, SLOTS // 2, count)
    both = rows_in[64:72, :] + cols_in[64:72, :]
    bb, bv, vv, sigma = (scalar(both[i : i + 1]) for i in range(4))
    rows, cols = rows_in[:64, :], unpack(cols_in[:64, :])
    inverse = 1.0 / sigma
    lift = UP * inverse
    alpha = bb / (bv * lift)
    known[...] = jnp.zeros_like(known)
    for place, value in enumerate((bb, bv * lift, (vv * lift) * lift, inverse)):
        known[place : place + 1, :] = jnp.broadcast_to(value, (1, LANES))
    found = []
    for given, vectors, image, out, height in ((pb, pv, rows, pw, 64), (qb, qv, cols, qw, 8)):
        b, v, g = given[:height, :], vectors[:height, :], vectors[height:, :]
        second = g * v + image
        first = v * lift
        next_image = (second * lift) * inverse
        residual = b - alpha * first
        turned = first - alpha * next_image
        out[:height, :] = residual
        out[height : 2 * height, :] = turned
        out[2 * height :, :] = first
        found.append(
            (
                lane_partial(residual * residual),
                lane_partial(residual * turned),
                lane_partial(residual * first),
                lane_partial(turned * turned),
                lane_partial(turned * first),
                lane_partial(next_image * turned),
                lane_partial(first * next_image),
                lane_partial((g * inverse) * turned * turned),
                *(lane_largest(jnp.abs(vector)) for vector in (b, residual, turned, first)),
                lane_largest(g),
            )
        )
    acc[...] = jnp.zeros_like(acc)

    def tile(slot, carry):
        rb, cb = meta[slot], meta[8 + slot]
        kernel = kern.at[slot]
        q = lane_blocks(qw[pl.ds(8 + cb, 1), :] * inverse, 8)
        fill_columns(column, pw[pl.ds(pl.multiple_of(64 + 8 * rb, 8), 8), :])

        cprods = no_sums()
        for u in range(TILE // 8):
            at = slice(8 * u, 8 * u + 8)
            p = column[at, :]
            cprods = tuple(cprods[l] + kernel[at, lanes_of(l)] * p for l in range(WIDE))
        acc[...] = acc[...] + total([cprods[l] * q[l] for l in range(WIDE)])
        return carry

    lax.fori_loop(0, meta[16], tile, 0)
    for place in range(8):
        value = (found[0][place] + found[1][place]) * (1.0 / 16.0)
        if place == 7:
            value = value + 2.0 * jnp.sum(acc[...], axis=0, keepdims=True)
        dots[place : place + 1, :] = value
    for place in range(8, 13):
        dots[place : place + 1, :] = jnp.maximum(found[0][place], found[1][place])
    dots[13:16, :] = jnp.zeros((3, LANES), F32)
    finish_storing(kern, stored, out_sems, SLOTS // 2, count)


def grad_kernel(
    meta, dots, known_in, pb_in, qb_in, pw_in, qw_in, s0, s1, t0, t1, t2, t3, t4, low, high,
    adj_s, adj_t, level, near, far, x0, x1, x2, x3, x4,
    known, pb, qb, pw, qw, xs, ys,
    ap, aq, column, ahead, behind, x_block, y_block, row_wy, col_wx, held, sems, vector_sems,
    part_sems,
):
    tiles = meta[16]
    me_s, me_t = meta[17], meta[18]
    vectors_in = ((known_in, known), (pb_in, pb), (qb_in, qb), (pw_in, pw), (qw_in, qw))
    copies = [
        pltpu.make_async_copy(source, place, vector_sems.at[i])
        for i, (source, place) in enumerate(vectors_in)
    ]
    for copy in copies:
        copy.start()
    start_fetching(low, held, sems, tiles)
    part_moves = part_copies((s0, s1, t0, t1, t2, t3, t4), xs, ys, part_sems)
    for copy in part_moves:
        copy.start()
    row_wy[...] = jnp.zeros_like(row_wy)
    col_wx[...] = jnp.zeros_like(col_wx)
    for copy in copies:
        copy.wait()
    ee, ew, eh, ww, wh, uw, hu, waw = (scalar(dots[i : i + 1, :]) for i in range(8))
    bb, bh, hh, inverse = (known[i : i + 1, 0:1] for i in range(4))
    alpha1 = bb / bh
    beta1 = ee / bb
    dad = ew + 2.0 * beta1 * eh + beta1 * beta1 * bh
    alpha2 = ee / dad
    e_ad = ew + beta1 * eh
    ad_ad = ww + 2.0 * beta1 * wh + beta1 * beta1 * hh
    rr2 = ee - 2.0 * alpha2 * e_ad + alpha2 * alpha2 * ad_ad
    beta2 = rr2 / ee
    form = waw + 2.0 * beta1 * uw + beta1 * beta1 * hu
    r_ar = ew - 2.0 * alpha2 * (ww + beta1 * wh) + alpha2 * alpha2 * form
    d2_ar2 = ew + beta1 * eh - alpha2 * ad_ad
    d3ad3 = r_ar + 2.0 * beta2 * d2_ar2 + beta2 * beta2 * dad
    alpha3 = rr2 / d3ad3
    on_b = (alpha1 + alpha2 * beta1 + alpha3 * beta2 * beta1) * inverse
    on_e = (alpha2 + alpha3 * (1.0 + beta2)) * inverse
    on_w = -(alpha3 * alpha2) * inverse
    on_h = on_w * beta1
    for given, vectors, out, height in ((pb, pw, ap, 64), (qb, qw, aq, 8)):
        e, w, h = (vectors[height * i : height * (i + 1), :] for i in range(3))
        out[...] = on_b * given[:height, :] + on_e * e + on_w * w + on_h * h
    own = ap[block_rows(me_t // 2), :]
    own = jnp.where(me_t % 2 == 1, own[:, 64:], own[:, :64])
    for r in range(8):
        adj_s[:, 64 * r : 64 * (r + 1)] = own[r : r + 1, :]
    row = aq[pl.ds(me_s // 2, 1), :]
    adj_t[...] = jnp.where(me_s % 2 == 1, row[:, PART:], row[:, :PART])


    largest = [jnp.max(dots[i : i + 1, :], axis=1, keepdims=True) for i in range(8, 13)]
    reach = total(
        [jnp.abs(c) * m for c, m in zip((on_b, on_e, on_w, on_h), largest[:4])]
    )
    bound = jnp.maximum((60.0 * 1.05) * (reach * largest[4]), 1e-30)
    scale = 60000.0 / bound
    level[...] = jnp.broadcast_to(1.0 / scale, (8, LANES))

    def tile(slot, carry):
        rb, cb = meta[slot], meta[8 + slot]
        fill_columns(column, ap[block_rows(rb), :])
        q = lane_blocks(aq[pl.ds(cb, 1), :], 16)
        kernel = next_tile(low, high, held, sems, slot, tiles)


        @pl.when(slot == 0)
        def _():
            for copy in part_moves:
                copy.wait()

        x_block[...] = src_pair(meta, xs, rb)
        y_block[...] = tgt_pair(meta, ys, cb)
        halves = (ahead, behind)

        def weights(chunk):
            for u in range(CHUNK // 16):
                at = slice(CHUNK * chunk + 16 * u, CHUNK * chunk + 16 * u + 16)
                p = column[at, :]
                for l in range(WIDE):
                    halves[chunk % 2][16 * u : 16 * u + 16, lanes_of(l)] = (
                        kernel[at, lanes_of(l)] * (p + q[l])
                    ).astype(BF16)

        weights(0)
        for chunk in range(TILE // CHUNK):
            cells = slice(CHUNK * chunk, CHUNK * (chunk + 1))
            if CHUNK * (chunk + 1) < TILE:
                weights(chunk + 1)
            half = halves[chunk % 2][...]
            part, inner = 2 * rb + chunk // 2, slice(CHUNK * (chunk % 2), CHUNK * (chunk % 2 + 1))
            row_wy[part, :, inner] = row_wy[part, :, inner] + lax.dot_general(
                y_block[...], half, (((1,), (1,)), ((), ())), preferred_element_type=F32
            )
            for side in range(2):
                columns = slice(PART * side, PART * (side + 1))
                col_wx[2 * cb + side] = col_wx[2 * cb + side] + jnp.dot(
                    x_block[:, cells], half[:, columns], preferred_element_type=F32
                )
        return carry

    lax.fori_loop(0, tiles, tile, 0)


    def part_of(payload, mixed, ones, part):
        wide = payload[:FEATS, :].astype(F32)
        weight = mixed[part, ones : ones + 1, :]
        return (wide * weight - mixed[part, :FEATS, :]) * (scale * (2.0 / EPS))

    for k in range(8):
        for other, out in enumerate((near, far)):
            out[k] = part_of(
                xs[8 * other + k], row_wy, FEATS, ring_block(me_t, RING[k], other)
            )
    for k in range(4):
        for step, (dx, out) in enumerate(((0, x0), (-1, x2), (1, x1), (2, None))):
            part = part_of(
                ys[4 * step + k], col_wx, FEATS + 3, quad_block(me_s, QUAD[k], dx)
            )
            if out is None:
                x3[k] = part[:32]
                x4[k] = part[32:]
            else:
                out[k] = part


def finish_kernel(value, level, out, turned):
    whole = jnp.concatenate([value[...], jnp.zeros((FEATS, PART), F32)], axis=0)
    out[...] = to_cells(whole, turned)[:FEATS] * level[0:1, 0:1]


def swap(value, axis, mask):
    return lax.ppermute(value, axis, [(i, i ^ mask) for i in range(16)])


def along_z(value, step):
    return lax.ppermute(value, "tgt", [(i, (i + 2 * step) % 16) for i in range(16)])


def along_y(value, step):
    return lax.ppermute(value, "src", [(i, (i + 4 * step) % 16) for i in range(16)])


def along_x(value, step):
    return lax.ppermute(value, "src", [(i, i // 4 * 4 + (i + step) % 4) for i in range(16)])


def exchange(value, axis):
    return lax.all_to_all(value, axis, 0, 0)


def summed(value, axis):
    everywhere = jnp.broadcast_to(value[None], (16, *value.shape))
    found = exchange(everywhere, axis)
    return jnp.concatenate([jnp.sum(found[:, :8], axis=0), jnp.max(found[:, 8:], axis=0)])


def sum_pieces(row, col):
    for masks in ((4, 8, 12), (1, 2, 3)):
        rows = [row] + [swap(row, "tgt", mask) for mask in masks]
        cols = [col] + [swap(col, "src", mask) for mask in masks]
        both = together(*rows, *cols)
        row = (both[0] + both[1]) + (both[2] + both[3])
        col = (both[4] + both[5]) + (both[6] + both[7])
    return row, col


def together(*values):
    return lax.optimization_barrier(values)


def gather_all(own_s, own_t):
    after, before, across = along_z(own_s, 1), along_z(own_s, -1), along_z(own_s, 4)
    up, down, over = along_y(own_t, 1), along_y(own_t, -1), along_y(own_t, 2)
    after, before, across, up, down, over = together(after, before, across, up, down, over)
    stack = jnp.stack([own_t, down, up, over])
    low, high = jnp.stack([own_s, after]), jnp.stack([own_s, before])
    right, left = along_x(stack, 1), along_x(stack, -1)
    low, high = along_z(low, 2), along_z(high, -2)
    right, left, low, high = together(right, left, low, high)
    near = jnp.concatenate([jnp.stack([own_s, after, before, across]), low, high])
    far = swap(near, "tgt", 1)
    return (near, far), (stack, right, left, along_x(right[:2], 1), along_x(left[2:], -1))


def narrow(value):
    return value.astype(jnp.float16)


def widened(values):
    return [value.astype(F32) for value in values]


def scatter_all(level, near, far, own, next_up, next_down, top, bottom):
    half = FEATS // 2
    other = swap(far, "tgt", 1)
    top, bottom = along_x(narrow(top), 1), along_x(narrow(bottom), -1)
    other, top, bottom = together(other, top, bottom)
    near = near + other
    top, bottom = widened((top, bottom))
    up = jnp.concatenate([next_up[:, :half] + top, next_up[:, half:]], axis=1)
    down = jnp.concatenate([next_down[:, :half], next_down[:, half:] + bottom], axis=1)
    up, down = along_x(narrow(up), 1), along_x(narrow(down), -1)
    after, before = along_z(narrow(near[6:8]), 2), along_z(narrow(near[4:6]), -2)
    up, down, after, before = widened(together(up, down, after, before))
    part = (own + up) + down
    last = (
        along_z(narrow(near[2] + after[1]), 1),
        along_z(narrow(near[1] + before[1]), -1),
        along_z(narrow(near[3]), 4),
        along_y(narrow(part[1]), 1),
        along_y(narrow(part[2]), -1),
        along_y(narrow(part[3]), 2),
    )
    last = widened(together(*last))
    grad_src = ((near[0] + after[0]) + before[0]) + ((last[0] + last[1]) + last[2])
    grad_src = pl.pallas_call(
        finish_kernel,
        out_shape=shape((FEATS, PART)),
        in_specs=[VMEM] * 2,
        out_specs=VMEM,
        scratch_shapes=[pltpu.VMEM((PART, LANES), F32)],
        compiler_params=params(24),
    )(grad_src, level)
    grad_tgt = ((part[0] + last[3]) + (last[4] + last[5])) * level[0, 0]
    return grad_src, grad_tgt


def shards(
    src_feat, tgt_feat, row_pot, col_pot, src_mass, tgt_mass, rhs_src, rhs_tgt,
    tile_rows, tile_cols, tile_count,
):
    me_s, me_t = lax.axis_index("src"), lax.axis_index("tgt")
    meta = jnp.concatenate(
        [
            tile_rows.reshape(8),
            tile_cols.reshape(8),
            tile_count.reshape(1),
            me_s.reshape(1).astype(jnp.int32),
            me_t.reshape(1).astype(jnp.int32),
            *places(me_s, me_t),
        ]
    )
    line = lambda v: v.reshape(1, PART)
    pay = (FEATS + 16, PART)
    pay_s, pay_t = pl.pallas_call(
        payload_kernel,
        out_shape=[shape(pay, BF16), shape(pay, BF16)],
        in_specs=[HBM] * 8,
        out_specs=[VMEM] * 2,
        scratch_shapes=[pltpu.VMEM((FEATS, PART), BF16)] * 2
        + [pltpu.VMEM((1, PART), F32)] * 6
        + [pltpu.VMEM((PART, LANES), F32), pltpu.SemaphoreType.DMA((8,))],
        compiler_params=params(24),
    )(
        *(
            pltpu.with_memory_space_constraint(value, pltpu.HBM)
            for value in (
                src_feat, tgt_feat, line(row_pot), line(col_pot), line(src_mass), line(tgt_mass),
                line(rhs_src), line(rhs_tgt),
            )
        )
    )
    s_parts, t_parts = gather_all(pay_s, pay_t)

    feats = pltpu.VMEM((16, *pay), BF16)
    packed = shape((2 * 64, LANES))
    natural = shape((2 * BLOCKS, TILE))
    column = pltpu.VMEM((TILE, LANES), F32)
    kern, pb, qb, rsum, csum = pl.pallas_call(
        build_kernel,
        out_shape=[
            pltpu.VMEM((SLOTS, TILE, TILE), F32),
            packed, natural, packed, packed,
        ],
        in_specs=[SMEM] + [ANY] * 7,
        out_specs=[VMEM] * 5,
        scratch_shapes=[
            feats,
            feats,
            pltpu.VMEM((TILE, LANES), BF16),
            pltpu.VMEM((LANES, TILE), BF16),
            column,
            column,
            column,
            pltpu.VMEM((2 * BLOCKS, TILE), F32),
            pltpu.VMEM((4, 16, PART), F32),
            pltpu.VMEM((CHUNK, TILE), F32),
            pltpu.VMEM((CHUNK, TILE), F32),
            pltpu.SemaphoreType.DMA((7,)),
        ],
        compiler_params=params(24),
    )(meta, *s_parts, *t_parts)
    kern = pltpu.with_memory_space_constraint(kern, pltpu.VMEM)

    rsum, csum = sum_pieces(rsum, csum)
    pv, qv, rimg, cimg, stored_low = pl.pallas_call(
        apply_kernel,
        out_shape=[packed, natural, packed, packed, shape((SLOTS // 2, TILE, TILE))],
        in_specs=[SMEM] + [VMEM] * 5,
        out_specs=[VMEM] * 4 + [ANY],
        scratch_shapes=[
            column, column, pltpu.VMEM((BLOCKS, TILE), F32), pltpu.SemaphoreType.DMA((SLOTS // 2,)),
        ],
        compiler_params=params(24),
    )(meta, rsum, csum, pb, qb, kern)

    rimg, cimg = sum_pieces(rimg, cimg)
    pw, qw, dots, known, stored_high = pl.pallas_call(
        form_kernel,
        out_shape=[
            shape((3 * 64, LANES)), shape((3 * BLOCKS, TILE)), shape((16, LANES)), shape((8, LANES)),
            shape((SLOTS // 2, TILE, TILE)),
        ],
        in_specs=[SMEM] + [VMEM] * 7,
        out_specs=[VMEM] * 4 + [ANY],
        scratch_shapes=[
            column, pltpu.VMEM((8, LANES), F32), pltpu.SemaphoreType.DMA((SLOTS // 2,)),
        ],
        compiler_params=params(24),
    )(meta, rimg, cimg, pb, qb, pv, qv, kern)

    dots = summed(summed(dots, "tgt"), "src")
    vectors = [
        pltpu.with_memory_space_constraint(value, pltpu.HBM) for value in (known, pb, qb, pw, qw)
    ]
    outs = pl.pallas_call(
        grad_kernel,
        out_shape=[shape((1, PART))] * 2
        + [shape((8, LANES))]
        + [shape((8, FEATS, PART))] * 2
        + [shape((4, FEATS, PART))] * 3
        + [shape((4, FEATS // 2, PART))] * 2,
        in_specs=[SMEM, VMEM] + [HBM] * 5 + [ANY] * 9,
        out_specs=[VMEM] * 10,
        scratch_shapes=[
            *(pltpu.VMEM(value.shape, F32) for value in (known, pb, qb, pw, qw)),
            feats,
            feats,
            pltpu.VMEM((64, LANES), F32),
            pltpu.VMEM((BLOCKS, TILE), F32),
            column,
            pltpu.VMEM((CHUNK, TILE), BF16),
            pltpu.VMEM((CHUNK, TILE), BF16),
            pltpu.VMEM((FEATS + 16, TILE), BF16),
            pltpu.VMEM((FEATS + 16, TILE), BF16),
            pltpu.VMEM((16, FEATS + 16, PART), F32),
            pltpu.VMEM((16, FEATS + 16, PART), F32),
            pltpu.VMEM((3, TILE, TILE), F32),
            pltpu.SemaphoreType.DMA((3,)),
            pltpu.SemaphoreType.DMA((5,)),
            pltpu.SemaphoreType.DMA((7,)),
        ],
        compiler_params=params(40),
    )(meta, dots, *vectors, *s_parts, *t_parts, stored_low, stored_high)
    adj_s, adj_t = outs[:2]
    grad_src, grad_tgt = scatter_all(*outs[2:])
    return adj_s.reshape(PART), adj_t.reshape(PART), grad_src, grad_tgt


def solution(mesh):
    in_specs = (
        P(None, ("src", "tgt")),
        P(None, ("tgt", "src")),
        P(("src", "tgt")),
        P(("tgt", "src")),
        P(("src", "tgt")),
        P(("tgt", "src")),
        P(("src", "tgt")),
        P(("tgt", "src")),
        P("src", "tgt", None),
        P("src", "tgt", None),
        P("src", "tgt"),
    )
    out_specs = (
        P(("src", "tgt")),
        P(("tgt", "src")),
        P(None, ("src", "tgt")),
        P(None, ("tgt", "src")),
    )
    return jax.shard_map(shards, mesh=mesh, in_specs=in_specs, out_specs=out_specs, check_vma=False)
```

```python
import math

import jax
import jax.numpy as jnp
from jax import lax
from jax.experimental import pallas as pl
from jax.experimental.pallas import tpu as pltpu
from jax.sharding import PartitionSpec as P

TILE = 1024
FEATS = 64
LANES = 128
BLOCKS = 8
SLOTS = 8
PART = 512
EPS = 0.05
RHO = 1.0
SCALE = 2.0 * math.log2(math.e) / EPS
DOWN = 2.0**-40
UP = 2.0**40
F32 = jnp.float32
BF16 = jnp.bfloat16
VMEM = pl.BlockSpec(memory_space=pltpu.VMEM)
SMEM = pl.BlockSpec(memory_space=pltpu.SMEM)
ANY = pl.BlockSpec(memory_space=pl.ANY)
HBM = pl.BlockSpec(memory_space=pltpu.HBM)
RING = (0, -1, 1, 4, -2, -3, 2, 3)
QUAD = (0, 1, -1, 2)


def params(mib):
    return pltpu.CompilerParams(vmem_limit_bytes=mib * 2**20)


def shape(dims, dtype=F32):
    return jax.ShapeDtypeStruct(dims, dtype)


def split3(value):
    high = value.astype(BF16).astype(F32)
    rest = value - high
    middle = rest.astype(BF16).astype(F32)
    low = (rest - middle).astype(BF16).astype(F32)
    return high, middle, low


def to_positions(value, turned):
    turned[...] = value.T
    groups = [turned[pl.ds(g, 8, stride=64), :] for g in range(64)]
    return jnp.concatenate(groups, axis=0).T


def to_cells(value, turned):
    turned[...] = value.T
    groups = [turned[pl.ds(r, 64, stride=8), :] for r in range(8)]
    return jnp.concatenate(groups, axis=0).T


def payload_kernel(*refs):
    sources, (out_s, out_t), held = refs[:8], refs[8:10], refs[10:18]
    turned, sems = refs[18:]
    copies = [
        pltpu.make_async_copy(source, place, sems.at[i])
        for i, (source, place) in enumerate(zip(sources, held))
    ]
    for copy in copies:
        copy.start()
    for copy in copies:
        copy.wait()
    sf, tf, rp, cp, sm, tm, rs, rt = held
    for feat, pot, mass, rhs, out, first in (
        (sf, rp, sm, rs, out_s, True),
        (tf, cp, tm, rt, out_t, False),
    ):
        wide = feat[...].astype(F32)
        potential = pot[...]
        term = (potential - jnp.sum(wide * wide, axis=0, keepdims=True)) * 0.5
        damp = EPS / RHO * mass[...] * jnp.exp(-potential / RHO)
        ones = jnp.ones((3, PART), F32)
        pieces = list(split3(term))
        rows = pieces + [ones] if first else [ones] + pieces
        rows += list(split3(rhs[...])) + list(split3(damp))
        rows.append(jnp.zeros((4, PART), F32))
        tail = jnp.concatenate(rows, axis=0)
        if first:
            whole = jnp.concatenate([wide, tail, jnp.zeros((48, PART), F32)], axis=0)
            whole = to_positions(whole, turned)
            out[0:FEATS, :] = whole[:FEATS].astype(BF16)
            keep = lax.broadcasted_iota(jnp.int32, (16, PART), 0) < 6
            tail = jnp.where(keep, whole[FEATS : FEATS + 16], tail)
        else:
            out[0:FEATS, :] = feat[...]
        out[FEATS : FEATS + 16, :] = tail.astype(BF16)


def three(rows, start):
    return rows[start : start + 1] + (rows[start + 1 : start + 2] + rows[start + 2 : start + 3])


def lane_blocks(row, height):
    return [
        jnp.broadcast_to(row[:, LANES * l : LANES * (l + 1)], (height, LANES))
        for l in range(TILE // LANES)
    ]


def total(values):
    while len(values) > 1:
        joined = [values[i] + values[i + 1] for i in range(0, len(values) - 1, 2)]
        values = joined + list(values[len(values) // 2 * 2 :])
    return values[0]


def block_rows(block):
    return pl.ds(pl.multiple_of(8 * block, 8), 8)


def fill_columns(column, packed):
    for g in range(LANES):
        column[8 * g : 8 * g + 8, :] = jnp.broadcast_to(packed[:, g : g + 1], (8, LANES))


def lane_sums(partial):
    lane = lax.broadcasted_iota(jnp.int32, (8, LANES), 1)
    result = jnp.zeros((8, LANES), F32)
    for g in range(LANES):
        group = jnp.sum(partial[8 * g : 8 * g + 8, :], axis=1, keepdims=True)
        result = jnp.where(lane == g, group, result)
    return result


def add_block(ref, first, block, value):
    rows = pl.ds(pl.multiple_of(first + 8 * block, 8), 8)
    ref[rows, :] = ref[rows, :] + value


def add_sums(ref, index, sums):
    row = jnp.sum(jnp.concatenate(sums, axis=1), axis=0, keepdims=True)
    ref[pl.ds(index, 1), :] = ref[pl.ds(index, 1), :] + row


def unpack(value):
    return jnp.concatenate(
        [value[BLOCKS * l : BLOCKS * (l + 1)] for l in range(TILE // LANES)], axis=1
    )


def pack_into(out, first, value):
    for l in range(TILE // LANES):
        out[first + BLOCKS * l : first + BLOCKS * (l + 1), :] = value[:, LANES * l : LANES * (l + 1)]


def ring_block(me, dz, other):
    place = lax.rem(me // 2 + (dz + 8), 8)
    core = lax.rem(me, 2)
    return 2 * place + (1 - core if other else core)


def quad_block(me, dy, dx):
    return 4 * lax.rem(me // 4 + (dy + 4), 4) + lax.rem(lax.rem(me, 4) + (dx + 4), 4)


def fetch(kern, held, sems, slot):
    place = lax.rem(slot, 3)
    return pltpu.make_async_copy(kern, held.at[place], sems.at[place])


def start_fetch(low, high, held, sems, slot):
    @pl.when(slot < SLOTS // 2)
    def _():
        fetch(low.at[slot], held, sems, slot).start()

    @pl.when(slot >= SLOTS // 2)
    def _():
        fetch(high.at[slot - SLOTS // 2], held, sems, slot).start()


def start_fetching(low, held, sems, count):
    fetch(low.at[0], held, sems, 0).start()

    @pl.when(count > 1)
    def _():
        fetch(low.at[1], held, sems, 1).start()


def next_tile(low, high, held, sems, slot, count):
    @pl.when(slot + 2 < count)
    def _():
        start_fetch(low, high, held, sems, slot + 2)

    fetch(low.at[0], held, sems, slot).wait()
    return held.at[lax.rem(slot, 3)]


WIDE = TILE // LANES
CHUNK = 256


def no_sums():
    return tuple(jnp.zeros((8, LANES), F32) for l in range(WIDE))


def lanes_of(l):
    return slice(LANES * l, LANES * (l + 1))


def part_copies(pieces, xs, ys, sems):
    s0, s1, t0, t1, t2, t3, t4 = pieces
    moves = (
        (s0, xs.at[0:8]),
        (s1, xs.at[8:16]),
        (t0, ys.at[0:4]),
        (t1, ys.at[4:8]),
        (t2, ys.at[8:12]),
        (t3, ys.at[12:14]),
        (t4, ys.at[14:16]),
    )
    return [
        pltpu.make_async_copy(source, place, sems.at[i])
        for i, (source, place) in enumerate(moves)
    ]


def places(me_s, me_t):
    part = jnp.arange(16, dtype=jnp.int32)
    dz = lax.rem(part // 2 - me_t // 2 + 8, 8)
    src = sum(jnp.where(dz == z % 8, k, 0) for k, z in enumerate(RING))
    src = src + 8 * jnp.not_equal(lax.rem(part, 2), lax.rem(me_t, 2)).astype(jnp.int32)
    dy = lax.rem(part // 4 - me_s // 4 + 4, 4)
    dx = lax.rem(lax.rem(part, 4) - lax.rem(me_s, 4) + 4, 4)
    tgt = sum(jnp.where(dy == y % 4, k, 0) for k, y in enumerate(QUAD))
    tgt = tgt + sum(jnp.where(dx == x % 4, 4 * k, 0) for k, x in enumerate((0, -1, 1, 2)))
    return src, tgt


def src_pair(meta, ref, block):
    return jnp.concatenate([ref[meta[19 + 2 * block]], ref[meta[20 + 2 * block]]], axis=1)


def tgt_pair(meta, ref, block):
    return jnp.concatenate([ref[meta[35 + 2 * block]], ref[meta[36 + 2 * block]]], axis=1)


def build_kernel(
    meta, s0, s1, t0, t1, t2, t3, t4,
    kern, pb, qb, rout, cout,
    xs, ys, left, right, sums, prods, column, csum, parts, ahead, behind, sems,
):
    pieces = (s0, s1, t0, t1, t2, t3, t4)
    copies = part_copies(pieces, xs, ys, sems)
    for copy in copies:
        copy.start()
    rout[...] = jnp.zeros_like(rout)
    csum[...] = jnp.zeros_like(csum)
    for copy in copies:
        copy.wait()
    for part in range(16):
        for place, ref, first in ((0, xs, 19), (2, ys, 35)):
            rows = ref[meta[first + part], FEATS : FEATS + 16, :].astype(F32)
            at = part // 2 + 8 * (part % 2)
            parts[place, at : at + 1, :] = three(rows, 6)
            parts[place + 1, at : at + 1, :] = three(rows, 9)
    for place in range(2):
        even, odd = parts[place, 0:8, :], parts[place, 8:16, :]
        for r in range(8):
            cells = slice(64 * r, 64 * (r + 1))
            pb[pl.ds(64 * place + r, 8, stride=8), :] = jnp.concatenate(
                [even[:, cells], odd[:, cells]], axis=1
            )
        for side in range(2):
            qb[8 * place : 8 * place + 8, PART * side : PART * (side + 1)] = parts[
                2 + place, 8 * side : 8 * side + 8, :
            ]

    keep = lax.broadcasted_iota(jnp.int32, (16, TILE), 0) < 6
    blank = jnp.zeros((48, TILE), BF16)

    def with_terms(payload):
        terms = jnp.where(keep, payload[FEATS:].astype(F32), 0.0).astype(BF16)
        return jnp.concatenate([payload[:FEATS], terms, blank], axis=0)

    def tile(slot, carry):
        rb, cb = meta[slot], meta[8 + slot]
        kernel = kern.at[slot]
        left[...] = with_terms(src_pair(meta, xs, rb)).T
        right[...] = with_terms(tgt_pair(meta, ys, cb))
        q = lane_blocks(qb[pl.ds(cb, 1), :], 8)
        fill_columns(column, pb[block_rows(rb), :])

        products = (ahead, behind)

        def product(chunk):
            products[chunk % 2][...] = jnp.dot(
                left[CHUNK * chunk : CHUNK * (chunk + 1), :],
                right[...],
                preferred_element_type=F32,
            )

        csums, cprods = no_sums(), no_sums()
        product(0)
        for chunk in range(TILE // CHUNK):
            if CHUNK * (chunk + 1) < TILE:
                product(chunk + 1)
            for u in range(CHUNK // 8):
                near = slice(8 * u, 8 * u + 8)
                at = slice(CHUNK * chunk + 8 * u, CHUNK * chunk + 8 * u + 8)
                ks = [
                    jnp.exp2(products[chunk % 2][near, lanes_of(l)] * SCALE) for l in range(WIDE)
                ]
                for l in range(WIDE):
                    kernel[at, lanes_of(l)] = ks[l]
                p = column[at, :]
                sums[at, :] = total(ks)
                prods[at, :] = total([ks[l] * q[l] for l in range(WIDE)])
                csums = tuple(csums[l] + ks[l] for l in range(WIDE))
                cprods = tuple(cprods[l] + ks[l] * p for l in range(WIDE))
        add_block(rout, 0, rb, lane_sums(sums))
        add_block(rout, 64, rb, lane_sums(prods))
        add_sums(csum, cb, csums)
        add_sums(csum, 8 + cb, cprods)
        return carry

    lax.fori_loop(0, meta[16], tile, 0)
    pack_into(cout, 0, csum[:8, :])
    pack_into(cout, 64, csum[8:, :])


def folded(value, join):
    if value.shape[1] == LANES:
        return value
    result = value[:, :LANES]
    for l in range(1, WIDE):
        result = join(result, value[:, lanes_of(l)])
    return result


def lane_partial(value):
    return folded(jnp.sum(value, axis=0, keepdims=True), jnp.add)


def lane_largest(value):
    return folded(jnp.max(value, axis=0, keepdims=True), jnp.maximum)


def scalar(row):
    return jnp.sum(row, axis=1, keepdims=True)


def storing(kern, stored, sems, first, slot):
    return pltpu.make_async_copy(kern.at[first + slot], stored.at[slot], sems.at[slot])


def start_storing(kern, stored, sems, first, count):
    def begin(slot, carry):
        storing(kern, stored, sems, first, slot).start()
        return carry

    lax.fori_loop(0, count, begin, 0)


def finish_storing(kern, stored, sems, first, count):
    def finish(slot, carry):
        storing(kern, stored, sems, first, slot).wait()
        return carry

    lax.fori_loop(0, count, finish, 0)


def four(pieces):
    return (pieces[0][...] + pieces[1][...]) + (pieces[2][...] + pieces[3][...])


def apply_kernel(
    meta, r0, r1, r2, r3, c0, c1, c2, c3, pb, qb, kern,
    pv, qv, rout, cout, stored,
    prods, column, csum, out_sems,
):
    count = jnp.minimum(meta[16], SLOTS // 2)
    start_storing(kern, stored, out_sems, 0, count)
    rows_in, cols_in = four((r0, r1, r2, r3)), four((c0, c1, c2, c3))
    rows = (rows_in[:64], rows_in[64:])
    cols = (unpack(cols_in[:64]), unpack(cols_in[64:]))
    rout[...] = jnp.zeros_like(rout)
    csum[...] = jnp.zeros_like(csum)
    cout[64:72, :] = jnp.zeros((8, LANES), F32)
    for (marg, prod), given, out, image, height in (
        (rows, pb, pv, cout, 64),
        (cols, qb, qv, rout, 8),
    ):
        b, d = given[:height, :], given[height:, :]
        g = marg + d
        v = g * (b * DOWN) + prod * DOWN
        out[:height, :] = v
        out[height:, :] = g
        for place, value in enumerate(
            (lane_partial(b * b), lane_partial(b * v), lane_partial(v * v), lane_largest(g))
        ):
            image[64 + place : 65 + place, :] = value

    def tile(slot, carry):
        rb, cb = meta[slot], meta[8 + slot]
        kernel = kern.at[slot]
        q = lane_blocks(qv[pl.ds(cb, 1), :], 8)
        fill_columns(column, pv[block_rows(rb), :])

        cprods = no_sums()
        for u in range(TILE // 8):
            at = slice(8 * u, 8 * u + 8)
            ks = [kernel[at, lanes_of(l)] for l in range(WIDE)]
            p = column[at, :]
            prods[at, :] = total([ks[l] * q[l] for l in range(WIDE)])
            cprods = tuple(cprods[l] + ks[l] * p for l in range(WIDE))
        add_block(rout, 0, rb, lane_sums(prods))
        add_sums(csum, cb, cprods)
        return carry

    lax.fori_loop(0, meta[16], tile, 0)
    pack_into(cout, 0, csum[...])
    finish_storing(kern, stored, out_sems, 0, count)


def form_kernel(
    meta, r0, r1, r2, r3, c0, c1, c2, c3, pb, qb, pv, qv, kern,
    pw, qw, dots, known, stored,
    column, acc, out_sems,
):
    count = jnp.maximum(meta[16] - SLOTS // 2, 0)
    start_storing(kern, stored, out_sems, SLOTS // 2, count)
    rows_in, cols_in = four((r0, r1, r2, r3)), four((c0, c1, c2, c3))
    both = rows_in[64:72] + cols_in[64:72]
    bb, bv, vv, sigma = (scalar(both[i : i + 1]) for i in range(4))
    rows, cols = rows_in[:64], unpack(cols_in[:64])
    inverse = 1.0 / sigma
    lift = UP * inverse
    alpha = bb / (bv * lift)
    known[...] = jnp.zeros_like(known)
    for place, value in enumerate((bb, bv * lift, (vv * lift) * lift, inverse)):
        known[place : place + 1, :] = jnp.broadcast_to(value, (1, LANES))
    found = []
    for given, vectors, image, out, height in ((pb, pv, rows, pw, 64), (qb, qv, cols, qw, 8)):
        b, v, g = given[:height, :], vectors[:height, :], vectors[height:, :]
        second = g * v + image
        first = v * lift
        next_image = (second * lift) * inverse
        residual = b - alpha * first
        turned = first - alpha * next_image
        out[:height, :] = residual
        out[height : 2 * height, :] = turned
        out[2 * height :, :] = first
        found.append(
            (
                lane_partial(residual * residual),
                lane_partial(residual * turned),
                lane_partial(residual * first),
                lane_partial(turned * turned),
                lane_partial(turned * first),
                lane_partial(next_image * turned),
                lane_partial(first * next_image),
                lane_partial((g * inverse) * turned * turned),
                *(lane_largest(jnp.abs(vector)) for vector in (b, residual, turned, first)),
                lane_largest(g),
            )
        )
    acc[...] = jnp.zeros_like(acc)

    def tile(slot, carry):
        rb, cb = meta[slot], meta[8 + slot]
        kernel = kern.at[slot]
        q = lane_blocks(qw[pl.ds(8 + cb, 1), :] * inverse, 8)
        fill_columns(column, pw[pl.ds(pl.multiple_of(64 + 8 * rb, 8), 8), :])

        cprods = no_sums()
        for u in range(TILE // 8):
            at = slice(8 * u, 8 * u + 8)
            p = column[at, :]
            cprods = tuple(cprods[l] + kernel[at, lanes_of(l)] * p for l in range(WIDE))
        acc[...] = acc[...] + total([cprods[l] * q[l] for l in range(WIDE)])
        return carry

    lax.fori_loop(0, meta[16], tile, 0)
    for place in range(8):
        value = (found[0][place] + found[1][place]) * (1.0 / 16.0)
        if place == 7:
            value = value + 2.0 * jnp.sum(acc[...], axis=0, keepdims=True)
        dots[place : place + 1, :] = value
    for place in range(8, 13):
        dots[place : place + 1, :] = jnp.maximum(found[0][place], found[1][place])
    dots[13:16, :] = jnp.zeros((3, LANES), F32)
    finish_storing(kern, stored, out_sems, SLOTS // 2, count)


def grad_kernel(
    meta, found, known_in, pb_in, qb_in, pw_in, qw_in, s0, s1, t0, t1, t2, t3, t4, low, high,
    adj_s, adj_t, level, near, far, x0, x1, x2, x3, x4,
    known, pb, qb, pw, qw, xs, ys,
    ap, aq, column, ahead, behind, x_block, y_block, row_wy, col_wx, held, sems, vector_sems,
    part_sems,
):
    tiles = meta[16]
    me_s, me_t = meta[17], meta[18]
    vectors_in = ((known_in, known), (pb_in, pb), (qb_in, qb), (pw_in, pw), (qw_in, qw))
    copies = [
        pltpu.make_async_copy(source, place, vector_sems.at[i])
        for i, (source, place) in enumerate(vectors_in)
    ]
    for copy in copies:
        copy.start()
    start_fetching(low, held, sems, tiles)
    part_moves = part_copies((s0, s1, t0, t1, t2, t3, t4), xs, ys, part_sems)
    for copy in part_moves:
        copy.start()
    row_wy[...] = jnp.zeros_like(row_wy)
    col_wx[...] = jnp.zeros_like(col_wx)
    for copy in copies:
        copy.wait()
    sums = total([found[i, :8, :] for i in range(16)])
    peaks = found[0, 8:, :]
    for i in range(1, 16):
        peaks = jnp.maximum(peaks, found[i, 8:, :])
    ee, ew, eh, ww, wh, uw, hu, waw = (scalar(sums[i : i + 1]) for i in range(8))
    bb, bh, hh, inverse = (known[i : i + 1, 0:1] for i in range(4))
    alpha1 = bb / bh
    beta1 = ee / bb
    dad = ew + 2.0 * beta1 * eh + beta1 * beta1 * bh
    alpha2 = ee / dad
    e_ad = ew + beta1 * eh
    ad_ad = ww + 2.0 * beta1 * wh + beta1 * beta1 * hh
    rr2 = ee - 2.0 * alpha2 * e_ad + alpha2 * alpha2 * ad_ad
    beta2 = rr2 / ee
    form = waw + 2.0 * beta1 * uw + beta1 * beta1 * hu
    r_ar = ew - 2.0 * alpha2 * (ww + beta1 * wh) + alpha2 * alpha2 * form
    d2_ar2 = ew + beta1 * eh - alpha2 * ad_ad
    d3ad3 = r_ar + 2.0 * beta2 * d2_ar2 + beta2 * beta2 * dad
    alpha3 = rr2 / d3ad3
    on_b = (alpha1 + alpha2 * beta1 + alpha3 * beta2 * beta1) * inverse
    on_e = (alpha2 + alpha3 * (1.0 + beta2)) * inverse
    on_w = -(alpha3 * alpha2) * inverse
    on_h = on_w * beta1
    for given, vectors, out, height in ((pb, pw, ap, 64), (qb, qw, aq, 8)):
        e, w, h = (vectors[height * i : height * (i + 1), :] for i in range(3))
        out[...] = on_b * given[:height, :] + on_e * e + on_w * w + on_h * h
    own = ap[block_rows(me_t // 2), :]
    own = jnp.where(me_t % 2 == 1, own[:, 64:], own[:, :64])
    for r in range(8):
        adj_s[:, 64 * r : 64 * (r + 1)] = own[r : r + 1, :]
    row = aq[pl.ds(me_s // 2, 1), :]
    adj_t[...] = jnp.where(me_s % 2 == 1, row[:, PART:], row[:, :PART])


    largest = [jnp.max(peaks[i : i + 1], axis=1, keepdims=True) for i in range(5)]
    reach = total(
        [jnp.abs(c) * m for c, m in zip((on_b, on_e, on_w, on_h), largest[:4])]
    )
    bound = jnp.maximum((60.0 * 1.05) * (reach * largest[4]), 1e-30)
    scale = 60000.0 / bound
    level[...] = jnp.broadcast_to(1.0 / scale, (8, LANES))

    def tile(slot, carry):
        rb, cb = meta[slot], meta[8 + slot]
        fill_columns(column, ap[block_rows(rb), :])
        q = lane_blocks(aq[pl.ds(cb, 1), :], 16)
        kernel = next_tile(low, high, held, sems, slot, tiles)


        @pl.when(slot == 0)
        def _():
            for copy in part_moves:
                copy.wait()

        x_block[...] = src_pair(meta, xs, rb)
        y_block[...] = tgt_pair(meta, ys, cb)
        halves = (ahead, behind)

        def weights(chunk):
            for u in range(CHUNK // 16):
                at = slice(CHUNK * chunk + 16 * u, CHUNK * chunk + 16 * u + 16)
                p = column[at, :]
                for l in range(WIDE):
                    halves[chunk % 2][16 * u : 16 * u + 16, lanes_of(l)] = (
                        kernel[at, lanes_of(l)] * (p + q[l])
                    ).astype(BF16)

        weights(0)
        for chunk in range(TILE // CHUNK):
            cells = slice(CHUNK * chunk, CHUNK * (chunk + 1))
            if CHUNK * (chunk + 1) < TILE:
                weights(chunk + 1)
            half = halves[chunk % 2][...]
            part, inner = 2 * rb + chunk // 2, slice(CHUNK * (chunk % 2), CHUNK * (chunk % 2 + 1))
            row_wy[part, :, inner] = row_wy[part, :, inner] + lax.dot_general(
                y_block[...], half, (((1,), (1,)), ((), ())), preferred_element_type=F32
            )
            for side in range(2):
                columns = slice(PART * side, PART * (side + 1))
                col_wx[2 * cb + side] = col_wx[2 * cb + side] + jnp.dot(
                    x_block[:, cells], half[:, columns], preferred_element_type=F32
                )
        return carry

    lax.fori_loop(0, tiles, tile, 0)


    def part_of(payload, mixed, ones, part):
        wide = payload[:FEATS, :].astype(F32)
        weight = mixed[part, ones : ones + 1, :]
        return (wide * weight - mixed[part, :FEATS, :]) * (scale * (2.0 / EPS))

    for k in range(8):
        for other, out in enumerate((near, far)):
            out[k] = part_of(
                xs[8 * other + k], row_wy, FEATS, ring_block(me_t, RING[k], other)
            )
    for k in range(4):
        for step, (dx, out) in enumerate(((0, x0), (-1, x2), (1, x1), (2, None))):
            part = part_of(
                ys[4 * step + k], col_wx, FEATS + 3, quad_block(me_s, QUAD[k], dx)
            )
            if out is None:
                x3[k] = part[:32]
                x4[k] = part[32:]
            else:
                out[k] = part


def finish_kernel(value, level, out, turned):
    whole = jnp.concatenate([value[...], jnp.zeros((FEATS, PART), F32)], axis=0)
    out[...] = to_cells(whole, turned)[:FEATS] * level[0:1, 0:1]


def swap(value, axis, mask):
    return lax.ppermute(value, axis, [(i, i ^ mask) for i in range(16)])


def along_z(value, step):
    return lax.ppermute(value, "tgt", [(i, (i + 2 * step) % 16) for i in range(16)])


def along_y(value, step):
    return lax.ppermute(value, "src", [(i, (i + 4 * step) % 16) for i in range(16)])


def along_x(value, step):
    return lax.ppermute(value, "src", [(i, i // 4 * 4 + (i + step) % 4) for i in range(16)])


def exchange(value, axis):
    return lax.all_to_all(value, axis, 0, 0)


def everywhere(value, axis):
    return exchange(jnp.broadcast_to(value[None], (16, *value.shape)), axis)


def summed(found):
    return jnp.concatenate([jnp.sum(found[:, :8], axis=0), jnp.max(found[:, 8:], axis=0)])


def spread(row, col, masks):
    rows = [row] + [swap(row, "tgt", mask) for mask in masks]
    cols = [col] + [swap(col, "src", mask) for mask in masks]
    return together(*rows, *cols)


def sum_pieces(row, col):
    both = spread(row, col, (4, 8, 12))
    row = (both[0] + both[1]) + (both[2] + both[3])
    col = (both[4] + both[5]) + (both[6] + both[7])
    return spread(row, col, (1, 2, 3))


def together(*values):
    return lax.optimization_barrier(values)


def gather_all(own_s, own_t):
    after, before, across = along_z(own_s, 1), along_z(own_s, -1), along_z(own_s, 4)
    up, down, over = along_y(own_t, 1), along_y(own_t, -1), along_y(own_t, 2)
    after, before, across, up, down, over = together(after, before, across, up, down, over)
    stack = jnp.stack([own_t, down, up, over])
    low, high = jnp.stack([own_s, after]), jnp.stack([own_s, before])
    right, left = along_x(stack, 1), along_x(stack, -1)
    low, high = along_z(low, 2), along_z(high, -2)
    right, left, low, high = together(right, left, low, high)
    near = jnp.concatenate([jnp.stack([own_s, after, before, across]), low, high])
    far = swap(near, "tgt", 1)
    return (near, far), (stack, right, left, along_x(right[:2], 1), along_x(left[2:], -1))


def narrow(value):
    return value.astype(jnp.float16)


def widened(values):
    return [value.astype(F32) for value in values]


def scatter_all(level, near, far, own, next_up, next_down, top, bottom):
    half = FEATS // 2
    other = swap(far, "tgt", 1)
    top, bottom = along_x(narrow(top), 1), along_x(narrow(bottom), -1)
    other, top, bottom = together(other, top, bottom)
    near = near + other
    top, bottom = widened((top, bottom))
    up = jnp.concatenate([next_up[:, :half] + top, next_up[:, half:]], axis=1)
    down = jnp.concatenate([next_down[:, :half], next_down[:, half:] + bottom], axis=1)
    up, down = along_x(narrow(up), 1), along_x(narrow(down), -1)
    after, before = along_z(narrow(near[6:8]), 2), along_z(narrow(near[4:6]), -2)
    up, down, after, before = widened(together(up, down, after, before))
    part = (own + up) + down
    last = (
        along_z(narrow(near[2] + after[1]), 1),
        along_z(narrow(near[1] + before[1]), -1),
        along_z(narrow(near[3]), 4),
        along_y(narrow(part[1]), 1),
        along_y(narrow(part[2]), -1),
        along_y(narrow(part[3]), 2),
    )
    last = widened(last)
    grad_src = ((near[0] + after[0]) + before[0]) + ((last[0] + last[1]) + last[2])
    grad_src = pl.pallas_call(
        finish_kernel,
        out_shape=shape((FEATS, PART)),
        in_specs=[VMEM] * 2,
        out_specs=VMEM,
        scratch_shapes=[pltpu.VMEM((PART, LANES), F32)],
        compiler_params=params(24),
    )(grad_src, level)
    grad_tgt = ((part[0] + last[3]) + (last[4] + last[5])) * level[0, 0]
    return grad_src, grad_tgt


def shards(
    src_feat, tgt_feat, row_pot, col_pot, src_mass, tgt_mass, rhs_src, rhs_tgt,
    tile_rows, tile_cols, tile_count,
):
    me_s, me_t = lax.axis_index("src"), lax.axis_index("tgt")
    meta = jnp.concatenate(
        [
            tile_rows.reshape(8),
            tile_cols.reshape(8),
            tile_count.reshape(1),
            me_s.reshape(1).astype(jnp.int32),
            me_t.reshape(1).astype(jnp.int32),
            *places(me_s, me_t),
        ]
    )
    line = lambda v: v.reshape(1, PART)
    pay = (FEATS + 16, PART)
    pay_s, pay_t = pl.pallas_call(
        payload_kernel,
        out_shape=[shape(pay, BF16), shape(pay, BF16)],
        in_specs=[HBM] * 8,
        out_specs=[VMEM] * 2,
        scratch_shapes=[pltpu.VMEM((FEATS, PART), BF16)] * 2
        + [pltpu.VMEM((1, PART), F32)] * 6
        + [pltpu.VMEM((PART, LANES), F32), pltpu.SemaphoreType.DMA((8,))],
        compiler_params=params(24),
    )(
        *(
            pltpu.with_memory_space_constraint(value, pltpu.HBM)
            for value in (
                src_feat, tgt_feat, line(row_pot), line(col_pot), line(src_mass), line(tgt_mass),
                line(rhs_src), line(rhs_tgt),
            )
        )
    )
    s_parts, t_parts = gather_all(pay_s, pay_t)

    feats = pltpu.VMEM((16, *pay), BF16)
    packed = shape((2 * 64, LANES))
    natural = shape((2 * BLOCKS, TILE))
    column = pltpu.VMEM((TILE, LANES), F32)
    kern, pb, qb, rsum, csum = pl.pallas_call(
        build_kernel,
        out_shape=[
            pltpu.VMEM((SLOTS, TILE, TILE), F32),
            packed, natural, packed, packed,
        ],
        in_specs=[SMEM] + [ANY] * 7,
        out_specs=[VMEM] * 5,
        scratch_shapes=[
            feats,
            feats,
            pltpu.VMEM((TILE, LANES), BF16),
            pltpu.VMEM((LANES, TILE), BF16),
            column,
            column,
            column,
            pltpu.VMEM((2 * BLOCKS, TILE), F32),
            pltpu.VMEM((4, 16, PART), F32),
            pltpu.VMEM((CHUNK, TILE), F32),
            pltpu.VMEM((CHUNK, TILE), F32),
            pltpu.SemaphoreType.DMA((7,)),
        ],
        compiler_params=params(24),
    )(meta, *s_parts, *t_parts)
    kern = pltpu.with_memory_space_constraint(kern, pltpu.VMEM)

    pieces = sum_pieces(rsum, csum)
    pv, qv, rimg, cimg, stored_low = pl.pallas_call(
        apply_kernel,
        out_shape=[
            packed, natural, shape((72, LANES)), shape((72, LANES)),
            shape((SLOTS // 2, TILE, TILE)),
        ],
        in_specs=[SMEM] + [VMEM] * 11,
        out_specs=[VMEM] * 4 + [ANY],
        scratch_shapes=[
            column, column, pltpu.VMEM((BLOCKS, TILE), F32), pltpu.SemaphoreType.DMA((SLOTS // 2,)),
        ],
        compiler_params=params(24),
    )(meta, *pieces, pb, qb, kern)

    pieces = sum_pieces(rimg, cimg)
    pw, qw, dots, known, stored_high = pl.pallas_call(
        form_kernel,
        out_shape=[
            shape((3 * 64, LANES)), shape((3 * BLOCKS, TILE)), shape((16, LANES)), shape((8, LANES)),
            shape((SLOTS // 2, TILE, TILE)),
        ],
        in_specs=[SMEM] + [VMEM] * 13,
        out_specs=[VMEM] * 4 + [ANY],
        scratch_shapes=[
            column, pltpu.VMEM((8, LANES), F32), pltpu.SemaphoreType.DMA((SLOTS // 2,)),
        ],
        compiler_params=params(24),
    )(meta, *pieces, pb, qb, pv, qv, kern)

    dots = everywhere(summed(everywhere(dots, "tgt")), "src")
    vectors = [
        pltpu.with_memory_space_constraint(value, pltpu.HBM) for value in (known, pb, qb, pw, qw)
    ]
    outs = pl.pallas_call(
        grad_kernel,
        out_shape=[shape((1, PART))] * 2
        + [shape((8, LANES))]
        + [shape((8, FEATS, PART))] * 2
        + [shape((4, FEATS, PART))] * 3
        + [shape((4, FEATS // 2, PART))] * 2,
        in_specs=[SMEM, VMEM] + [HBM] * 5 + [ANY] * 9,
        out_specs=[VMEM] * 10,
        scratch_shapes=[
            *(pltpu.VMEM(value.shape, F32) for value in (known, pb, qb, pw, qw)),
            feats,
            feats,
            pltpu.VMEM((64, LANES), F32),
            pltpu.VMEM((BLOCKS, TILE), F32),
            column,
            pltpu.VMEM((CHUNK, TILE), BF16),
            pltpu.VMEM((CHUNK, TILE), BF16),
            pltpu.VMEM((FEATS + 16, TILE), BF16),
            pltpu.VMEM((FEATS + 16, TILE), BF16),
            pltpu.VMEM((16, FEATS + 16, PART), F32),
            pltpu.VMEM((16, FEATS + 16, PART), F32),
            pltpu.VMEM((3, TILE, TILE), F32),
            pltpu.SemaphoreType.DMA((3,)),
            pltpu.SemaphoreType.DMA((5,)),
            pltpu.SemaphoreType.DMA((7,)),
        ],
        compiler_params=params(40),
    )(meta, dots, *vectors, *s_parts, *t_parts, stored_low, stored_high)
    adj_s, adj_t = outs[:2]
    grad_src, grad_tgt = scatter_all(*outs[2:])
    return adj_s.reshape(PART), adj_t.reshape(PART), grad_src, grad_tgt


def solution(mesh):
    in_specs = (
        P(None, ("src", "tgt")),
        P(None, ("tgt", "src")),
        P(("src", "tgt")),
        P(("tgt", "src")),
        P(("src", "tgt")),
        P(("tgt", "src")),
        P(("src", "tgt")),
        P(("tgt", "src")),
        P("src", "tgt", None),
        P("src", "tgt", None),
        P("src", "tgt"),
    )
    out_specs = (
        P(("src", "tgt")),
        P(("tgt", "src")),
        P(None, ("src", "tgt")),
        P(None, ("tgt", "src")),
    )
    return jax.shard_map(shards, mesh=mesh, in_specs=in_specs, out_specs=out_specs, check_vma=False)
```

```python
import math

import jax
import jax.numpy as jnp
from jax import lax
from jax.experimental import pallas as pl
from jax.experimental.pallas import tpu as pltpu
from jax.sharding import PartitionSpec as P

TILE = 1024
FEATS = 64
LANES = 128
BLOCKS = 8
SLOTS = 8
PART = 512
EPS = 0.05
RHO = 1.0
SCALE = 2.0 * math.log2(math.e) / EPS
DOWN = 2.0**-40
UP = 2.0**40
F32 = jnp.float32
BF16 = jnp.bfloat16
VMEM = pl.BlockSpec(memory_space=pltpu.VMEM)
SMEM = pl.BlockSpec(memory_space=pltpu.SMEM)
ANY = pl.BlockSpec(memory_space=pl.ANY)
HBM = pl.BlockSpec(memory_space=pltpu.HBM)
RING = (0, -1, 1, 4, -2, -3, 2, 3)
QUAD = (0, 1, -1, 2)


def params(mib):
    return pltpu.CompilerParams(vmem_limit_bytes=mib * 2**20)


def shape(dims, dtype=F32):
    return jax.ShapeDtypeStruct(dims, dtype)


def split3(value):
    high = value.astype(BF16).astype(F32)
    rest = value - high
    middle = rest.astype(BF16).astype(F32)
    low = (rest - middle).astype(BF16).astype(F32)
    return high, middle, low


def to_positions(value, turned):
    turned[...] = value.T
    groups = [turned[pl.ds(g, 8, stride=64), :] for g in range(64)]
    return jnp.concatenate(groups, axis=0).T


def to_cells(value, turned):
    turned[...] = value.T
    groups = [turned[pl.ds(r, 64, stride=8), :] for r in range(8)]
    return jnp.concatenate(groups, axis=0).T


def payload_kernel(*refs):
    sources, (out_s, out_t), held = refs[:8], refs[8:10], refs[10:18]
    turned, sems = refs[18:]
    copies = [
        pltpu.make_async_copy(source, place, sems.at[i])
        for i, (source, place) in enumerate(zip(sources, held))
    ]
    for copy in copies:
        copy.start()
    for copy in copies:
        copy.wait()
    sf, tf, rp, cp, sm, tm, rs, rt = held
    for feat, pot, mass, rhs, out, first in (
        (sf, rp, sm, rs, out_s, True),
        (tf, cp, tm, rt, out_t, False),
    ):
        wide = feat[...].astype(F32)
        potential = pot[...]
        term = (potential - jnp.sum(wide * wide, axis=0, keepdims=True)) * 0.5
        damp = EPS / RHO * mass[...] * jnp.exp(-potential / RHO)
        ones = jnp.ones((3, PART), F32)
        pieces = list(split3(term))
        rows = pieces + [ones] if first else [ones] + pieces
        rows += list(split3(rhs[...])) + list(split3(damp))
        rows.append(jnp.zeros((4, PART), F32))
        tail = jnp.concatenate(rows, axis=0)
        if first:
            whole = jnp.concatenate([wide, tail, jnp.zeros((48, PART), F32)], axis=0)
            whole = to_positions(whole, turned)
            out[0:FEATS, :] = whole[:FEATS].astype(BF16)
            keep = lax.broadcasted_iota(jnp.int32, (16, PART), 0) < 6
            tail = jnp.where(keep, whole[FEATS : FEATS + 16], tail)
        else:
            out[0:FEATS, :] = feat[...]
        out[FEATS : FEATS + 16, :] = tail.astype(BF16)


def three(rows, start):
    return rows[start : start + 1] + (rows[start + 1 : start + 2] + rows[start + 2 : start + 3])


def lane_blocks(row, height):
    return [
        jnp.broadcast_to(row[:, LANES * l : LANES * (l + 1)], (height, LANES))
        for l in range(TILE // LANES)
    ]


def total(values):
    while len(values) > 1:
        joined = [values[i] + values[i + 1] for i in range(0, len(values) - 1, 2)]
        values = joined + list(values[len(values) // 2 * 2 :])
    return values[0]


def block_rows(block):
    return pl.ds(pl.multiple_of(8 * block, 8), 8)


def fill_columns(column, packed):
    for g in range(LANES):
        column[8 * g : 8 * g + 8, :] = jnp.broadcast_to(packed[:, g : g + 1], (8, LANES))


def lane_sums(partial):
    lane = lax.broadcasted_iota(jnp.int32, (8, LANES), 1)
    result = jnp.zeros((8, LANES), F32)
    for g in range(LANES):
        group = jnp.sum(partial[8 * g : 8 * g + 8, :], axis=1, keepdims=True)
        result = jnp.where(lane == g, group, result)
    return result


def add_block(ref, first, block, value):
    rows = pl.ds(pl.multiple_of(first + 8 * block, 8), 8)
    ref[rows, :] = ref[rows, :] + value


def add_sums(ref, index, sums):
    row = jnp.sum(jnp.concatenate(sums, axis=1), axis=0, keepdims=True)
    ref[pl.ds(index, 1), :] = ref[pl.ds(index, 1), :] + row


def unpack(value):
    return jnp.concatenate(
        [value[BLOCKS * l : BLOCKS * (l + 1)] for l in range(TILE // LANES)], axis=1
    )


def pack_into(out, first, value):
    for l in range(TILE // LANES):
        out[first + BLOCKS * l : first + BLOCKS * (l + 1), :] = value[:, LANES * l : LANES * (l + 1)]


def ring_block(me, dz, other):
    place = lax.rem(me // 2 + (dz + 8), 8)
    core = lax.rem(me, 2)
    return 2 * place + (1 - core if other else core)


def quad_block(me, dy, dx):
    return 4 * lax.rem(me // 4 + (dy + 4), 4) + lax.rem(lax.rem(me, 4) + (dx + 4), 4)


def fetch(kern, held, sems, slot):
    place = lax.rem(slot, 3)
    return pltpu.make_async_copy(kern, held.at[place], sems.at[place])


def start_fetch(stores, held, sems, slot):
    first = 0
    for store, size in zip(stores, (EARLY, MIDDLE, SLOTS - EARLY - MIDDLE)):
        place = slot - first

        @pl.when(jnp.logical_and(place >= 0, place < size))
        def _():
            fetch(store.at[place], held, sems, slot).start()

        first += size


def start_fetching(stores, held, sems, count):
    fetch(stores[0].at[0], held, sems, 0).start()

    @pl.when(count > 1)
    def _():
        fetch(stores[0].at[1], held, sems, 1).start()


def next_tile(stores, held, sems, slot, count):
    @pl.when(slot + 2 < count)
    def _():
        start_fetch(stores, held, sems, slot + 2)

    fetch(stores[0].at[0], held, sems, slot).wait()
    return held.at[lax.rem(slot, 3)]


WIDE = TILE // LANES
CHUNK = 256


def no_sums():
    return tuple(jnp.zeros((8, LANES), F32) for l in range(WIDE))


def lanes_of(l):
    return slice(LANES * l, LANES * (l + 1))


def part_copies(pieces, xs, ys, sems):
    s0, s1, t0, t1, t2, t3, t4 = pieces
    moves = (
        (s0, xs.at[0:8]),
        (s1, xs.at[8:16]),
        (t0, ys.at[0:4]),
        (t1, ys.at[4:8]),
        (t2, ys.at[8:12]),
        (t3, ys.at[12:14]),
        (t4, ys.at[14:16]),
    )
    return [
        pltpu.make_async_copy(source, place, sems.at[i])
        for i, (source, place) in enumerate(moves)
    ]


def places(me_s, me_t):
    part = jnp.arange(16, dtype=jnp.int32)
    dz = lax.rem(part // 2 - me_t // 2 + 8, 8)
    src = sum(jnp.where(dz == z % 8, k, 0) for k, z in enumerate(RING))
    src = src + 8 * jnp.not_equal(lax.rem(part, 2), lax.rem(me_t, 2)).astype(jnp.int32)
    dy = lax.rem(part // 4 - me_s // 4 + 4, 4)
    dx = lax.rem(lax.rem(part, 4) - lax.rem(me_s, 4) + 4, 4)
    tgt = sum(jnp.where(dy == y % 4, k, 0) for k, y in enumerate(QUAD))
    tgt = tgt + sum(jnp.where(dx == x % 4, 4 * k, 0) for k, x in enumerate((0, -1, 1, 2)))
    return src, tgt


def src_pair(meta, ref, block):
    return jnp.concatenate([ref[meta[19 + 2 * block]], ref[meta[20 + 2 * block]]], axis=1)


def tgt_pair(meta, ref, block):
    return jnp.concatenate([ref[meta[35 + 2 * block]], ref[meta[36 + 2 * block]]], axis=1)


def build_kernel(
    meta, s0, s1, t0, t1, t2, t3, t4,
    kern, pb, qb, rout, cout, stored,
    xs, ys, left, right, sums, prods, column, csum, parts, ahead, behind, sems, out_sems,
):
    pieces = (s0, s1, t0, t1, t2, t3, t4)
    copies = part_copies(pieces, xs, ys, sems)
    for copy in copies:
        copy.start()
    rout[...] = jnp.zeros_like(rout)
    csum[...] = jnp.zeros_like(csum)
    for copy in copies:
        copy.wait()
    for part in range(16):
        for place, ref, first in ((0, xs, 19), (2, ys, 35)):
            rows = ref[meta[first + part], FEATS : FEATS + 16, :].astype(F32)
            at = part // 2 + 8 * (part % 2)
            parts[place, at : at + 1, :] = three(rows, 6)
            parts[place + 1, at : at + 1, :] = three(rows, 9)
    for place in range(2):
        even, odd = parts[place, 0:8, :], parts[place, 8:16, :]
        for r in range(8):
            cells = slice(64 * r, 64 * (r + 1))
            pb[pl.ds(64 * place + r, 8, stride=8), :] = jnp.concatenate(
                [even[:, cells], odd[:, cells]], axis=1
            )
        for side in range(2):
            qb[8 * place : 8 * place + 8, PART * side : PART * (side + 1)] = parts[
                2 + place, 8 * side : 8 * side + 8, :
            ]

    keep = lax.broadcasted_iota(jnp.int32, (16, TILE), 0) < 6
    blank = jnp.zeros((48, TILE), BF16)

    def with_terms(payload):
        terms = jnp.where(keep, payload[FEATS:].astype(F32), 0.0).astype(BF16)
        return jnp.concatenate([payload[:FEATS], terms, blank], axis=0)

    def tile(slot, carry):
        rb, cb = meta[slot], meta[8 + slot]
        kernel = kern.at[slot]
        left[...] = with_terms(src_pair(meta, xs, rb)).T
        right[...] = with_terms(tgt_pair(meta, ys, cb))
        q = lane_blocks(qb[pl.ds(cb, 1), :], 8)
        fill_columns(column, pb[block_rows(rb), :])

        products = (ahead, behind)

        def product(chunk):
            products[chunk % 2][...] = jnp.dot(
                left[CHUNK * chunk : CHUNK * (chunk + 1), :],
                right[...],
                preferred_element_type=F32,
            )

        csums, cprods = no_sums(), no_sums()
        product(0)
        for chunk in range(TILE // CHUNK):
            if CHUNK * (chunk + 1) < TILE:
                product(chunk + 1)
            for u in range(CHUNK // 8):
                near = slice(8 * u, 8 * u + 8)
                at = slice(CHUNK * chunk + 8 * u, CHUNK * chunk + 8 * u + 8)
                ks = [
                    jnp.exp2(products[chunk % 2][near, lanes_of(l)] * SCALE) for l in range(WIDE)
                ]
                for l in range(WIDE):
                    kernel[at, lanes_of(l)] = ks[l]
                p = column[at, :]
                sums[at, :] = total(ks)
                prods[at, :] = total([ks[l] * q[l] for l in range(WIDE)])
                csums = tuple(csums[l] + ks[l] for l in range(WIDE))
                cprods = tuple(cprods[l] + ks[l] * p for l in range(WIDE))

        @pl.when(slot < EARLY)
        def _():
            storing(kern, stored, out_sems, 0, slot).start()

        add_block(rout, 0, rb, lane_sums(sums))
        add_block(rout, 64, rb, lane_sums(prods))
        add_sums(csum, cb, csums)
        add_sums(csum, 8 + cb, cprods)
        return carry

    lax.fori_loop(0, meta[16], tile, 0)
    pack_into(cout, 0, csum[:8, :])
    pack_into(cout, 64, csum[8:, :])
    finish_storing(kern, stored, out_sems, 0, jnp.minimum(meta[16], EARLY))


def folded(value, join):
    if value.shape[1] == LANES:
        return value
    result = value[:, :LANES]
    for l in range(1, WIDE):
        result = join(result, value[:, lanes_of(l)])
    return result


def lane_partial(value):
    return folded(jnp.sum(value, axis=0, keepdims=True), jnp.add)


def lane_largest(value):
    return folded(jnp.max(value, axis=0, keepdims=True), jnp.maximum)


def scalar(row):
    return jnp.sum(row, axis=1, keepdims=True)


EARLY, MIDDLE = 4, 2


def storing(kern, stored, sems, first, slot):
    return pltpu.make_async_copy(kern.at[first + slot], stored.at[slot], sems.at[slot])


def start_storing(kern, stored, sems, first, count):
    def begin(slot, carry):
        storing(kern, stored, sems, first, slot).start()
        return carry

    lax.fori_loop(0, count, begin, 0)


def finish_storing(kern, stored, sems, first, count):
    def finish(slot, carry):
        storing(kern, stored, sems, first, slot).wait()
        return carry

    lax.fori_loop(0, count, finish, 0)


def four(pieces):
    return (pieces[0][...] + pieces[1][...]) + (pieces[2][...] + pieces[3][...])


def apply_kernel(
    meta, r0, r1, r2, r3, c0, c1, c2, c3, pb, qb, kern,
    pv, qv, rout, cout, stored,
    prods, column, csum, out_sems,
):
    count = jnp.clip(meta[16] - EARLY, 0, MIDDLE)
    start_storing(kern, stored, out_sems, EARLY, count)
    rows_in, cols_in = four((r0, r1, r2, r3)), four((c0, c1, c2, c3))
    rows = (rows_in[:64], rows_in[64:])
    cols = (unpack(cols_in[:64]), unpack(cols_in[64:]))
    rout[...] = jnp.zeros_like(rout)
    csum[...] = jnp.zeros_like(csum)
    cout[64:72, :] = jnp.zeros((8, LANES), F32)
    for (marg, prod), given, out, image, height in (
        (rows, pb, pv, cout, 64),
        (cols, qb, qv, rout, 8),
    ):
        b, d = given[:height, :], given[height:, :]
        g = marg + d
        v = g * (b * DOWN) + prod * DOWN
        out[:height, :] = v
        out[height:, :] = g
        for place, value in enumerate(
            (lane_partial(b * b), lane_partial(b * v), lane_partial(v * v), lane_largest(g))
        ):
            image[64 + place : 65 + place, :] = value

    def tile(slot, carry):
        rb, cb = meta[slot], meta[8 + slot]
        kernel = kern.at[slot]
        q = lane_blocks(qv[pl.ds(cb, 1), :], 8)
        fill_columns(column, pv[block_rows(rb), :])

        cprods = no_sums()
        for u in range(TILE // 8):
            at = slice(8 * u, 8 * u + 8)
            ks = [kernel[at, lanes_of(l)] for l in range(WIDE)]
            p = column[at, :]
            prods[at, :] = total([ks[l] * q[l] for l in range(WIDE)])
            cprods = tuple(cprods[l] + ks[l] * p for l in range(WIDE))
        add_block(rout, 0, rb, lane_sums(prods))
        add_sums(csum, cb, cprods)
        return carry

    lax.fori_loop(0, meta[16], tile, 0)
    pack_into(cout, 0, csum[...])
    finish_storing(kern, stored, out_sems, EARLY, count)


def form_kernel(
    meta, r0, r1, r2, r3, c0, c1, c2, c3, pb, qb, pv, qv, kern,
    pw, qw, dots, known, stored,
    column, acc, out_sems,
):
    count = jnp.maximum(meta[16] - EARLY - MIDDLE, 0)
    start_storing(kern, stored, out_sems, EARLY + MIDDLE, count)
    rows_in, cols_in = four((r0, r1, r2, r3)), four((c0, c1, c2, c3))
    both = rows_in[64:72] + cols_in[64:72]
    bb, bv, vv, sigma = (scalar(both[i : i + 1]) for i in range(4))
    rows, cols = rows_in[:64], unpack(cols_in[:64])
    inverse = 1.0 / sigma
    lift = UP * inverse
    alpha = bb / (bv * lift)
    known[...] = jnp.zeros_like(known)
    for place, value in enumerate((bb, bv * lift, (vv * lift) * lift, inverse)):
        known[place : place + 1, :] = jnp.broadcast_to(value, (1, LANES))
    found = []
    for given, vectors, image, out, height in ((pb, pv, rows, pw, 64), (qb, qv, cols, qw, 8)):
        b, v, g = given[:height, :], vectors[:height, :], vectors[height:, :]
        second = g * v + image
        first = v * lift
        next_image = (second * lift) * inverse
        residual = b - alpha * first
        turned = first - alpha * next_image
        out[:height, :] = residual
        out[height : 2 * height, :] = turned
        out[2 * height :, :] = first
        found.append(
            (
                lane_partial(residual * residual),
                lane_partial(residual * turned),
                lane_partial(residual * first),
                lane_partial(turned * turned),
                lane_partial(turned * first),
                lane_partial(next_image * turned),
                lane_partial(first * next_image),
                lane_partial((g * inverse) * turned * turned),
                *(lane_largest(jnp.abs(vector)) for vector in (b, residual, turned, first)),
                lane_largest(g),
            )
        )
    acc[...] = jnp.zeros_like(acc)

    def tile(slot, carry):
        rb, cb = meta[slot], meta[8 + slot]
        kernel = kern.at[slot]
        q = lane_blocks(qw[pl.ds(8 + cb, 1), :] * inverse, 8)
        fill_columns(column, pw[pl.ds(pl.multiple_of(64 + 8 * rb, 8), 8), :])

        cprods = no_sums()
        for u in range(TILE // 8):
            at = slice(8 * u, 8 * u + 8)
            p = column[at, :]
            cprods = tuple(cprods[l] + kernel[at, lanes_of(l)] * p for l in range(WIDE))
        acc[...] = acc[...] + total([cprods[l] * q[l] for l in range(WIDE)])
        return carry

    lax.fori_loop(0, meta[16], tile, 0)
    for place in range(8):
        value = (found[0][place] + found[1][place]) * (1.0 / 16.0)
        if place == 7:
            value = value + 2.0 * jnp.sum(acc[...], axis=0, keepdims=True)
        dots[place : place + 1, :] = value
    for place in range(8, 13):
        dots[place : place + 1, :] = jnp.maximum(found[0][place], found[1][place])
    dots[13:16, :] = jnp.zeros((3, LANES), F32)
    finish_storing(kern, stored, out_sems, EARLY + MIDDLE, count)


def grad_kernel(
    meta, found, known_in, pb_in, qb_in, pw_in, qw_in, s0, s1, t0, t1, t2, t3, t4, early, middle, late,
    adj_s, adj_t, level, near, far, x0, x1, x2, x3, x4,
    known, pb, qb, pw, qw, xs, ys,
    ap, aq, column, ahead, behind, x_block, y_block, row_wy, col_wx, held, sems, vector_sems,
    part_sems,
):
    tiles = meta[16]
    me_s, me_t = meta[17], meta[18]
    vectors_in = ((known_in, known), (pb_in, pb), (qb_in, qb), (pw_in, pw), (qw_in, qw))
    copies = [
        pltpu.make_async_copy(source, place, vector_sems.at[i])
        for i, (source, place) in enumerate(vectors_in)
    ]
    for copy in copies:
        copy.start()
    stores = (early, middle, late)
    start_fetching(stores, held, sems, tiles)
    part_moves = part_copies((s0, s1, t0, t1, t2, t3, t4), xs, ys, part_sems)
    for copy in part_moves:
        copy.start()
    row_wy[...] = jnp.zeros_like(row_wy)
    col_wx[...] = jnp.zeros_like(col_wx)
    for copy in copies:
        copy.wait()
    sums = total([found[i, :8, :] for i in range(16)])
    peaks = found[0, 8:, :]
    for i in range(1, 16):
        peaks = jnp.maximum(peaks, found[i, 8:, :])
    ee, ew, eh, ww, wh, uw, hu, waw = (scalar(sums[i : i + 1]) for i in range(8))
    bb, bh, hh, inverse = (known[i : i + 1, 0:1] for i in range(4))
    alpha1 = bb / bh
    beta1 = ee / bb
    dad = ew + 2.0 * beta1 * eh + beta1 * beta1 * bh
    alpha2 = ee / dad
    e_ad = ew + beta1 * eh
    ad_ad = ww + 2.0 * beta1 * wh + beta1 * beta1 * hh
    rr2 = ee - 2.0 * alpha2 * e_ad + alpha2 * alpha2 * ad_ad
    beta2 = rr2 / ee
    form = waw + 2.0 * beta1 * uw + beta1 * beta1 * hu
    r_ar = ew - 2.0 * alpha2 * (ww + beta1 * wh) + alpha2 * alpha2 * form
    d2_ar2 = ew + beta1 * eh - alpha2 * ad_ad
    d3ad3 = r_ar + 2.0 * beta2 * d2_ar2 + beta2 * beta2 * dad
    alpha3 = rr2 / d3ad3
    on_b = (alpha1 + alpha2 * beta1 + alpha3 * beta2 * beta1) * inverse
    on_e = (alpha2 + alpha3 * (1.0 + beta2)) * inverse
    on_w = -(alpha3 * alpha2) * inverse
    on_h = on_w * beta1
    for given, vectors, out, height in ((pb, pw, ap, 64), (qb, qw, aq, 8)):
        e, w, h = (vectors[height * i : height * (i + 1), :] for i in range(3))
        out[...] = on_b * given[:height, :] + on_e * e + on_w * w + on_h * h
    own = ap[block_rows(me_t // 2), :]
    own = jnp.where(me_t % 2 == 1, own[:, 64:], own[:, :64])
    for r in range(8):
        adj_s[:, 64 * r : 64 * (r + 1)] = own[r : r + 1, :]
    row = aq[pl.ds(me_s // 2, 1), :]
    adj_t[...] = jnp.where(me_s % 2 == 1, row[:, PART:], row[:, :PART])


    largest = [jnp.max(peaks[i : i + 1], axis=1, keepdims=True) for i in range(5)]
    reach = total(
        [jnp.abs(c) * m for c, m in zip((on_b, on_e, on_w, on_h), largest[:4])]
    )
    bound = jnp.maximum((60.0 * 1.05) * (reach * largest[4]), 1e-30)
    scale = 60000.0 / bound
    level[...] = jnp.broadcast_to(1.0 / scale, (8, LANES))

    def tile(slot, carry):
        rb, cb = meta[slot], meta[8 + slot]
        fill_columns(column, ap[block_rows(rb), :])
        q = lane_blocks(aq[pl.ds(cb, 1), :], 16)
        kernel = next_tile(stores, held, sems, slot, tiles)


        @pl.when(slot == 0)
        def _():
            for copy in part_moves:
                copy.wait()

        x_block[...] = src_pair(meta, xs, rb)
        y_block[...] = tgt_pair(meta, ys, cb)
        halves = (ahead, behind)

        def weights(chunk):
            for u in range(CHUNK // 16):
                at = slice(CHUNK * chunk + 16 * u, CHUNK * chunk + 16 * u + 16)
                p = column[at, :]
                for l in range(WIDE):
                    halves[chunk % 2][16 * u : 16 * u + 16, lanes_of(l)] = (
                        kernel[at, lanes_of(l)] * (p + q[l])
                    ).astype(BF16)

        weights(0)
        for chunk in range(TILE // CHUNK):
            cells = slice(CHUNK * chunk, CHUNK * (chunk + 1))
            if CHUNK * (chunk + 1) < TILE:
                weights(chunk + 1)
            half = halves[chunk % 2][...]
            part, inner = 2 * rb + chunk // 2, slice(CHUNK * (chunk % 2), CHUNK * (chunk % 2 + 1))
            row_wy[part, :, inner] = row_wy[part, :, inner] + lax.dot_general(
                y_block[...], half, (((1,), (1,)), ((), ())), preferred_element_type=F32
            )
            for side in range(2):
                columns = slice(PART * side, PART * (side + 1))
                col_wx[2 * cb + side] = col_wx[2 * cb + side] + jnp.dot(
                    x_block[:, cells], half[:, columns], preferred_element_type=F32
                )
        return carry

    lax.fori_loop(0, tiles, tile, 0)


    def part_of(payload, mixed, ones, part):
        wide = payload[:FEATS, :].astype(F32)
        weight = mixed[part, ones : ones + 1, :]
        return (wide * weight - mixed[part, :FEATS, :]) * (scale * (2.0 / EPS))

    for k in range(8):
        for other, out in enumerate((near, far)):
            out[k] = part_of(
                xs[8 * other + k], row_wy, FEATS, ring_block(me_t, RING[k], other)
            )
    for k in range(4):
        for step, (dx, out) in enumerate(((0, x0), (-1, x2), (1, x1), (2, None))):
            part = part_of(
                ys[4 * step + k], col_wx, FEATS + 3, quad_block(me_s, QUAD[k], dx)
            )
            if out is None:
                x3[k] = part[:32]
                x4[k] = part[32:]
            else:
                out[k] = part


def finish_kernel(value, level, out, turned):
    whole = jnp.concatenate([value[...], jnp.zeros((FEATS, PART), F32)], axis=0)
    out[...] = to_cells(whole, turned)[:FEATS] * level[0:1, 0:1]


def swap(value, axis, mask):
    return lax.ppermute(value, axis, [(i, i ^ mask) for i in range(16)])


def along_z(value, step):
    return lax.ppermute(value, "tgt", [(i, (i + 2 * step) % 16) for i in range(16)])


def along_y(value, step):
    return lax.ppermute(value, "src", [(i, (i + 4 * step) % 16) for i in range(16)])


def along_x(value, step):
    return lax.ppermute(value, "src", [(i, i // 4 * 4 + (i + step) % 4) for i in range(16)])


def exchange(value, axis):
    return lax.all_to_all(value, axis, 0, 0)


def everywhere(value, axis):
    return exchange(jnp.broadcast_to(value[None], (16, *value.shape)), axis)


def summed(found):
    return jnp.concatenate([jnp.sum(found[:, :8], axis=0), jnp.max(found[:, 8:], axis=0)])


def spread(row, col, masks):
    rows = [row] + [swap(row, "tgt", mask) for mask in masks]
    cols = [col] + [swap(col, "src", mask) for mask in masks]
    return together(*rows, *cols)


def sum_pieces(row, col):
    both = spread(row, col, (4, 8, 12))
    row = (both[0] + both[1]) + (both[2] + both[3])
    col = (both[4] + both[5]) + (both[6] + both[7])
    return spread(row, col, (1, 2, 3))


def together(*values):
    return lax.optimization_barrier(values)


def gather_all(own_s, own_t):
    after, before, across = along_z(own_s, 1), along_z(own_s, -1), along_z(own_s, 4)
    up, down, over = along_y(own_t, 1), along_y(own_t, -1), along_y(own_t, 2)
    after, before, across, up, down, over = together(after, before, across, up, down, over)
    stack = jnp.stack([own_t, down, up, over])
    low, high = jnp.stack([own_s, after]), jnp.stack([own_s, before])
    right, left = along_x(stack, 1), along_x(stack, -1)
    low, high = along_z(low, 2), along_z(high, -2)
    right, left, low, high = together(right, left, low, high)
    near = jnp.concatenate([jnp.stack([own_s, after, before, across]), low, high])
    far = swap(near, "tgt", 1)
    return (near, far), (stack, right, left, along_x(right[:2], 1), along_x(left[2:], -1))


def narrow(value):
    return value.astype(jnp.float16)


def widened(values):
    return [value.astype(F32) for value in values]


def scatter_all(level, near, far, own, next_up, next_down, top, bottom):
    half = FEATS // 2
    other = swap(far, "tgt", 1)
    top, bottom = along_x(narrow(top), 1), along_x(narrow(bottom), -1)
    other, top, bottom = together(other, top, bottom)
    near = near + other
    top, bottom = widened((top, bottom))
    up = jnp.concatenate([next_up[:, :half] + top, next_up[:, half:]], axis=1)
    down = jnp.concatenate([next_down[:, :half], next_down[:, half:] + bottom], axis=1)
    up, down = along_x(narrow(up), 1), along_x(narrow(down), -1)
    after, before = along_z(narrow(near[6:8]), 2), along_z(narrow(near[4:6]), -2)
    up, down, after, before = widened(together(up, down, after, before))
    part = (own + up) + down
    last = (
        along_z(narrow(near[2] + after[1]), 1),
        along_z(narrow(near[1] + before[1]), -1),
        along_z(narrow(near[3]), 4),
        along_y(narrow(part[1]), 1),
        along_y(narrow(part[2]), -1),
        along_y(narrow(part[3]), 2),
    )
    last = widened(last)
    grad_src = ((near[0] + after[0]) + before[0]) + ((last[0] + last[1]) + last[2])
    grad_src = pl.pallas_call(
        finish_kernel,
        out_shape=shape((FEATS, PART)),
        in_specs=[VMEM] * 2,
        out_specs=VMEM,
        scratch_shapes=[pltpu.VMEM((PART, LANES), F32)],
        compiler_params=params(24),
    )(grad_src, level)
    grad_tgt = ((part[0] + last[3]) + (last[4] + last[5])) * level[0, 0]
    return grad_src, grad_tgt


def shards(
    src_feat, tgt_feat, row_pot, col_pot, src_mass, tgt_mass, rhs_src, rhs_tgt,
    tile_rows, tile_cols, tile_count,
):
    me_s, me_t = lax.axis_index("src"), lax.axis_index("tgt")
    meta = jnp.concatenate(
        [
            tile_rows.reshape(8),
            tile_cols.reshape(8),
            tile_count.reshape(1),
            me_s.reshape(1).astype(jnp.int32),
            me_t.reshape(1).astype(jnp.int32),
            *places(me_s, me_t),
        ]
    )
    line = lambda v: v.reshape(1, PART)
    pay = (FEATS + 16, PART)
    pay_s, pay_t = pl.pallas_call(
        payload_kernel,
        out_shape=[shape(pay, BF16), shape(pay, BF16)],
        in_specs=[HBM] * 8,
        out_specs=[VMEM] * 2,
        scratch_shapes=[pltpu.VMEM((FEATS, PART), BF16)] * 2
        + [pltpu.VMEM((1, PART), F32)] * 6
        + [pltpu.VMEM((PART, LANES), F32), pltpu.SemaphoreType.DMA((8,))],
        compiler_params=params(24),
    )(
        *(
            pltpu.with_memory_space_constraint(value, pltpu.HBM)
            for value in (
                src_feat, tgt_feat, line(row_pot), line(col_pot), line(src_mass), line(tgt_mass),
                line(rhs_src), line(rhs_tgt),
            )
        )
    )
    s_parts, t_parts = gather_all(pay_s, pay_t)

    feats = pltpu.VMEM((16, *pay), BF16)
    packed = shape((2 * 64, LANES))
    natural = shape((2 * BLOCKS, TILE))
    column = pltpu.VMEM((TILE, LANES), F32)
    kern, pb, qb, rsum, csum, stored_early = pl.pallas_call(
        build_kernel,
        out_shape=[
            pltpu.VMEM((SLOTS, TILE, TILE), F32),
            packed, natural, packed, packed, shape((EARLY, TILE, TILE)),
        ],
        in_specs=[SMEM] + [ANY] * 7,
        out_specs=[VMEM] * 5 + [ANY],
        scratch_shapes=[
            feats,
            feats,
            pltpu.VMEM((TILE, LANES), BF16),
            pltpu.VMEM((LANES, TILE), BF16),
            column,
            column,
            column,
            pltpu.VMEM((2 * BLOCKS, TILE), F32),
            pltpu.VMEM((4, 16, PART), F32),
            pltpu.VMEM((CHUNK, TILE), F32),
            pltpu.VMEM((CHUNK, TILE), F32),
            pltpu.SemaphoreType.DMA((7,)),
            pltpu.SemaphoreType.DMA((EARLY,)),
        ],
        compiler_params=params(24),
    )(meta, *s_parts, *t_parts)
    kern = pltpu.with_memory_space_constraint(kern, pltpu.VMEM)

    pieces = sum_pieces(rsum, csum)
    pv, qv, rimg, cimg, stored_middle = pl.pallas_call(
        apply_kernel,
        out_shape=[
            packed, natural, shape((72, LANES)), shape((72, LANES)),
            shape((2, TILE, TILE)),
        ],
        in_specs=[SMEM] + [VMEM] * 11,
        out_specs=[VMEM] * 4 + [ANY],
        scratch_shapes=[
            column, column, pltpu.VMEM((BLOCKS, TILE), F32), pltpu.SemaphoreType.DMA((2,)),
        ],
        compiler_params=params(24),
    )(meta, *pieces, pb, qb, kern)

    pieces = sum_pieces(rimg, cimg)
    pw, qw, dots, known, stored_late = pl.pallas_call(
        form_kernel,
        out_shape=[
            shape((3 * 64, LANES)), shape((3 * BLOCKS, TILE)), shape((16, LANES)), shape((8, LANES)),
            shape((2, TILE, TILE)),
        ],
        in_specs=[SMEM] + [VMEM] * 13,
        out_specs=[VMEM] * 4 + [ANY],
        scratch_shapes=[
            column, pltpu.VMEM((8, LANES), F32), pltpu.SemaphoreType.DMA((2,)),
        ],
        compiler_params=params(24),
    )(meta, *pieces, pb, qb, pv, qv, kern)

    dots = everywhere(summed(everywhere(dots, "tgt")), "src")
    vectors = [
        pltpu.with_memory_space_constraint(value, pltpu.HBM) for value in (known, pb, qb, pw, qw)
    ]
    outs = pl.pallas_call(
        grad_kernel,
        out_shape=[shape((1, PART))] * 2
        + [shape((8, LANES))]
        + [shape((8, FEATS, PART))] * 2
        + [shape((4, FEATS, PART))] * 3
        + [shape((4, FEATS // 2, PART))] * 2,
        in_specs=[SMEM, VMEM] + [HBM] * 5 + [ANY] * 10,
        out_specs=[VMEM] * 10,
        scratch_shapes=[
            *(pltpu.VMEM(value.shape, F32) for value in (known, pb, qb, pw, qw)),
            feats,
            feats,
            pltpu.VMEM((64, LANES), F32),
            pltpu.VMEM((BLOCKS, TILE), F32),
            column,
            pltpu.VMEM((CHUNK, TILE), BF16),
            pltpu.VMEM((CHUNK, TILE), BF16),
            pltpu.VMEM((FEATS + 16, TILE), BF16),
            pltpu.VMEM((FEATS + 16, TILE), BF16),
            pltpu.VMEM((16, FEATS + 16, PART), F32),
            pltpu.VMEM((16, FEATS + 16, PART), F32),
            pltpu.VMEM((3, TILE, TILE), F32),
            pltpu.SemaphoreType.DMA((3,)),
            pltpu.SemaphoreType.DMA((5,)),
            pltpu.SemaphoreType.DMA((7,)),
        ],
        compiler_params=params(40),
    )(meta, dots, *vectors, *s_parts, *t_parts, stored_early, stored_middle, stored_late)
    adj_s, adj_t = outs[:2]
    grad_src, grad_tgt = scatter_all(*outs[2:])
    return adj_s.reshape(PART), adj_t.reshape(PART), grad_src, grad_tgt


def solution(mesh):
    in_specs = (
        P(None, ("src", "tgt")),
        P(None, ("tgt", "src")),
        P(("src", "tgt")),
        P(("tgt", "src")),
        P(("src", "tgt")),
        P(("tgt", "src")),
        P(("src", "tgt")),
        P(("tgt", "src")),
        P("src", "tgt", None),
        P("src", "tgt", None),
        P("src", "tgt"),
    )
    out_specs = (
        P(("src", "tgt")),
        P(("tgt", "src")),
        P(None, ("src", "tgt")),
        P(None, ("tgt", "src")),
    )
    return jax.shard_map(shards, mesh=mesh, in_specs=in_specs, out_specs=out_specs, check_vma=False)
```
